32 devices in a mesh: gx: 4 (over y, core), gy: 8 (over z, x).
Axes of the slice: x: 2, y: 2, z: 4, core: 2. Of those that a mesh axis runs over, the one named last changes fastest.
Arguments:
- inputs: bfloat16 [2, 128, 64, 768], P(None, ('gx', 'gy')), may hold values from -6 to 6
- lengths: int32 [2, 128], P(None, ('gx', 'gy')), may hold values from 3 to 64, as said below
- labels: int32 [128], P(('gx', 'gy')), may hold values from 0 to 127, as said below
- attention_input_weight: bfloat16 [2, 768, 2304], replicated, may hold values from -0.21875 to 0.21875
- attention_output_matrix: bfloat16 [2, 768, 768], replicated, may hold values from -0.875 to 0.875
- widen_weight: bfloat16 [2, 768, 3072], replicated, may hold values from -0.21875 to 0.21875
- narrowing_weight: bfloat16 [2, 3072, 768], replicated, may hold values from -0.109375 to 0.109375
- layer_bias_rows: float32 [2, 6, 768], replicated, may hold values from -1 to 1
- norm_gains: float32 [2, 2, 768], replicated, may hold values from 0.5 to 1.5
- widen_bias: float32 [2, 3072], replicated, may hold values from -1 to 1
- pool_weight: bfloat16 [768, 768], replicated, may hold values from -0.21875 to 0.21875
- pool_bias: float32 [768], replicated, may hold values from -1 to 1
Outputs:
- row_loss: float32 [128], P(('gx', 'gy'))
- input_grad: float32 [2, 128, 64, 768], P(None, ('gx', 'gy'))
- scaled_grad: float32 [2, 128, 64, 768], P(None, ('gx', 'gy'))
- grad_attend: float32 [2, 768, 2304], P(None, 'gx', 'gy')
- grad_output: float32 [2, 768, 768], P(None, 'gx', 'gy')
- grad_expand: float32 [2, 768, 3072], P(None, 'gx', 'gy')
- grad_reduce: float32 [2, 3072, 768], P(None, 'gx', 'gy')
- grad_bias_rows: float32 [2, 6, 768], P(None, None, ('gx', 'gy'))
- grad_gains: float32 [2, 2, 768], P(None, None, ('gx', 'gy'))
- grad_expand_bias: float32 [2, 3072], P(None, ('gx', 'gy'))
- grad_pool: float32 [768, 768], P('gx', 'gy')
- grad_pool_bias: float32 [768], P(('gx', 'gy'))
The draws below stay inside these ranges and needn't reach their ends.
Inputs may be any that keep to these rules, and one draw needn't show every extreme that they name: `lengths`: real tokens of each sentence; later positions are padding. `labels`: every target is the positive of exactly one source.
All inputs are finite; a program needn't handle non-finite values.
Results may differ from the reference program's by a relative error of at most 0.025.
Values may be sent and summed in bfloat16 or wider, within the bound.
No kernel may reach another device: no remote copies, remote signals or barrier semaphores. Data moves between devices by JAX's collectives and lax.ppermute only.
A program may use at most 320 MiB of HBM per device.

```python
import math
import jax
import jax.numpy as jnp
from jax import lax

D = 768
H = 12
HD = 64
FF = 3072
LAYERS = 2
L = 64
PAIRS = 128


def pair_order(key):
    return jax.random.permutation(jax.random.fold_in(key, 17), PAIRS)


def draw_labels(key, part):
    order = pair_order(key)
    return order.astype(jnp.int32)


def draw_inputs(key, part):
    order = pair_order(key)
    key = jax.random.fold_in(key, 2)
    first_key, second_key = jax.random.split(key)
    source = jax.random.normal(first_key, (PAIRS, L, D), jnp.float32)
    noise = jax.random.normal(second_key, (PAIRS, L, D), jnp.float32)
    aligned = jnp.zeros((PAIRS, L, D), jnp.float32).at[order].set(source)
    target = 0.6 * aligned + 0.8 * noise
    stacked = jnp.clip(jnp.stack([source, target]), -6.0, 6.0)
    return stacked.astype(jnp.bfloat16)


def draw_lengths(key, part):
    key = jax.random.fold_in(key, 3)
    first_key, second_key, third_key = jax.random.split(key, 3)
    place = jnp.arange(PAIRS, dtype=jnp.int32)
    quarter = L // 4
    upper = jnp.maximum(quarter + (L - quarter) * place // max(PAIRS - 1, 1), 3)
    draw_one = jax.random.randint(first_key, (2, PAIRS), 3, upper + 1)
    draw_two = jax.random.randint(second_key, (2, PAIRS), 3, upper + 1)
    draw_three = jax.random.randint(third_key, (2, PAIRS), 3, upper + 1)
    drawn = jnp.maximum(jnp.maximum(draw_one, draw_two), draw_three)
    drawn = jnp.where(place[None, :] == 0, 3, drawn)
    drawn = jnp.where(place[None, :] == PAIRS - 1, L, drawn)
    return drawn.astype(jnp.int32)


def centred(key, shape, scale, bound, kind=jnp.bfloat16):
    entries = scale * jax.random.normal(key, shape, jnp.float32)
    return jnp.clip(entries, min=-bound, max=bound).astype(kind)


def setup_inputs(seed: int = 0) -> dict:
    arg_keys = jax.random.split(jax.random.key(seed), 13)
    return {
        "inputs": draw_inputs(jax.random.fold_in(arg_keys[12], 71), 0),
        "lengths": draw_lengths(jax.random.fold_in(arg_keys[12], 71), 0),
        "labels": draw_labels(jax.random.fold_in(arg_keys[12], 71), 0),
        "attention_input_weight": centred(arg_keys[3], (LAYERS, D, 3 * D), D ** -0.5, 0.21875),
        "attention_output_matrix": centred(arg_keys[4], (LAYERS, D, D), (D // 16) ** -0.5, 0.875),
        "widen_weight": centred(arg_keys[5], (LAYERS, D, FF), D ** -0.5, 0.21875),
        "narrowing_weight": centred(arg_keys[6], (LAYERS, FF, D), FF ** -0.5, 0.109375),
        "layer_bias_rows": centred(arg_keys[7], (LAYERS, 6, D), 0.2, 1.0, jnp.float32),
        "norm_gains": jnp.clip(1.0 + 0.1 * jax.random.normal(arg_keys[8], (LAYERS, 2, D), jnp.float32), 0.5, 1.5),
        "widen_bias": centred(arg_keys[9], (LAYERS, FF), 0.2, 1.0, jnp.float32),
        "pool_weight": centred(arg_keys[10], (D, D), D ** -0.5, 0.21875),
        "pool_bias": centred(arg_keys[11], (D,), 0.2, 1.0, jnp.float32),
    }


EPS_NORM = 1e-12
EPS_UNIT = 1e-06
SCORE_SCALE = 10.0
MARGIN = 0.3
MASKED = -1000000000.0
PRECISION_TOP = lax.Precision.HIGHEST

@jax.custom_vjp
def low(v):
    return lax.optimization_barrier(v.astype(jnp.bfloat16)).astype(jnp.float32)

@jax.custom_vjp
def low_back(v):
    return v

def low_keep(v):
    return (low(v), None)

def low_pass(kept, grad):
    return (grad,)

def back_keep(v):
    return (v, None)

def back_low(kept, grad):
    return (low(grad),)
low.defvjp(low_keep, low_pass)
low_back.defvjp(back_keep, back_low)

def norm_rows(values, gain, shift):
    centered = values - lax.optimization_barrier(jnp.mean(values, -1, keepdims=True))
    variance = lax.optimization_barrier(jnp.mean(centered * centered, -1, keepdims=True))
    return centered * lax.rsqrt(variance + EPS_NORM) * gain + shift

def unit_rows(pre_pool):
    squashed = jnp.tanh(pre_pool)
    return squashed * lax.rsqrt(lax.optimization_barrier(jnp.sum(squashed * squashed, -1, keepdims=True)) + EPS_UNIT)

def exact_gelu(values):
    return jax.nn.gelu(values, approximate=False)

def block(layer_hidden_state, key_keep, attention_input_weight, attention_output_matrix, widen_weight, narrowing_weight, layer_bias_rows, norm_gains, widen_bias):
    sentences = layer_hidden_state.shape[0]
    output_projected = jnp.einsum('wyh,hr->wyr', low(layer_hidden_state), attention_input_weight, precision=PRECISION_TOP)
    queries = low_back(low((output_projected[..., :D] + layer_bias_rows[0]) * HD ** (-0.5))).reshape(sentences, L, H, HD)
    keys_full = low_back(low(output_projected[..., D:2 * D])).reshape(sentences, L, H, HD)
    values_full = low_back(low(output_projected[..., 2 * D:] + layer_bias_rows[1])).reshape(sentences, L, H, HD)
    scores = low_back(jnp.einsum('sqhc,skhc->shqk', queries, keys_full, precision=PRECISION_TOP))
    scores = jnp.where(key_keep[:, None, None, :], scores, MASKED)
    probs = low(jax.nn.softmax(scores, -1))
    attention_context = jnp.einsum('shqk,skhc->sqhc', probs, values_full, precision=PRECISION_TOP).reshape(sentences, L, D)
    attention_context = low_back(low(attention_context))
    attention_result = low_back(jnp.einsum('wyh,hr->wyr', attention_context, attention_output_matrix, precision=PRECISION_TOP) + layer_bias_rows[2])
    normalized_state = norm_rows(layer_hidden_state + attention_result, norm_gains[0], layer_bias_rows[3])
    hidden_inner = low_back(jnp.einsum('oqc,cv->oqv', low(normalized_state), widen_weight, precision=PRECISION_TOP) + widen_bias)
    activated_hidden = low(exact_gelu(hidden_inner))
    residual_branch = low_back(jnp.einsum('xhk,kw->xhw', activated_hidden, narrowing_weight, precision=PRECISION_TOP) + layer_bias_rows[4])
    return norm_rows(normalized_state + residual_branch, norm_gains[1], layer_bias_rows[5])

def reference(inputs, lengths, labels, attention_input_weight, attention_output_matrix, widen_weight, narrowing_weight, layer_bias_rows, norm_gains, widen_bias, pool_weight, pool_bias):
    group_size = math.gcd(4096 // L, 2 * PAIRS)
    group_count = 2 * PAIRS // group_size
    positions = jnp.arange(L, dtype=jnp.int32)
    key_keep = (positions[None, :] < lengths.reshape(2 * PAIRS)[:, None]).reshape(group_count, group_size, L)
    columns = jnp.arange(PAIRS, dtype=jnp.int32)
    chosen = (columns[None, :] == labels[:, None]).astype(jnp.float32)

    def forward(inputs_f, attend_f, output_f, expand_f, reduce_f, bias_f, gains_f, expand_bias_f, pool_f, pool_bias_f):

        def encode(pieces):
            layer_hidden_state, keep_rows = pieces
            for layer_index in range(LAYERS):
                layer_hidden_state = block(layer_hidden_state, keep_rows, attend_f[layer_index], output_f[layer_index], expand_f[layer_index], reduce_f[layer_index], bias_f[layer_index], gains_f[layer_index], expand_bias_f[layer_index])
            first_rows = low(layer_hidden_state[:, 0, :])
            pre_pool = low_back(jnp.einsum('sd,de->se', first_rows, pool_f, precision=PRECISION_TOP) + pool_bias_f)
            return low(unit_rows(pre_pool))
        grouped = inputs_f.reshape(group_count, group_size, L, D)
        pooled = lax.map(jax.checkpoint(encode), (grouped, key_keep)).reshape(2, PAIRS, D)
        similar = low_back(SCORE_SCALE * jnp.einsum('pd,qd->pq', pooled[0], pooled[1], precision=PRECISION_TOP))
        logits = similar - SCORE_SCALE * MARGIN * chosen
        return jax.nn.logsumexp(logits, -1) - lax.optimization_barrier(jnp.sum(chosen * logits, -1))
    floats = (inputs.astype(jnp.float32), attention_input_weight.astype(jnp.float32), attention_output_matrix.astype(jnp.float32), widen_weight.astype(jnp.float32), narrowing_weight.astype(jnp.float32), layer_bias_rows.astype(jnp.float32), norm_gains.astype(jnp.float32), widen_bias.astype(jnp.float32), pool_weight.astype(jnp.float32), pool_bias.astype(jnp.float32))
    row_loss, backward = jax.vjp(forward, *floats)
    grads = backward(jnp.ones_like(row_loss))
    input_grad = grads[0]
    token_total = jnp.sum(lengths).astype(jnp.float32)
    factor = 2 * PAIRS * lengths.astype(jnp.float32) / token_total
    scaled_grad = input_grad * factor[:, :, None, None]
    return (row_loss, input_grad, scaled_grad, grads[1], grads[2], grads[3], grads[4], grads[5], grads[6], grads[7], grads[8], grads[9])
```

```python
import functools
import jax
import jax.numpy as jnp
from jax import lax
from jax.sharding import PartitionSpec as P
from jax.experimental import pallas as pl
from jax.experimental.pallas import tpu as pltpu

H = 12
HD = 64
BF = jnp.bfloat16
F32 = jnp.float32
ROOT_HALF = 0.7071067811865476
PHI_ZERO = 0.3989422804014327
MASKED = -1e9
EPS_NORM = 1e-12
SCALE = HD ** -0.5

NN = (((1,), (0,)), ((), ()))
NT = (((1,), (1,)), ((), ()))
TN = (((0,), (0,)), ((), ()))


def dot(a, b, dims=NN):
    return lax.dot_general(a, b, dims, preferred_element_type=F32)


def normalize(z):
    centered = z - jnp.mean(z, -1, keepdims=True)
    variance = jnp.mean(centered * centered, -1, keepdims=True)
    root = lax.rsqrt(variance + EPS_NORM)
    return centered * root, root


def gelu_pair(f):
    cdf = 0.5 * (1.0 + lax.erf(f * ROOT_HALF))
    return f * cdf, cdf + f * (PHI_ZERO * jnp.exp(-0.5 * f * f))


def head_rows(values):
    lanes = lax.broadcasted_iota(jnp.int32, values.shape, 1) // HD
    return jnp.concatenate([jnp.where(lanes == h, values, 0) for h in range(H)], 0)


def head_fold(values):
    r = values.shape[0] // H
    lanes = lax.broadcasted_iota(jnp.int32, (r, values.shape[1]), 1) // HD
    out = jnp.zeros((r, values.shape[1]), values.dtype)
    for h in range(H):
        out = jnp.where(lanes == h, values[h * r:(h + 1) * r], out)
    return out


def fwd_kernel(len_ref, x_hbm, wqkv_hbm, wo_hbm, w1_hbm, w2_hbm, wp_hbm, bias_ref, gain_ref, wb_ref, pb_ref,
               q_out, k_out, v_out, a_out, c_out, n1_out, r1_out, hb_out, g_out, dg_out, n2_out, r2_out, xb_out,
               small_out, big_out, a1_out, ax_out, qm_out, qw_out, wide_out, rp_out,
               x, wqkv, wo, w1, w2, wqkv1, wo1, w11, w21, wp,
               q, k, v, a, c, n1, r1, hb, g, dg, n2, r2, xb, h1, acc, first, sem, osem):
    T, D = x.shape
    S = T // 64
    FF = w1.shape[1]
    loads = [(x_hbm, x)]
    for part in range(3):
        cols = pl.ds(part * D, D)
        loads.append((wqkv_hbm.at[0, :, cols], wqkv.at[part]))
    loads += [(wo_hbm.at[0], wo), (w1_hbm.at[0], w1), (w2_hbm.at[0], w2)]
    for part in range(3):
        cols = pl.ds(part * D, D)
        loads.append((wqkv_hbm.at[1, :, cols], wqkv1.at[part]))
    loads += [(wo_hbm.at[1], wo1), (w1_hbm.at[1], w11), (w2_hbm.at[1], w21), (wp_hbm, wp)]
    copies = [pltpu.make_async_copy(s, d, sem.at[i]) for i, (s, d) in enumerate(loads)]
    for copy in copies:
        copy.start()
    stores = []

    def store(src, dst):
        copy = pltpu.make_async_copy(src, dst, osem.at[len(stores)])
        copy.start()
        stores.append(copy)

    copies[0].wait()
    TILE = 256
    for part, dst in enumerate((q, k, v)):
        copies[1 + part].wait()

        def project(j, _, part=part, dst=dst):
            cols = pl.ds(pl.multiple_of(j * TILE, TILE), TILE)
            p = dot(x[...], wqkv[part, :, cols])
            if part == 0:
                p = (p + bias_ref[0, 0:1, cols]) * SCALE
            if part == 2:
                p = p + bias_ref[0, 1:2, cols]
            dst[:, cols] = p.astype(BF)
            return 0

        lax.fori_loop(0, D // TILE, project, 0)
    store(q, q_out)
    store(k, k_out)
    store(v, v_out)

    key = lax.broadcasted_iota(jnp.int32, (128, 256), 0)
    query = lax.broadcasted_iota(jnp.int32, (128, 256), 1)
    lane = lax.broadcasted_iota(jnp.int32, (128, 128), 1)
    low = lane < HD

    def attend(p, _):
        rows = pl.ds(pl.multiple_of(p * 128, 128), 128)
        limit = jnp.where(key < 64, len_ref[2 * p], len_ref[2 * p + 1] + 64)
        keep = ((key // 64) == ((query // 64) % 2)) & (key < limit)
        for j in range(D // 128):
            lanes = slice(128 * j, 128 * j + 128)
            qq = q[rows, lanes]
            qm = jnp.concatenate([jnp.where(low, qq, 0), jnp.where(low, 0, qq)], 0)
            s = jnp.where(keep, dot(k[rows, lanes], qm, NT), MASKED)
            e = jnp.exp(s - jnp.max(s, 0, keepdims=True))
            prob = (e * (1.0 / jnp.sum(e, 0, keepdims=True))).astype(BF)
            a[p * (D // 128) + j] = prob
            ctx = dot(prob, v[rows, lanes], TN)
            c[rows, lanes] = jnp.where(low, ctx[:128], ctx[128:]).astype(BF)
        return 0

    lax.fori_loop(0, S // 2, attend, 0)
    store(a, a_out)
    store(c, c_out)

    copies[4].wait()
    ROWS = 256

    def first_norm(i, _):
        rows = pl.ds(pl.multiple_of(i * ROWS, ROWS), ROWS)
        z = x[rows, :].astype(F32) + dot(c[rows, :], wo[...]) + bias_ref[0, 2:3, :]
        n, r = normalize(z)
        n1[rows, :] = n.astype(BF)
        r1[rows, :] = jnp.broadcast_to(r, (ROWS, 128))
        h = n * gain_ref[0, 0:1, :] + bias_ref[0, 3:4, :]
        h1[rows, :] = h
        hb[rows, :] = h.astype(BF)
        acc[rows, :] = h + bias_ref[0, 4:5, :]
        return 0

    lax.fori_loop(0, T // ROWS, first_norm, 0)
    store(n1, n1_out)
    store(r1, r1_out)
    store(hb, hb_out)
    copies[5].wait()
    copies[6].wait()

    def widen(j, _):
        cols = pl.ds(pl.multiple_of(j * TILE, TILE), TILE)
        f = dot(hb[...], w1[:, cols]) + wb_ref[0:1, cols]
        gj, dgj = gelu_pair(f)
        gj = gj.astype(BF)
        g[:, cols] = gj
        dg[:, cols] = dgj.astype(BF)
        acc[...] += dot(gj, w2[cols, :])
        return 0

    lax.fori_loop(0, FF // TILE, widen, 0)
    store(g, g_out)
    store(dg, dg_out)

    def second_norm(i, _):
        rows = pl.ds(pl.multiple_of(i * ROWS, ROWS), ROWS)
        n, r = normalize(acc[rows, :])
        n2[rows, :] = n.astype(BF)
        r2[rows, :] = jnp.broadcast_to(r, (ROWS, 128))
        h = n * gain_ref[0, 1:2, :] + bias_ref[0, 5:6, :]
        acc[rows, :] = h
        xb[rows, :] = h.astype(BF)
        return 0

    lax.fori_loop(0, T // ROWS, second_norm, 0)
    store(n2, n2_out)
    store(r2, r2_out)
    store(xb, xb_out)

    for s in range(S):
        first[s:s + 1, :] = acc[64 * s:64 * s + 1, :]
    x0 = first[...]
    x0b = x0.astype(BF)
    for i in (7, 8, 9):
        copies[i].wait()
    q0 = ((dot(x0b, wqkv1[0]) + bias_ref[1, 0:1, :]) * SCALE).astype(BF)
    qm = head_rows(q0.astype(F32)).astype(BF)
    qw = dot(qm, wqkv1[1], NT).astype(BF)
    xall = xb[...]
    scores = dot(qw, xall, NT)
    row = lax.broadcasted_iota(jnp.int32, scores.shape, 0) % S
    col = lax.broadcasted_iota(jnp.int32, scores.shape, 1)
    keep = jnp.zeros(scores.shape, jnp.bool_)
    for s in range(S):
        keep = keep | ((row == s) & (col >= 64 * s) & (col < 64 * s + len_ref[s]))
    scores = jnp.where(keep, scores, MASKED)
    e = jnp.exp(scores - jnp.max(scores, 1, keepdims=True))
    prob = e * (1.0 / jnp.sum(e, 1, keepdims=True))
    probb = prob.astype(BF)
    ax = dot(probb, xall).astype(BF)
    c0 = (head_fold(dot(ax, wqkv1[2])) + bias_ref[1, 1:2, :]).astype(BF)
    copies[10].wait()
    n10, r10 = normalize(x0 + dot(c0, wo1[...]) + bias_ref[1, 2:3, :])
    h10 = n10 * gain_ref[1, 0:1, :] + bias_ref[1, 3:4, :]
    h10b = h10.astype(BF)
    copies[11].wait()
    f0 = dot(h10b, w11[...]) + wb_ref[1:2, :]
    g0, dg0 = gelu_pair(f0)
    g0b = g0.astype(BF)
    copies[12].wait()
    n20, r20 = normalize(h10 + dot(g0b, w21[...]) + bias_ref[1, 4:5, :])
    x20 = n20 * gain_ref[1, 1:2, :] + bias_ref[1, 5:6, :]
    e0 = x20.astype(BF)
    copies[13].wait()
    rp_out[...] = dot(e0, wp[...]) + pb_ref[...]
    small_out[0] = n10
    small_out[1] = n20
    small_out[2] = jnp.broadcast_to(r10, n10.shape)
    small_out[3] = jnp.broadcast_to(r20, n10.shape)
    wide_out[...] = dg0
    big_out[:, 0:D] = e0
    big_out[:, D:2 * D] = h10b
    big_out[:, 2 * D:3 * D] = c0
    big_out[:, 3 * D:4 * D] = x0b
    big_out[:, 4 * D:] = g0b
    a1_out[...] = probb
    ax_out[...] = ax
    qm_out[...] = qm
    qw_out[...] = qw
    for copy in stores:
        copy.wait()


def forward(x, lengths, wqkv, wo, w1, w2, wp, bias, gains, wb, pb):
    T, D = x.shape
    S = T // 64
    FF = w1.shape[2]
    nb = (S // 2) * (D // 128)
    sd = jax.ShapeDtypeStruct
    hbm = pl.BlockSpec(memory_space=pltpu.HBM)
    vm = pl.BlockSpec(memory_space=pltpu.VMEM)
    outs = [sd((T, D), BF), sd((T, D), BF), sd((T, D), BF), sd((nb, 128, 256), BF), sd((T, D), BF),
            sd((T, D), BF), sd((T, 128), F32), sd((T, D), BF), sd((T, FF), BF), sd((T, FF), BF),
            sd((T, D), BF), sd((T, 128), F32), sd((T, D), BF),
            sd((4, S, D), F32), sd((S, 4 * D + FF), BF), sd((H * S, T), BF), sd((H * S, D), BF),
            sd((H * S, D), BF), sd((H * S, D), BF), sd((S, FF), F32), sd((S, D), F32)]
    out_specs = [hbm] * 13 + [vm] * 8
    V = pltpu.VMEM
    scratch = [V((T, D), BF), V((3, D, D), BF), V((D, D), BF), V((D, FF), BF), V((FF, D), BF),
               V((3, D, D), BF), V((D, D), BF), V((D, FF), BF), V((FF, D), BF), V((D, D), BF),
               V((T, D), BF), V((T, D), BF), V((T, D), BF), V((nb, 128, 256), BF), V((T, D), BF),
               V((T, D), BF), V((T, 128), F32), V((T, D), BF), V((T, FF), BF), V((T, FF), BF),
               V((T, D), BF), V((T, 128), F32), V((T, D), BF), V((T, D), F32), V((T, D), F32), V((S, D), F32),
               pltpu.SemaphoreType.DMA((14,)), pltpu.SemaphoreType.DMA((13,))]
    return pl.pallas_call(
        fwd_kernel, out_shape=outs, out_specs=out_specs,
        in_specs=[pl.BlockSpec(memory_space=pltpu.SMEM)] + [hbm] * 6 + [vm] * 4,
        scratch_shapes=scratch, name="encode",
        compiler_params=pltpu.CompilerParams(vmem_limit_bytes=60 << 20),
        cost_estimate=pl.CostEstimate(flops=8 * 10 ** 9, bytes_accessed=45 * 10 ** 6, transcendentals=0),
    )(lengths, x, wqkv, wo, w1, w2, wp, bias, gains, wb, pb)


class Cut:
    def __init__(self, C, Y, X, Z):
        self.C, self.Y, self.X, self.Z = C, Y, X, Z
        self.GX, self.GY = C * Y, X * Z


def chunk_copies(part, keep, send, cut, core, sems, y_first):
    copies = []
    ends = [(keep, core)] + ([(send, 1 - core)] if cut.C == 2 else [])
    for dst, c in ends:
        for y in range(cut.Y):
            if y_first:
                copies.append(pltpu.make_async_copy(part.at[y * cut.C + c], dst.at[y], sems.at[len(copies)]))
            else:
                for x in range(cut.X):
                    copies.append(pltpu.make_async_copy(
                        part.at[y * cut.C + c, x], dst.at[x, y], sems.at[len(copies)]))
    for copy in copies:
        copy.start()
    return copies


def chunk_shapes(cut, rows, lanes, y_first):
    lead = (cut.Y, cut.X) if y_first else (cut.X, cut.Y)
    shape = jax.ShapeDtypeStruct(lead + (cut.Z, rows, lanes), BF)
    return [shape] * cut.C


def norm_back(grad, n, root, gain):
    gn = grad * gain
    inner = jnp.mean(gn * n, -1, keepdims=True)
    return root * (gn - jnp.mean(gn, -1, keepdims=True) - n * inner)


def total_rows(values):
    return jnp.sum(values, 0, keepdims=True)


def lane_blocks(values, cut, width, padded, offset):
    rows = values.shape[0]
    out = []
    for x in range(cut.X):
        for z in range(cut.Z):
            start = (z * cut.X + x) * width
            pieces = []
            if offset:
                pieces.append(jnp.zeros((rows, offset), values.dtype))
            pieces.append(values[:, start:start + width])
            if padded > offset + width:
                pieces.append(jnp.zeros((rows, padded - offset - width), values.dtype))
            out.append(jnp.concatenate(pieces, 1) if len(pieces) > 1 else pieces[0])
    return out


def top_kernel(cut, PH, pos_ref, len_ref, all_ref, own_ref, rp_ref, small_ref, big_ref, dg_ref, a1_ref, ax_ref, qm_ref,
               qw_ref, xb_ref, wqkv_hbm, wo_hbm, w1_hbm, w2_hbm, wp_hbm, gain_ref, *rest):
    n_out = 6 + cut.C
    loss_out, tot_out, gx_out, fac_out, vec_out, eb_out = rest[:6]
    chunks = rest[6:n_out]
    wqkv, wo, w1, w2, wp, part, sem, osem = rest[n_out:]
    D = wo.shape[0]
    FF = w1.shape[1]
    S = own_ref.shape[0]
    R = all_ref.shape[0]
    T = xb_ref.shape[0]
    loads = [(wp_hbm, wp), (w2_hbm.at[1], w2), (w1_hbm.at[1], w1), (wo_hbm.at[1], wo)]
    for p in range(3):
        loads.append((wqkv_hbm.at[1, :, pl.ds(p * D, D)], wqkv.at[p]))
    copies = [pltpu.make_async_copy(s, d, sem.at[i]) for i, (s, d) in enumerate(loads)]
    for copy in copies:
        copy.start()
    me = pos_ref[0]
    core = pos_ref[1]

    units = all_ref[:, 0:D]
    extra = all_ref[:, D:D + 128]
    i8 = lax.broadcasted_iota(jnp.int32, (8, 128), 0)
    l8 = lax.broadcasted_iota(jnp.int32, (8, 128), 1)
    pick = jnp.where((i8 == 0) & (l8 == 0), 32.0, 0.0) + jnp.where((i8 == 0) & (l8 == 1), 1.0, 0.0)
    pick = pick + jnp.where((i8 == 1) & (l8 == 2), 1.0, 0.0)
    meta = dot(pick.astype(BF), extra, NT)
    label_row = meta[0:1, :]
    tokens = jnp.sum(meta[1:2, :], 1, keepdims=True)
    tot_out[...] = jnp.broadcast_to(tokens, tot_out.shape)
    parts = []
    BLK = min(R, 256)
    for b in range(R // BLK):
        mat = SCORE * dot(units, all_ref[b * BLK:(b + 1) * BLK, 0:D], NT)
        j = lax.broadcasted_iota(jnp.int32, (R, BLK), 0)
        target = (j % S) >= PH
        pair = ((j // S) * PH + (j % S) - PH).astype(F32)
        chosen = target & (pair == label_row[:, b * BLK:(b + 1) * BLK])
        logits = jnp.where(target, mat - jnp.where(chosen, SCORE * MARGIN, 0.0), -1e30)
        top = jnp.max(logits, 0, keepdims=True)
        parts.append(top + jnp.log(jnp.sum(jnp.exp(logits - top), 0, keepdims=True)))
    lse_row = jnp.concatenate(parts, 1) if len(parts) > 1 else parts[0]
    own_units = own_ref[:, 0:D]
    own_extra = own_ref[:, D:D + 128].astype(F32)
    own_label = 32.0 * own_extra[:, 0:1] + own_extra[:, 1:2]
    mat = SCORE * dot(own_units, units, NT)
    j = lax.broadcasted_iota(jnp.int32, (S, R), 1)
    r = lax.broadcasted_iota(jnp.int32, (S, R), 0)
    target = (j % S) >= PH
    pair = ((j // S) * PH + (j % S) - PH).astype(F32)
    chosen = target & (pair == own_label)
    logits = jnp.where(target, mat - jnp.where(chosen, SCORE * MARGIN, 0.0), -1e30)
    top = jnp.max(logits, 1, keepdims=True)
    lse = top + jnp.log(jnp.sum(jnp.exp(logits - top), 1, keepdims=True))
    loss = lse - jnp.sum(jnp.where(chosen, logits, 0.0), 1, keepdims=True)
    loss_out[...] = jnp.broadcast_to(loss, loss_out.shape)
    from_source = jnp.where(target, jnp.exp(logits - lse), 0.0) - jnp.where(chosen, 1.0, 0.0)
    pair_own = (me * PH + r - PH).astype(F32)
    source = (j % S) < PH
    chosen_t = source & (label_row == pair_own)
    logits_t = mat - jnp.where(chosen_t, SCORE * MARGIN, 0.0)
    from_target = jnp.where(source, jnp.exp(jnp.where(source, logits_t - lse_row, 0.0)), 0.0)
    from_target = from_target - jnp.where(chosen_t, 1.0, 0.0)
    glog = jnp.where(r < PH, from_source, from_target).astype(BF)
    gu = SCORE * dot(glog, units)
    squashed = jnp.tanh(rp_ref[...])
    rs = lax.rsqrt(jnp.sum(squashed * squashed, -1, keepdims=True) + EPS_UNIT)
    gt = rs * (gu - squashed * (rs * rs * jnp.sum(gu * squashed, -1, keepdims=True)))
    gr = (gt * (1.0 - squashed * squashed)).astype(BF)
    copies[0].wait()
    gx2 = dot(gr, wp[...], NT)

    n1, n2, r1, r2 = small_ref[0], small_ref[1], small_ref[2], small_ref[3]
    gz2 = norm_back(gx2, n2, r2, gain_ref[1, 1:2, :])
    gy = gz2.astype(BF)
    copies[1].wait()
    gf = (dot(gy, w2[...], NT) * dg_ref[...]).astype(BF)
    copies[2].wait()
    gh1 = gz2 + dot(gf, w1[...], NT)
    gz1 = norm_back(gh1, n1, r1, gain_ref[1, 0:1, :])
    go = gz1.astype(BF)
    copies[3].wait()
    gc = dot(go, wo[...], NT).astype(BF).astype(F32)
    gcm = head_rows(gc).astype(BF)
    for i in (4, 5, 6):
        copies[i].wait()
    gcw = dot(gcm, wqkv[2], NT).astype(BF)
    xall = xb_ref[...]
    prob = a1_ref[...].astype(F32)
    ga = dot(gcw, xall, NT)
    gs = (prob * (ga - jnp.sum(ga * prob, 1, keepdims=True))).astype(BF)
    mm = dot(gs, xall).astype(BF)
    gpq = head_fold(dot(mm, wqkv[1])).astype(BF).astype(F32) * SCALE
    gpqb = gpq.astype(BF)
    back = dot(jnp.concatenate([gs, a1_ref[...]], 0), jnp.concatenate([qw_ref[...], gcw], 0), TN)
    gx_out[...] = back
    first = gz1 + dot(gpqb, wqkv[0], NT)
    for s in range(S):
        gx_out[64 * s:64 * s + 1, :] += first[s:s + 1, :]

    fac_out[:, 0:D] = gr
    fac_out[:, D:2 * D] = gy
    fac_out[:, 2 * D:] = gf
    vec_out[0:1, :] = total_rows(gpqb.astype(F32))
    vec_out[1:2, :] = total_rows(gc)
    vec_out[2:3, :] = total_rows(go.astype(F32))
    vec_out[3:4, :] = total_rows(gh1)
    vec_out[4:5, :] = total_rows(gy.astype(F32))
    vec_out[5:6, :] = total_rows(gx2)
    vec_out[6:7, :] = total_rows(gh1 * n1)
    vec_out[7:8, :] = total_rows(gx2 * n2)
    vec_out[8:9, :] = total_rows(gr.astype(F32))
    vec_out[9:16, :] = jnp.zeros((7, D), F32)
    eb_out[...] = total_rows(gf.astype(F32))

    x0 = big_ref[:, 3 * D:4 * D].astype(F32)
    c0 = big_ref[:, 2 * D:3 * D].astype(F32)
    pad = jnp.zeros((16 - S, D), F32) if S < 16 else None
    ext = lambda v: (jnp.concatenate([v, pad], 0) if S < 16 else v).astype(BF)
    K = 2 * H * S + 2 * max(S, 16)
    left = jnp.concatenate([mm, ax_ref[...], ext(x0), ext(c0)], 0).T
    zero = lambda n, m: jnp.zeros((n, m), BF)
    hs, e = H * S, max(S, 16)
    qkv = jnp.concatenate([
        jnp.concatenate([zero(hs, D), zero(hs, D), ext(gpq), zero(e, D)], 0),
        jnp.concatenate([qm_ref[...], zero(hs, D), zero(e, D), zero(e, D)], 0),
        jnp.concatenate([zero(hs, D), gcm, zero(e, D), zero(e, D)], 0)], 1)
    outp = jnp.concatenate([zero(hs, D), zero(hs, D), zero(e, D), ext(go.astype(F32))], 0)
    wa, wb = 3 * D // cut.GY, D // cut.GY
    blk_a = lane_blocks(qkv, cut, wa, wa + wb, 0)
    blk_b = lane_blocks(outp, cut, wb, wa + wb, wa)
    kr = D // cut.GX
    for x in range(cut.X):
        for z in range(cut.Z):
            b = x * cut.Z + z
            res = dot(left, blk_a[b] + blk_b[b]).astype(BF)
            for g in range(cut.GX):
                part[g, x, z] = res[g * kr:(g + 1) * kr, :]
    outs = chunk_copies(part, chunks[0], chunks[-1], cut, core, osem, True)
    for copy in outs:
        copy.wait()


SCORE = 10.0
MARGIN = 0.3
EPS_UNIT = 1e-6
HBM = pl.BlockSpec(memory_space=pltpu.HBM)
VM = pl.BlockSpec(memory_space=pltpu.VMEM)
SM = pl.BlockSpec(memory_space=pltpu.SMEM)


def params(mb=60):
    return pltpu.CompilerParams(vmem_limit_bytes=mb << 20)


def cost(flops, nbytes):
    return pl.CostEstimate(flops=int(flops), bytes_accessed=int(nbytes), transcendentals=0)


def top(cut, pos, lengths, pall, own, rp, small, big, dg, a1, ax, qm, qw, xb, wqkv, wo, w1, w2, wp, gains):
    S = own.shape[0]
    T, D = xb.shape
    FF = w1.shape[2]
    sd = jax.ShapeDtypeStruct
    V = pltpu.VMEM
    kr, lanes = D // cut.GX, 4 * D // cut.GY
    outs = [sd((S, 128), F32), sd((8, 128), F32), sd((T, D), F32), sd((S, 2 * D + FF), BF), sd((16, D), F32),
            sd((1, FF), F32)] + chunk_shapes(cut, kr, lanes, True)
    return pl.pallas_call(
        functools.partial(top_kernel, cut, S // 2), out_shape=outs,
        in_specs=[SM, SM] + [VM] * 11 + [HBM] * 5 + [VM], out_specs=[VM] * 6 + [HBM] * cut.C,
        scratch_shapes=[V((3, D, D), BF), V((D, D), BF), V((D, FF), BF), V((FF, D), BF), V((D, D), BF),
                        V((cut.GX, cut.X, cut.Z, kr, lanes), BF),
                        pltpu.SemaphoreType.DMA((7,)), pltpu.SemaphoreType.DMA((16,))],
        name="rank_and_top_back", compiler_params=params(), cost_estimate=cost(2e9, 25e6),
    )(pos, lengths, pall, own, rp, small, big, dg, a1, ax, qm, qw, xb, wqkv, wo, w1, w2, wp, gains)


def narrow_kernel(cut, pos_ref, gx_ref, n_ref, r_ref, gain_ref, g_hbm, *rest):
    gy_out, gz_out, vec_out = rest[:3]
    chunks = rest[3:3 + cut.C]
    g, gyt, part, sem, osem = rest[3 + cut.C:]
    T, D = gx_ref.shape
    FF = g.shape[1]
    load = pltpu.make_async_copy(g_hbm, g, sem.at[0])
    load.start()
    gx = gx_ref[...]
    n = n_ref[...].astype(F32)
    gz = norm_back(gx, n, r_ref[:, 0:1], gain_ref[0, 1:2, :])
    gy = gz.astype(BF)
    gz_out[...] = gz
    gy_out[...] = gy
    gyt[...] = gy.T
    vec_out[0:1, :] = total_rows(gx)
    vec_out[1:2, :] = total_rows(gx * n)
    vec_out[2:3, :] = total_rows(gy.astype(F32))
    vec_out[3:8, :] = jnp.zeros((5, D), F32)
    load.wait()
    mw = FF // cut.GX
    nw = D // cut.GY

    def tile(i, _):
        cols = pl.ds(pl.multiple_of(i * mw, 128), mw)
        res = dot(gyt[...], g[:, cols]).astype(BF)
        for x in range(cut.X):
            for z in range(cut.Z):
                b = z * cut.X + x
                part[i, x, z] = res[b * nw:(b + 1) * nw, :]
        return 0

    lax.fori_loop(0, cut.GX, tile, 0)
    for copy in chunk_copies(part, chunks[0], chunks[-1], cut, pos_ref[1], osem, False):
        copy.wait()


def narrow(cut, pos, gx, n2, r2, gains, g):
    T, D = gx.shape
    FF = g.shape[1]
    sd = jax.ShapeDtypeStruct
    V = pltpu.VMEM
    nw, mw = D // cut.GY, FF // cut.GX
    outs = [sd((T, D), BF), sd((T, D), F32), sd((8, D), F32)] + chunk_shapes(cut, nw, mw, False)
    return pl.pallas_call(
        functools.partial(narrow_kernel, cut), out_shape=outs,
        in_specs=[SM] + [VM] * 4 + [HBM], out_specs=[VM] * 3 + [HBM] * cut.C,
        scratch_shapes=[V((T, FF), BF), V((D, T), BF), V((cut.GX, cut.X, cut.Z, nw, mw), BF),
                        pltpu.SemaphoreType.DMA((1,)), pltpu.SemaphoreType.DMA((16,))],
        name="narrowing_back", compiler_params=params(), cost_estimate=cost(2.5e9, 12e6),
    )(pos, gx, n2, r2, gains, g)


def widen_kernel(cut, pos_ref, gy_ref, hb_ref, dg_hbm, w2_hbm, *rest):
    gf_out, eb_out = rest[:2]
    chunks = rest[2:2 + cut.C]
    dg, w2, gf, hbt, part, sem, osem = rest[2 + cut.C:]
    T, D = gy_ref.shape
    FF = dg.shape[1]
    W = 768
    loads = []
    for i in range(FF // W):
        loads.append(pltpu.make_async_copy(w2_hbm.at[0, pl.ds(i * W, W), :], w2.at[pl.ds(i * W, W), :], sem.at[2 * i]))
        loads.append(pltpu.make_async_copy(dg_hbm.at[:, pl.ds(i * W, W)], dg.at[:, pl.ds(i * W, W)], sem.at[2 * i + 1]))
    for copy in loads:
        copy.start()
    hbt[...] = hb_ref[...].T
    kr = D // cut.GX
    lw = FF // cut.GY
    stores = []
    for i in range(FF // W):
        loads[2 * i].wait()
        loads[2 * i + 1].wait()
        cols = slice(i * W, (i + 1) * W)
        back = (dot(gy_ref[...], w2[cols, :], NT) * dg[:, cols].astype(F32)).astype(BF)
        gf[:, cols] = back
        stores.append(pltpu.make_async_copy(gf.at[:, pl.ds(i * W, W)], gf_out.at[:, pl.ds(i * W, W)], sem.at[8 + i]))
        stores[-1].start()
        eb_out[0:1, cols] = total_rows(back.astype(F32))
        res = dot(hbt[...], back).astype(BF)
        if cut.GY == 1:
            part[0, 0, 0, :, cols] = res
        else:
            for h in range(W // lw):
                b = (i * W) // lw + h
                for gx in range(cut.GX):
                    part[gx, b % cut.X, b // cut.X] = res[gx * kr:(gx + 1) * kr, h * lw:(h + 1) * lw]
    for copy in chunk_copies(part, chunks[0], chunks[-1], cut, pos_ref[1], osem, False):
        copy.wait()
    for copy in stores:
        copy.wait()


def widen_back(cut, pos, gy, hb, dg, w2):
    T, D = gy.shape
    FF = dg.shape[1]
    sd = jax.ShapeDtypeStruct
    V = pltpu.VMEM
    kr, lw = D // cut.GX, FF // cut.GY
    outs = [sd((T, FF), BF), sd((1, FF), F32)] + chunk_shapes(cut, kr, lw, False)
    return pl.pallas_call(
        functools.partial(widen_kernel, cut), out_shape=outs,
        in_specs=[SM, VM, VM, HBM, HBM], out_specs=[HBM, VM] + [HBM] * cut.C,
        scratch_shapes=[V((T, FF), BF), V((FF, D), BF), V((T, FF), BF), V((D, T), BF),
                        V((cut.GX, cut.X, cut.Z, kr, lw), BF),
                        pltpu.SemaphoreType.DMA((12,)), pltpu.SemaphoreType.DMA((16,))],
        name="widening_back", compiler_params=params(), cost_estimate=cost(4.9e9, 20e6),
    )(pos, gy, hb, dg, w2)


def attend_kernel(cut, pos_ref, gz2_ref, n_ref, r_ref, gain_ref, gf_hbm, w1_hbm, wo_hbm, q_hbm, k_hbm, v_hbm, a_hbm,
                  c_hbm, x_hbm, *rest):
    gz_out, gp_out, vec_out = rest[:3]
    chunks = rest[3:3 + cut.C]
    gf, w1, wo, q, k, v, a, c, x, gc, gp, xt, ct, part, sem, osem = rest[3 + cut.C:]
    T, D = gz2_ref.shape
    S = T // 64
    loads = [(gf_hbm, gf), (w1_hbm.at[0], w1), (wo_hbm.at[0], wo), (k_hbm, k), (v_hbm, v), (q_hbm, q), (a_hbm, a),
             (c_hbm, c), (x_hbm, x)]
    copies = [pltpu.make_async_copy(s, d, sem.at[i]) for i, (s, d) in enumerate(loads)]
    for copy in copies:
        copy.start()
    copies[0].wait()
    copies[1].wait()
    gh = gz2_ref[...] + dot(gf[...], w1[...], NT)
    n = n_ref[...].astype(F32)
    gz = norm_back(gh, n, r_ref[:, 0:1], gain_ref[0, 0:1, :])
    gz_out[...] = gz
    go = gz.astype(BF)
    vec_out[3:4, :] = total_rows(gh)
    vec_out[6:7, :] = total_rows(gh * n)
    vec_out[2:3, :] = total_rows(go.astype(F32))
    copies[2].wait()
    gc[...] = dot(go, wo[...], NT).astype(BF)
    for i in range(3, 9):
        copies[i].wait()
    lane = lax.broadcasted_iota(jnp.int32, (128, 128), 1)
    low = lane < HD
    NB = D // 128

    def heads(p, _):
        rows = pl.ds(pl.multiple_of(p * 128, 128), 128)
        for j in range(NB):
            lanes = slice(128 * j, 128 * j + 128)
            gcj = gc[rows, lanes]
            gcm = jnp.concatenate([jnp.where(low, gcj, 0), jnp.where(low, 0, gcj)], 0)
            qj = q[rows, lanes]
            qm = jnp.concatenate([jnp.where(low, qj, 0), jnp.where(low, 0, qj)], 0)
            pb = a[p * NB + j]
            prob = pb.astype(F32)
            gp[rows, 2 * D + 128 * j:2 * D + 128 * j + 128] = dot(pb, gcm).astype(BF)
            ga = dot(v[rows, lanes], gcm, NT)
            gs = (prob * (ga - jnp.sum(ga * prob, 0, keepdims=True))).astype(BF)
            gp[rows, D + 128 * j:D + 128 * j + 128] = dot(gs, qm).astype(BF)
            gq = dot(gs, k[rows, lanes], TN)
            gq = jnp.where(low, gq[:128], gq[128:]).astype(BF)
            gp[rows, lanes] = (gq.astype(F32) * SCALE).astype(BF)
        return 0

    lax.fori_loop(0, S // 2, heads, 0)
    gpv = gp[...]
    vec_out[0:1, :] = total_rows(gpv[:, 0:D].astype(F32))
    vec_out[1:2, :] = total_rows(gpv[:, 2 * D:].astype(F32))
    store = pltpu.make_async_copy(gp, gp_out, sem.at[9])
    store.start()
    xt[...] = x[...].T
    ct[...] = c[...].T
    wa, wb = 3 * D // cut.GY, D // cut.GY
    main = wa // 128 * 128
    kr = D // cut.GX
    for xi in range(cut.X):
        for z in range(cut.Z):
            start = (z * cut.X + xi) * wa
            res = dot(xt[...], gpv[:, start:start + main]).astype(BF)
            for g in range(cut.GX):
                part[g, xi, z, :, 0:main] = res[g * kr:(g + 1) * kr, :]
            ob = (z * cut.X + xi) * wb
            if wa > main:
                tail = wa - main
                ra = jnp.concatenate([gpv[:, start + main:start + wa], jnp.zeros((T, 128 - tail), BF)], 1)
                rb = jnp.concatenate([jnp.zeros((T, tail), BF), go[:, ob:ob + wb]], 1)
                res = (dot(xt[...], ra) + dot(ct[...], rb)).astype(BF)
            else:
                res = dot(ct[...], go[:, ob:ob + wb]).astype(BF)
            for g in range(cut.GX):
                part[g, xi, z, :, main:] = res[g * kr:(g + 1) * kr, :]
    for copy in chunk_copies(part, chunks[0], chunks[-1], cut, pos_ref[1], osem, True):
        copy.wait()
    store.wait()


def attend_back(cut, pos, gz2, n1, r1, gains, gf, w1, wo, q, k, v, a, c, x):
    T, D = gz2.shape
    FF = gf.shape[1]
    sd = jax.ShapeDtypeStruct
    V = pltpu.VMEM
    kr, lanes = D // cut.GX, 4 * D // cut.GY
    outs = [sd((T, D), F32), sd((T, 3 * D), BF), sd((8, D), F32)] + chunk_shapes(cut, kr, lanes, True)
    td = V((T, D), BF)
    return pl.pallas_call(
        functools.partial(attend_kernel, cut), out_shape=outs,
        in_specs=[SM] + [VM] * 4 + [HBM] * 9, out_specs=[VM, HBM, VM] + [HBM] * cut.C,
        scratch_shapes=[V((T, FF), BF), V((D, FF), BF), V((D, D), BF), td, td, td, V(a.shape, BF), td, td, td,
                        V((T, 3 * D), BF), V((D, T), BF), V((D, T), BF), V((cut.GX, cut.X, cut.Z, kr, lanes), BF),
                        pltpu.SemaphoreType.DMA((10,)), pltpu.SemaphoreType.DMA((16,))],
        name="attention_back", compiler_params=params(), cost_estimate=cost(7e9, 30e6),
    )(pos, gz2, n1, r1, gains, gf, w1, wo, q, k, v, a, c, x)


def input_kernel(pairs, len_ref, tot_ref, gz_ref, gp_hbm, w_hbm, gx_out, sc_out, gp, w, sem):
    T, D = gz_ref.shape
    copies = []
    for part in range(3):
        cols = pl.ds(part * D, D)
        copies.append(pltpu.make_async_copy(gp_hbm.at[:, cols], gp.at[part], sem.at[2 * part]))
        copies.append(pltpu.make_async_copy(w_hbm.at[0, :, cols], w.at[part], sem.at[2 * part + 1]))
    for copy in copies:
        copy.start()
    grad = gz_ref[...]
    for part in range(3):
        copies[2 * part].wait()
        copies[2 * part + 1].wait()
        grad = grad + dot(gp[part], w[part], NT)
    gx_out[...] = grad
    inverse = 1.0 / tot_ref[0:1, 0:1]
    for s in range(T // 64):
        rows = slice(64 * s, 64 * s + 64)
        factor = (2.0 * pairs) * len_ref[s].astype(F32) * inverse
        sc_out[rows, :] = grad[rows, :] * factor


def input_back(pairs, lengths, tot, gz1, gp, wqkv):
    T, D = gz1.shape
    sd = jax.ShapeDtypeStruct
    return pl.pallas_call(
        functools.partial(input_kernel, pairs), out_shape=[sd((T, D), F32)] * 2,
        in_specs=[SM, VM, VM, HBM, HBM], out_specs=[VM, VM],
        scratch_shapes=[pltpu.VMEM((3, T, D), BF), pltpu.VMEM((3, D, D), BF), pltpu.SemaphoreType.DMA((6,))],
        name="input_back", compiler_params=params(), cost_estimate=cost(1.9e9, 12e6),
    )(lengths, tot, gz1, gp, wqkv)


def payload(n, labels, lengths, rp):
    squashed = jnp.tanh(rp)
    unit = squashed * lax.rsqrt(jnp.sum(squashed * squashed, -1, keepdims=True) + EPS_UNIT)
    S, D = rp.shape
    lab = jnp.concatenate([labels, jnp.zeros((S - labels.shape[0],), jnp.int32)])
    tail = jnp.stack([lab // 32, lab % 32, lengths.reshape(S)], 1).astype(F32)
    tail = jnp.concatenate([tail, jnp.zeros((S, 125), F32)], 1)
    return jnp.concatenate([unit, tail], 1).astype(BF)


def halve(keep, send, axis, flip, bit, last):
    n = lax.axis_size(axis)
    got = lax.ppermute(send, axis, [(i, i ^ flip) for i in range(n)])
    total = (keep.astype(F32) + got.astype(F32)).astype(BF)
    if last:
        return total
    pick = lambda b: lax.dynamic_index_in_dim(total, b, 0, keepdims=False)
    return pick(bit), pick(1 - bit)


def share_sum(keep, send, y_first):
    gx, gy = lax.axis_index("gx"), lax.axis_index("gy")
    y, x, z = gx // 2, gy % 2, gy // 2
    steps = (("gx", 2, y), ("gy", 1, x)) if y_first else (("gy", 1, x), ("gx", 2, y))
    keep, send = halve(keep, send, "gx", 1, steps[0][2], False)
    keep, send = halve(keep, send, steps[0][0], steps[0][1], steps[1][2], False)
    total = halve(keep, send, steps[1][0], steps[1][1], 0, True)
    pick = lambda b: lax.dynamic_index_in_dim(total, b, 0, keepdims=False)
    out = pick(z).astype(F32)
    for d in (1, 2, 3):
        got = lax.ppermute(pick(z ^ d), "gy", [(i, i ^ (2 * d)) for i in range(8)])
        out = out + got.astype(F32)
    return out


def scatter(values, row_axis, col_axis):
    part = lax.psum_scatter(values, row_axis, scatter_dimension=0, tiled=True)
    return lax.psum_scatter(part, col_axis, scatter_dimension=1, tiled=True).astype(F32)


def shards(mesh, inputs, lengths, labels, wqkv, wo, w1, w2, bias, gains, wb, wp, pb):
    GX, GY = mesh.shape["gx"], mesh.shape["gy"]
    n = GX * GY
    cut = Cut(2, 2, 2, 4) if (GX, GY) == (4, 8) else Cut(1, 1, 1, 1)
    axes = ("gx", "gy")
    PH = labels.shape[0]
    S = 2 * PH
    L, D = inputs.shape[2], inputs.shape[3]
    T = S * L
    FF = w1.shape[2]
    gxi, gyi = lax.axis_index("gx"), lax.axis_index("gy")
    pos = jnp.stack([gxi * GY + gyi, gxi % 2]).astype(jnp.int32)
    lens = lengths.reshape(S)
    x = inputs.reshape(T, D)
    (q, k, v, a, c, n1, r1, hb, g, dg, n2, r2, xb, small, big, a1, ax, qm, qw, dg1, rp) = forward(
        x, lens, wqkv, wo, w1, w2, wp, bias, gains, wb, pb[None])
    own = payload(n, labels, lens, rp)
    pall = lax.all_to_all(jnp.broadcast_to(own[None], (n,) + own.shape), axes, 0, 0).reshape(n * S, D + 128)
    loss, tot, gx1, fac, vec1, eb1, *ch1 = top(
        cut, pos, lens, pall, own, rp, small, big, dg1, a1, ax, qm, qw, xb, wqkv, wo, w1, w2, wp, gains)
    gy, gz2, vec2, *ch2 = narrow(cut, pos, gx1, n2, r2, gains, g)
    gf, eb0, *ch3 = widen_back(cut, pos, gy, hb, dg, w2)
    gz1, gp, vec4, *ch4 = attend_back(cut, pos, gz2, n1, r1, gains, gf, w1, wo, q, k, v, a, c, x)
    gx0, sc0 = input_back(n * PH, lens, tot, gz1, gp, wqkv)

    e0, h1b, g1b = big[:, 0:D], big[:, D:2 * D], big[:, 4 * D:]
    gr, gy1, gf1 = fac[:, 0:D], fac[:, D:2 * D], fac[:, 2 * D:]
    rowsplit = jnp.concatenate([t.reshape(S, GX, -1) for t in (e0, h1b, g1b)], 2)
    colsplit = jnp.concatenate([t.reshape(S, GY, -1) for t in (gr, gy1, gf1)], 2)
    wr, wc = rowsplit.shape[2], colsplit.shape[2]
    pair = jnp.concatenate([
        jnp.broadcast_to(rowsplit.transpose(1, 0, 2)[:, None], (GX, GY, S, wr)),
        jnp.broadcast_to(colsplit.transpose(1, 0, 2)[None], (GX, GY, S, wc))], 3).reshape(n, S, wr + wc)
    rows = lax.all_to_all(pair, axes, 0, 0).reshape(n * S, wr + wc)
    left, right = rows[:, :wr], rows[:, wr:]
    dk, dn = D // GX, D // GY
    tn = lambda p, r: lax.dot_general(p, r, TN, preferred_element_type=F32)
    d_pool = tn(left[:, :dk], right[:, :dn])
    d_expand1 = tn(left[:, dk:2 * dk], right[:, 2 * dn:])
    d_reduce1 = tn(left[:, 2 * dk:], right[:, dn:2 * dn])

    vecs = jnp.concatenate([vec4[0:4], vec2[2:3], vec2[0:1], vec1[0:6], vec4[6:7], vec2[1:2], vec1[6:8], vec1[8:9],
                            eb0.reshape(4, D), eb1.reshape(4, D)], 0)
    flat = jnp.concatenate([vecs[:17].reshape(17, n, -1).transpose(1, 0, 2).reshape(n, -1),
                            vecs[17:].reshape(2, n, -1).transpose(1, 0, 2).reshape(n, -1)], 1)
    width = flat.shape[1]
    flat = jnp.pad(flat, ((0, 0), (0, -width % 128))).astype(BF)
    mine = jnp.sum(lax.all_to_all(flat[:, None, :], axes, 0, 0).astype(F32), (0, 1))[:width]
    dv = D // n
    vec = mine[:17 * dv].reshape(17, dv)
    d_bias = vec[0:12].reshape(2, 6, dv)
    d_gains = vec[12:16].reshape(2, 2, dv)
    d_pool_bias = vec[16]
    d_wb = mine[17 * dv:].reshape(2, FF // n)

    wa = 3 * D // GY
    if cut.C == 2:
        s1 = share_sum(*ch1, True)
        s2 = share_sum(*ch2, False)
        s3 = share_sum(*ch3, False)
        s4 = share_sum(*ch4, True)
        d_attend = jnp.stack([s4[:, :wa], s1[:, :wa]])
        d_output = jnp.stack([s4[:, wa:], s1[:, wa:]])
        d_reduce0 = s2.T
        d_expand0 = s3
    else:
        f1, f2, f3, f4 = (t[0].reshape(t[0].shape[-2:]) for t in (ch1, ch2, ch3, ch4))
        d_attend = jnp.stack([scatter(t[:, :3 * D], "gx", "gy") for t in (f4, f1)])
        d_output = jnp.stack([scatter(t[:, 3 * D:], "gx", "gy") for t in (f4, f1)])
        d_reduce0 = scatter(f2, "gy", "gx").T
        d_expand0 = scatter(f3, "gx", "gy")
    shape = (2, PH, L, D)
    return (loss[:PH, 0], gx0.reshape(shape), sc0.reshape(shape), d_attend, d_output,
            jnp.stack([d_expand0, d_expand1]), jnp.stack([d_reduce0, d_reduce1]),
            d_bias, d_gains, d_wb, d_pool, d_pool_bias)


def solution(mesh):
    both = ("gx", "gy")
    in_specs = (P(None, both, None, None), P(None, both), P(both)) + (P(),) * 9
    out_specs = (P(both), P(None, both, None, None), P(None, both, None, None), P(None, "gx", "gy"),
                 P(None, "gx", "gy"), P(None, "gx", "gy"), P(None, "gx", "gy"), P(None, None, both),
                 P(None, None, both), P(None, both), P("gx", "gy"), P(both))
    return jax.shard_map(functools.partial(shards, mesh), mesh=mesh, in_specs=in_specs, out_specs=out_specs,
                         check_vma=False)
```

```python
import functools
import jax
import jax.numpy as jnp
from jax import lax
from jax.sharding import PartitionSpec as P
from jax.experimental import pallas as pl
from jax.experimental.pallas import tpu as pltpu

H = 12
HD = 64


class Cut:
    def __init__(self, C, Y, X, Z):
        self.C, self.Y, self.X, self.Z = C, Y, X, Z
        self.GX, self.GY = C * Y, X * Z


BF = jnp.bfloat16
F32 = jnp.float32
ROOT_HALF = 0.7071067811865476
PHI_ZERO = 0.3989422804014327
MASKED = -1e9
EPS_NORM = 1e-12
EPS_UNIT = 1e-6
SCORE = 10.0
MARGIN = 0.3
SCALE = HD ** -0.5

NN = (((1,), (0,)), ((), ()))
NT = (((1,), (1,)), ((), ()))
TN = (((0,), (0,)), ((), ()))


def place():
    gx, gy = lax.axis_index("gx"), lax.axis_index("gy")
    return gx, lax.rem(gx, 2), lax.div(gx, 2), lax.rem(gy, 2), lax.div(gy, 2), gy


def dot(a, b, dims=NN):
    return lax.dot_general(a, b, dims, preferred_element_type=F32)


def normalize(z):
    centered = z - jnp.mean(z, -1, keepdims=True)
    variance = jnp.mean(centered * centered, -1, keepdims=True)
    root = lax.rsqrt(variance + EPS_NORM)
    return centered * root, root


def gelu_pair(f):
    cdf = 0.5 * (1.0 + lax.erf(f * ROOT_HALF))
    return f * cdf, cdf + f * (PHI_ZERO * jnp.exp(-0.5 * f * f))


def head_rows(values):
    lanes = lax.broadcasted_iota(jnp.int32, values.shape, 1) // HD
    return jnp.concatenate([jnp.where(lanes == h, values, 0) for h in range(H)], 0)


def head_fold(values):
    r = values.shape[0] // H
    lanes = lax.broadcasted_iota(jnp.int32, (r, values.shape[1]), 1) // HD
    out = jnp.zeros((r, values.shape[1]), values.dtype)
    for h in range(H):
        out = jnp.where(lanes == h, values[h * r:(h + 1) * r], out)
    return out


def by_core(cut, src, act, slot):
    if cut.C == 1:
        act[0, slot] = src[...]
        return
    width = src.shape[1] // cut.GX
    for ci in range(2):
        act[ci, slot] = jnp.concatenate(
            [src[:, (2 * y + ci) * width:(2 * y + ci + 1) * width] for y in range(cut.Y)], 1)


def fwd_kernel(cut, len_ref, lab_ref, x_hbm, wqkv_hbm, wo_hbm, w1_hbm, w2_hbm, wp_hbm, bias_ref, gain_ref, wb_ref, pb_ref,
               q_out, k_out, v_out, a_out, n1_out, r1_out, dg_out, n2_out, r2_out, xb_out,
               small_out, big_out, a1_out, ax_out, qm_out, qw_out, wide_out, rp_out, pay_out, *rest):
    acts = rest[:cut.C]
    (x, wqkv, wo, w1, w2, wqkv1, wo1, w11, w21, wp,
     q, k, v, a, c, n1, r1, hb, dg, n2, r2, xb, h1, acc, first, act, sem, osem) = rest[cut.C:]
    core = place()[1]
    PH = lab_ref.shape[0]
    tokens = lambda s: len_ref[s // PH, s % PH]
    T, D = x.shape
    S = T // 64
    FF = w1.shape[1]
    loads = [(x_hbm, x)]
    for part in range(3):
        cols = pl.ds(part * D, D)
        loads.append((wqkv_hbm.at[0, :, cols], wqkv.at[part]))
    loads += [(wo_hbm.at[0], wo), (w1_hbm.at[0], w1), (w2_hbm.at[0], w2)]
    for part in range(3):
        cols = pl.ds(part * D, D)
        loads.append((wqkv_hbm.at[1, :, cols], wqkv1.at[part]))
    loads += [(wo_hbm.at[1], wo1), (w1_hbm.at[1], w11), (w2_hbm.at[1], w21), (wp_hbm, wp)]
    copies = [pltpu.make_async_copy(s, d, sem.at[i]) for i, (s, d) in enumerate(loads)]
    for copy in copies:
        copy.start()
    stores = []

    def store(src, dst):
        copy = pltpu.make_async_copy(src, dst, osem.at[len(stores)])
        copy.start()
        stores.append(copy)

    copies[0].wait()
    TILE = 256
    for part, dst in enumerate((q, k, v)):
        copies[1 + part].wait()

        def project(j, _, part=part, dst=dst):
            cols = pl.ds(pl.multiple_of(j * TILE, TILE), TILE)
            p = dot(x[...], wqkv[part, :, cols])
            if part == 0:
                p = (p + bias_ref[0:1, 0, cols]) * SCALE
            if part == 2:
                p = p + bias_ref[1:2, 0, cols]
            dst[:, cols] = p.astype(BF)
            return 0

        lax.fori_loop(0, D // TILE, project, 0)
    store(q, q_out)
    store(k, k_out)
    store(v, v_out)

    key = lax.broadcasted_iota(jnp.int32, (128, 256), 0)
    query = lax.broadcasted_iota(jnp.int32, (128, 256), 1)
    lane = lax.broadcasted_iota(jnp.int32, (128, 128), 1)
    low = lane < HD

    def attend(p, _):
        rows = pl.ds(pl.multiple_of(p * 128, 128), 128)
        i = 2 * p
        limit = jnp.where(key < 64, len_ref[i // PH, i % PH], len_ref[i // PH, i % PH + 1] + 64)
        keep = ((key // 64) == ((query // 64) % 2)) & (key < limit)
        for j in range(D // 128):
            lanes = slice(128 * j, 128 * j + 128)
            qq = q[rows, lanes]
            qm = jnp.concatenate([jnp.where(low, qq, 0), jnp.where(low, 0, qq)], 0)
            s = jnp.where(keep, dot(k[rows, lanes], qm, NT), MASKED)
            e = jnp.exp(s - jnp.max(s, 0, keepdims=True))
            prob = (e * (1.0 / jnp.sum(e, 0, keepdims=True))).astype(BF)
            a[p * (D // 128) + j] = prob
            ctx = dot(prob, v[rows, lanes], TN)
            c[rows, lanes] = jnp.where(low, ctx[:128], ctx[128:]).astype(BF)
        return 0

    lax.fori_loop(0, S // 2, attend, 0)
    store(a, a_out)
    by_core(cut, c, act, 5)
    by_core(cut, x, act, 6)

    copies[4].wait()
    ROWS = 256

    def first_norm(i, _):
        rows = pl.ds(pl.multiple_of(i * ROWS, ROWS), ROWS)
        z = x[rows, :].astype(F32) + dot(c[rows, :], wo[...]) + bias_ref[2:3, 0, :]
        n, r = normalize(z)
        n1[rows, :] = n.astype(BF)
        r1[rows, :] = jnp.broadcast_to(r, (ROWS, 128))
        h = n * gain_ref[0, 0:1, :] + bias_ref[3:4, 0, :]
        h1[rows, :] = h
        hb[rows, :] = h.astype(BF)
        acc[rows, :] = h + bias_ref[4:5, 0, :]
        return 0

    lax.fori_loop(0, T // ROWS, first_norm, 0)
    store(n1, n1_out)
    store(r1, r1_out)
    by_core(cut, hb, act, 4)
    copies[5].wait()
    copies[6].wait()

    WIDE = D // cut.C
    for y in range(4 // cut.C):
        for ci in range(cut.C):
            for half in range(cut.C):
                start = (cut.C * y + ci) * cut.C * WIDE + half * WIDE
                cols = slice(start, start + WIDE)
                f = dot(hb[...], w1[:, cols]) + wb_ref[0:1, cols]
                gj, dgj = gelu_pair(f)
                gj = gj.astype(BF)
                act[ci, cut.C * y + half] = gj
                dg[:, cols] = dgj.astype(BF)
                acc[...] += dot(gj, w2[cols, :])
    store(dg, dg_out)
    store(act.at[core], acts[0])
    if cut.C == 2:
        store(act.at[1 - core], acts[1])

    def second_norm(i, _):
        rows = pl.ds(pl.multiple_of(i * ROWS, ROWS), ROWS)
        n, r = normalize(acc[rows, :])
        n2[rows, :] = n.astype(BF)
        r2[rows, :] = jnp.broadcast_to(r, (ROWS, 128))
        h = n * gain_ref[0, 1:2, :] + bias_ref[5:6, 0, :]
        acc[rows, :] = h
        xb[rows, :] = h.astype(BF)
        return 0

    lax.fori_loop(0, T // ROWS, second_norm, 0)
    store(n2, n2_out)
    store(r2, r2_out)
    store(xb, xb_out)

    for s in range(S):
        first[s:s + 1, :] = acc[64 * s:64 * s + 1, :]
    x0 = first[...]
    x0b = x0.astype(BF)
    for i in (7, 8, 9):
        copies[i].wait()
    q0 = ((dot(x0b, wqkv1[0]) + bias_ref[0:1, 1, :]) * SCALE).astype(BF)
    qm = head_rows(q0.astype(F32)).astype(BF)
    qw = dot(qm, wqkv1[1], NT).astype(BF)
    xall = xb[...]
    scores = dot(qw, xall, NT)
    row = lax.broadcasted_iota(jnp.int32, scores.shape, 0) % S
    col = lax.broadcasted_iota(jnp.int32, scores.shape, 1)
    keep = jnp.zeros(scores.shape, jnp.bool_)
    for s in range(S):
        keep = keep | ((row == s) & (col >= 64 * s) & (col < 64 * s + tokens(s)))
    scores = jnp.where(keep, scores, MASKED)
    e = jnp.exp(scores - jnp.max(scores, 1, keepdims=True))
    prob = e * (1.0 / jnp.sum(e, 1, keepdims=True))
    probb = prob.astype(BF)
    ax = dot(probb, xall).astype(BF)
    c0 = (head_fold(dot(ax, wqkv1[2])) + bias_ref[1:2, 1, :]).astype(BF)
    copies[10].wait()
    n10, r10 = normalize(x0 + dot(c0, wo1[...]) + bias_ref[2:3, 1, :])
    h10 = n10 * gain_ref[1, 0:1, :] + bias_ref[3:4, 1, :]
    h10b = h10.astype(BF)
    copies[11].wait()
    f0 = dot(h10b, w11[...]) + wb_ref[1:2, :]
    g0, dg0 = gelu_pair(f0)
    g0b = g0.astype(BF)
    copies[12].wait()
    n20, r20 = normalize(h10 + dot(g0b, w21[...]) + bias_ref[4:5, 1, :])
    x20 = n20 * gain_ref[1, 1:2, :] + bias_ref[5:6, 1, :]
    e0 = x20.astype(BF)
    copies[13].wait()
    rp = dot(e0, wp[...]) + pb_ref[...].reshape(1, D)
    rp_out[...] = rp
    squashed = jnp.tanh(rp)
    unit = squashed * lax.rsqrt(jnp.sum(squashed * squashed, -1, keepdims=True) + EPS_UNIT)
    row = lax.broadcasted_iota(jnp.int32, (S, 128), 0)
    lane = lax.broadcasted_iota(jnp.int32, (S, 128), 1)
    tail = jnp.zeros((S, 128), F32)
    for s in range(S):
        if s < PH:
            label = lab_ref[s]
            tail = jnp.where((row == s) & (lane == 0), (label // 32).astype(F32), tail)
            tail = jnp.where((row == s) & (lane == 1), (label % 32).astype(F32), tail)
        tail = jnp.where((row == s) & (lane == 2), tokens(s).astype(F32), tail)
    pay_out[...] = jnp.concatenate([unit, tail], 1).astype(BF)
    small_out[0] = n10
    small_out[1] = n20
    small_out[2] = jnp.broadcast_to(r10, n10.shape)
    small_out[3] = jnp.broadcast_to(r20, n10.shape)
    wide_out[...] = dg0
    big_out[:, 0:D] = e0
    big_out[:, D:2 * D] = h10b
    big_out[:, 2 * D:3 * D] = c0
    big_out[:, 3 * D:4 * D] = x0b
    big_out[:, 4 * D:] = g0b
    a1_out[...] = probb
    ax_out[...] = ax
    qm_out[...] = qm
    qw_out[...] = qw
    for copy in stores:
        copy.wait()


def forward(cut, x, lengths, labels, wqkv, wo, w1, w2, wp, bias, gains, wb, pb):
    T, D = x.shape
    S = T // 64
    FF = w1.shape[2]
    nb = (S // 2) * (D // 128)
    sd = jax.ShapeDtypeStruct
    hbm = pl.BlockSpec(memory_space=pltpu.HBM)
    vm = pl.BlockSpec(memory_space=pltpu.VMEM)
    td = sd((T, D), BF)
    tr = sd((T, 128), F32)
    outs = [td, td, td, sd((nb, 128, 256), BF), td, tr, sd((T, FF), BF), td, tr, td,
            sd((4, S, D), F32), sd((S, 4 * D + FF), BF), sd((H * S, T), BF), sd((H * S, D), BF),
            sd((H * S, D), BF), sd((H * S, D), BF), sd((S, FF), F32), sd((S, D), F32), sd((S, D + 128), BF)]
    outs += [sd((7, T, D // cut.C), BF)] * cut.C
    out_specs = [hbm] * 10 + [vm] * 9 + [hbm] * cut.C
    V = pltpu.VMEM
    b, r = V((T, D), BF), V((T, 128), F32)
    scratch = [b, V((3, D, D), BF), V((D, D), BF), V((D, FF), BF), V((FF, D), BF),
               V((3, D, D), BF), V((D, D), BF), V((D, FF), BF), V((FF, D), BF), V((D, D), BF),
               b, b, b, V((nb, 128, 256), BF), b, b, r, b, V((T, FF), BF), b, r, b,
               V((T, D), F32), V((T, D), F32), V((S, D), F32), V((cut.C, 7, T, D // cut.C), BF),
               pltpu.SemaphoreType.DMA((14,)), pltpu.SemaphoreType.DMA((12,))]
    return pl.pallas_call(
        functools.partial(fwd_kernel, cut), out_shape=outs, out_specs=out_specs,
        in_specs=[pl.BlockSpec(memory_space=pltpu.SMEM)] * 2 + [hbm] * 6 + [vm] * 4,
        scratch_shapes=scratch, name="encode",
        compiler_params=pltpu.CompilerParams(vmem_limit_bytes=55 << 20),
    )(lengths, labels, x, wqkv, wo, w1, w2, wp, bias, gains, wb, pb)


HBM = pl.BlockSpec(memory_space=pltpu.HBM)
VM = pl.BlockSpec(memory_space=pltpu.VMEM)
SM = pl.BlockSpec(memory_space=pltpu.SMEM)


def norm_back(grad, n, root, gain):
    gn = grad * gain
    inner = jnp.mean(gn * n, -1, keepdims=True)
    return root * (gn - jnp.mean(gn, -1, keepdims=True) - n * inner)


def total_rows(values):
    return jnp.sum(values, 0, keepdims=True)


def emit(cut, parts, outs):
    if cut.C == 1:
        outs[0][...] = parts[0][...]
        return
    ybit, xbit = place()[2:4]
    n = len(outs) // 2
    for part, bit, (keep, *sends) in ((parts[0], ybit, outs[:n]), (parts[1], xbit, outs[n:])):
        keep[...] = part[bit]
        for i, send in enumerate(sends):
            send[...] = part[1 - bit] if n == 2 else part[1 - bit, i // 2, i % 2]


def pieces(cut, rows, lanes, fine=False):
    if cut.C == 1:
        return [pltpu.VMEM((1, 1, 1, rows, lanes), BF)], [sds((1, 1, 1, rows, lanes), BF)]
    whole, block = sds((2, 2, rows, lanes), BF), sds((rows, lanes), BF)
    return [pltpu.VMEM((2, 2, 2, rows, lanes), BF)] * 2, [whole, *([block] * 4 if fine else [whole])] * 2


def put(cut, parts, y, x, z, value, rows=slice(None), lanes=slice(None)):
    if cut.C == 1 or z < 2:
        parts[0][y, x, z, rows, lanes] = value
    else:
        parts[1][x, y, z - 2, rows, lanes] = value


def start_all(pairs, sem):
    copies = [pltpu.make_async_copy(s, d, sem.at[i]) for i, (s, d) in enumerate(pairs)]
    for copy in copies:
        copy.start()
    return copies


def top_kernel(cut, PH, count, gain_ref, *refs):
    (own_hbm, rp_hbm, small_hbm, big_hbm, dg_hbm, a1_hbm, ax_hbm, qm_hbm, qw_hbm, xb_hbm, n2_hbm, r2_hbm,
     wqkv_hbm, wo_hbm, w1_hbm, w2_hbm, wp_hbm), rest = refs[:17], refs[17:]
    bufs, rest = rest[-13:-1], rest[:-13] + rest[-1:]
    (own_ref, rp_ref, small_ref, big_ref, dg_ref, a1_ref, ax_ref, qm_ref, qw_ref, xb_ref, n2_ref, r2_ref) = bufs
    early = start_all(list(zip(refs[:12], bufs)), rest[-1].at[pl.ds(7, 12)])
    gathered = rest[:count]
    (loss_out, tot_out, gy_out, gz_out, vec_out, eb_out), rest = rest[count:count + 6], rest[count + 6:]
    (stay_out, go_out), rest = (rest[0], rest[1 if cut.C == 2 else 0]), rest[cut.C:]
    wqkv, wo, w1, w2, wp, gx, left_s, sem = rest
    D = wo.shape[0]
    FF = w1.shape[1]
    for copy in early:
        copy.wait()
    S = own_ref.shape[0]
    R = sum(g.shape[0] for g in gathered)
    T = xb_ref.shape[0]
    loads = [(wp_hbm, wp), (w2_hbm.at[1], w2), (w1_hbm.at[1], w1), (wo_hbm.at[1], wo)]
    for p in range(3):
        loads.append((wqkv_hbm.at[1, :, pl.ds(p * D, D)], wqkv.at[p]))
    copies = [pltpu.make_async_copy(s, d, sem.at[i]) for i, (s, d) in enumerate(loads)]
    for copy in copies:
        copy.start()
    gxi, gyi = place()[0], place()[5]
    me = gxi * lax.axis_size("gy") + gyi

    def device(j):
        r = j // S
        if cut.C == 1:
            return r
        flips = ((r // 8) % 2 * 2 + r // 16) * 8 + r % 4 * 2 + (r // 4) % 2
        return me ^ flips


    everyone = jnp.concatenate([g[...] for g in gathered], 0) if count > 1 else gathered[0][...]
    units = everyone[:, 0:D]
    extra = everyone[:, D:D + 128]
    i8 = lax.broadcasted_iota(jnp.int32, (8, 128), 0)
    l8 = lax.broadcasted_iota(jnp.int32, (8, 128), 1)
    pick = jnp.where((i8 == 0) & (l8 == 0), 32.0, 0.0) + jnp.where((i8 == 0) & (l8 == 1), 1.0, 0.0)
    pick = pick + jnp.where((i8 == 1) & (l8 == 2), 1.0, 0.0)
    meta = dot(pick.astype(BF), extra, NT)
    label_row = meta[0:1, :]
    tokens = jnp.sum(meta[1:2, :], 1, keepdims=True)
    tot_out[...] = jnp.broadcast_to(tokens, tot_out.shape)
    parts = []
    BLK = min(R, 256)
    for b in range(R // BLK):
        mat = SCORE * dot(units, units[b * BLK:(b + 1) * BLK, :], NT)
        j = lax.broadcasted_iota(jnp.int32, (R, BLK), 0)
        target = (j % S) >= PH
        pair = (device(j) * PH + (j % S) - PH).astype(F32)
        chosen = target & (pair == label_row[:, b * BLK:(b + 1) * BLK])
        logits = jnp.where(target, mat - jnp.where(chosen, SCORE * MARGIN, 0.0), -1e30)
        top = jnp.max(logits, 0, keepdims=True)
        parts.append(top + jnp.log(jnp.sum(jnp.exp(logits - top), 0, keepdims=True)))
    lse_row = jnp.concatenate(parts, 1) if len(parts) > 1 else parts[0]
    own_units = own_ref[:, 0:D]
    own_extra = own_ref[:, D:D + 128].astype(F32)
    own_label = 32.0 * own_extra[:, 0:1] + own_extra[:, 1:2]
    mat = SCORE * dot(own_units, units, NT)
    j = lax.broadcasted_iota(jnp.int32, (S, R), 1)
    r = lax.broadcasted_iota(jnp.int32, (S, R), 0)
    target = (j % S) >= PH
    pair = (device(j) * PH + (j % S) - PH).astype(F32)
    chosen = target & (pair == own_label)
    logits = jnp.where(target, mat - jnp.where(chosen, SCORE * MARGIN, 0.0), -1e30)
    top = jnp.max(logits, 1, keepdims=True)
    lse = top + jnp.log(jnp.sum(jnp.exp(logits - top), 1, keepdims=True))
    loss = lse - jnp.sum(jnp.where(chosen, logits, 0.0), 1, keepdims=True)
    loss_out[...] = jnp.broadcast_to(loss, loss_out.shape)
    from_source = jnp.where(target, jnp.exp(logits - lse), 0.0) - jnp.where(chosen, 1.0, 0.0)
    pair_own = (me * PH + r - PH).astype(F32)
    source = (j % S) < PH
    chosen_t = source & (label_row == pair_own)
    logits_t = mat - jnp.where(chosen_t, SCORE * MARGIN, 0.0)
    from_target = jnp.where(source, jnp.exp(jnp.where(source, logits_t - lse_row, 0.0)), 0.0)
    from_target = from_target - jnp.where(chosen_t, 1.0, 0.0)
    glog = jnp.where(r < PH, from_source, from_target).astype(BF)
    gu = SCORE * dot(glog, units)
    squashed = jnp.tanh(rp_ref[...])
    rs = lax.rsqrt(jnp.sum(squashed * squashed, -1, keepdims=True) + EPS_UNIT)
    gt = rs * (gu - squashed * (rs * rs * jnp.sum(gu * squashed, -1, keepdims=True)))
    gr = (gt * (1.0 - squashed * squashed)).astype(BF)
    copies[0].wait()
    gx2 = dot(gr, wp[...], NT)

    n1, n2, r1, r2 = small_ref[0], small_ref[1], small_ref[2], small_ref[3]
    gz2 = norm_back(gx2, n2, r2, gain_ref[1, 1:2, :])
    gy = gz2.astype(BF)
    copies[1].wait()
    gf = (dot(gy, w2[...], NT) * dg_ref[...]).astype(BF)
    copies[2].wait()
    gh1 = gz2 + dot(gf, w1[...], NT)
    gz1 = norm_back(gh1, n1, r1, gain_ref[1, 0:1, :])
    go = gz1.astype(BF)
    copies[3].wait()
    gc = dot(go, wo[...], NT).astype(BF).astype(F32)
    gcm = head_rows(gc).astype(BF)
    for i in (4, 5, 6):
        copies[i].wait()
    gcw = dot(gcm, wqkv[2], NT).astype(BF)
    xall = xb_ref[...]
    prob = a1_ref[...].astype(F32)
    ga = dot(gcw, xall, NT)
    gs = (prob * (ga - jnp.sum(ga * prob, 1, keepdims=True))).astype(BF)
    mm = dot(gs, xall).astype(BF)
    gpq = head_fold(dot(mm, wqkv[1])).astype(BF).astype(F32) * SCALE
    gpqb = gpq.astype(BF)
    back = dot(jnp.concatenate([gs, a1_ref[...]], 0), jnp.concatenate([qw_ref[...], gcw], 0), TN)
    gx[...] = back
    first = gz1 + dot(gpqb, wqkv[0], NT)
    for s in range(S):
        gx[64 * s:64 * s + 1, :] += first[s:s + 1, :]

    nx = n2_ref[...].astype(F32)
    gxv = gx[...]
    gzx = norm_back(gxv, nx, r2_ref[:, 0:1], gain_ref[0, 1:2, :])
    gyx = gzx.astype(BF)
    gz_out[...] = gzx
    gy_out[...] = gyx

    vec_out[0:1, :] = total_rows(gpqb.astype(F32))
    vec_out[1:2, :] = total_rows(gc)
    vec_out[2:3, :] = total_rows(go.astype(F32))
    vec_out[3:4, :] = total_rows(gh1)
    vec_out[4:5, :] = total_rows(gy.astype(F32))
    vec_out[5:6, :] = total_rows(gx2)
    vec_out[6:7, :] = total_rows(gh1 * n1)
    vec_out[7:8, :] = total_rows(gx2 * n2)
    vec_out[8:9, :] = total_rows(gr.astype(F32))
    vec_out[9:10, :] = total_rows(gxv)
    vec_out[10:11, :] = total_rows(gxv * nx)
    vec_out[11:12, :] = total_rows(gyx.astype(F32))
    vec_out[12:16, :] = jnp.zeros((4, D), F32)
    eb_out[...] = total_rows(gf.astype(F32))

    width = D // cut.GX
    cut_up = lambda v: [v[:, i * width:(i + 1) * width] for i in range(v.shape[1] // width)]
    e0, h1b, c0, x0, g1b = (big_ref[:, a:b].astype(F32) for a, b in (
        (0, D), (D, 2 * D), (2 * D, 3 * D), (3 * D, 4 * D), (4 * D, 4 * D + FF)))
    mmf, axf = mm.astype(F32), ax_ref[...].astype(F32)
    for g in range(cut.GX):
        lanes = slice(g * width, (g + 1) * width)
        blocks = [v[h * S:(h + 1) * S, lanes] for v in (mmf, axf) for h in range(H)]
        blocks += [x0[:, lanes], c0[:, lanes], e0[:, lanes], h1b[:, lanes]]
        blocks += cut_up(g1b[:, g * 4 * width:(g + 1) * 4 * width])
        dst = g if cut.C == 1 else g ^ gxi
        for i, block in enumerate(blocks):
            left_s[dst, i] = block.astype(BF)
    q0 = head_fold(qm_ref[...].astype(F32))
    right = cut_up(gpq) + cut_up(q0) + cut_up(gc) + cut_up(go.astype(F32))
    grf, gyf, gff = gr.astype(F32), gy.astype(F32), gf.astype(F32)
    dn, df = D // cut.GY, FF // cut.GY
    for g in range(cut.GY):
        mix = jnp.concatenate([grf[:, g * dn:(g + 1) * dn], gyf[:, g * dn:(g + 1) * dn],
                               gff[:, g * df:(g + 1) * df]], 1)
        right += cut_up(mix)
    right = [block.astype(BF) for block in right]
    L = LEFT
    for out, base in (((stay_out, 0), (go_out, 2)) if cut.C == 2 else ((stay_out, 0),)):
        for r in range(cut.C):
            out[r * L:(r + 1) * L] = left_s[base + r]
        for i, block in enumerate(right):
            out[cut.C * L + i] = block


LEFT = 2 * H + 8


def params(mb):
    return pltpu.CompilerParams(vmem_limit_bytes=mb << 20)


def cost(weight=0.0):
    return pl.CostEstimate(flops=int(weight * UNIT), bytes_accessed=1, transcendentals=0)


UNIT = 10 ** 10
LONG = 1000.0


def call(kernel, name, mb, outs, ins, hbm=(), smem=(), scratch=(), after=(), weight=0.0):
    hbm = [in_hbm(t) for t in hbm]
    return pl.pallas_call(
        functools.partial(kernel), out_shape=list(outs), name=name,
        in_specs=[SM] * len(smem) + [VM] * len(ins) + [HBM] * (len(hbm) + len(after)), out_specs=[VM] * len(outs),
        scratch_shapes=list(scratch), compiler_params=params(mb), cost_estimate=cost(weight),
    )(*smem, *ins, *hbm, *after)


def in_hbm(t):
    return pltpu.with_memory_space_constraint(t, pltpu.HBM)


def sds(shape, dtype):
    return jax.ShapeDtypeStruct(shape, dtype)


def top(cut, gathered, own, rp, small, big, dg, a1, ax, qm, qw, xb, n2, r2, gains, wqkv, wo, w1, w2, wp):
    S = own.shape[0]
    T, D = xb.shape
    FF = w1.shape[2]
    width = D // cut.GX
    V = pltpu.VMEM
    count = cut.C * LEFT + 4 * cut.GX + (2 * D + FF) // width
    outs = [sds((S, 128), F32), sds((8, 128), F32), sds((T, D), BF), sds((T, D), F32), sds((16, D), F32),
            sds((1, FF), F32)] + [sds((count, S, width), BF)] * cut.C
    local = (own, rp, small, big, dg, a1, ax, qm, qw, xb, n2, r2)
    bufs = [V(t.shape, t.dtype) for t in local]
    return pl.pallas_call(
        functools.partial(top_kernel, cut, S // 2, len(gathered)), out_shape=outs,
        in_specs=[VM] + [HBM] * 17 + [VM] * len(gathered), out_specs=[VM] * len(outs),
        scratch_shapes=[V((3, D, D), BF), V((D, D), BF), V((D, FF), BF), V((FF, D), BF), V((D, D), BF),
                        V((T, D), F32), V((cut.GX, LEFT, S, width), BF), *bufs, pltpu.SemaphoreType.DMA((19,))],
        name="rank_and_top_back", compiler_params=params(32 if cut.C == 2 else 55), cost_estimate=cost(),
    )(gains, *(in_hbm(t) for t in (*local, wqkv, wo, w1, w2, wp)), *gathered)


def peers_of(cut, refs):
    L = LEFT
    if cut.C == 1:
        return [(refs[0], 0, L)]
    stay, got_y, got_c = refs
    n = stay.shape[0] - 2 * L
    return [(stay, 0, 2 * L), (got_y, 0, 2 * L), (got_c, 0, 2 * L), (got_c, L, 2 * L + n)]


def top_weights_kernel(cut, S, count, *refs):
    peers = peers_of(cut, refs[:count])
    outs = refs[count:]
    sides = cut.X
    chunks, rows, part = outs[:sides], outs[sides:2 * sides], outs[-1]
    xbit = place()[3] if sides == 2 else 0
    width = refs[0].shape[2]
    D = width * cut.GX
    G = cut.GX
    get = lambda ref, i: ref[i].astype(F32)
    lane_cat = lambda ref, i, m: jnp.concatenate([get(ref, i + k) for k in range(m)], 1) if m > 1 else get(ref, i)
    rights = [[lane_cat(ref, ro + k * G, G) for k in range(4)] for ref, lo, ro in peers]
    low = lax.broadcasted_iota(jnp.int32, (S, 128), 1) < HD
    stack = lambda pieces: jnp.concatenate(pieces, 0).astype(BF)
    cols = [dot(stack([get(ref, lo + 2 * H) for ref, lo, ro in peers]), stack([r[0] for r in rights]), TN)]
    for kind in range(2):
        for j in range(D // 128):
            lhs, rhs = [], []
            for (ref, lo, ro), r in zip(peers, rights):
                lhs += [get(ref, lo + kind * H + 2 * j), get(ref, lo + kind * H + 2 * j + 1)]
                blk = r[kind + 1][:, 128 * j:128 * j + 128]
                rhs += [jnp.where(low, blk, 0.0), jnp.where(low, 0.0, blk)]
            cols.append(dot(stack(lhs), stack(rhs), TN))
    qkv = jnp.concatenate(cols, 1)
    out = dot(stack([get(ref, lo + 2 * H + 1) for ref, lo, ro in peers]), stack([r[3] for r in rights]), TN)
    wa, wb = 3 * D // cut.GY, D // cut.GY
    halves = []
    for x in range(sides):
        blocks = []
        for z in range(cut.Z):
            b = z * sides + x
            blocks.append(jnp.concatenate(
                [qkv[:, b * wa:(b + 1) * wa], out[:, b * wb:(b + 1) * wb]], 1).astype(BF))
        halves.append(blocks)
    for z in range(cut.Z):
        for x in range(sides):
            part[x, z] = halves[x][z]
    for r, dst in enumerate(chunks):
        dst[...] = part[xbit ^ r] if sides == 2 else part[0]
    m = (2 * D + 4 * D) // cut.GY // width
    if sides == 1:
        ref, lo, ro = peers[0]
        rows[0][0:6] = ref[lo + 2 * H + 2:lo + LEFT]
        rows[0][6:6 + m] = ref[ro + 4 * G:ro + 4 * G + m]
        return
    for r, dst in enumerate(rows):
        x = xbit ^ r
        for p, (ref, lo, ro) in enumerate(peers):
            at, lanes = p // 2, slice(p % 2 * width, (p % 2 + 1) * width)
            dst[at * 6:at * 6 + 6, :, lanes] = ref[lo + 2 * H + 2:lo + LEFT]
            for z in range(cut.Z):
                to = 12 + (z * 2 + at) * m
                dst[to:to + m, :, lanes] = ref[pl.ds(ro + 4 * G + (z * sides + x) * m, m)]


def top_weights(cut, arrays, after=()):
    S, width = arrays[0].shape[1:]
    D = width * cut.GX
    peers = 4 if cut.C == 2 else 1
    m = 6 * D // cut.GY // width
    chunk = sds((cut.Z, width, 4 * D // cut.GY), BF)
    rows = sds(((6 + cut.Z * m) * max(peers // 2, 1), S, width * min(peers, 2)), BF)
    kernel = lambda *refs: top_weights_kernel(
        cut, S, len(arrays), *refs[:len(arrays)], *refs[len(arrays) + len(after):])
    return call(kernel, "top_weights", 20, [chunk] * cut.X + [rows] * cut.X, arrays, after=after,
                scratch=[pltpu.VMEM((cut.X,) + chunk.shape, BF)])


def pack_kernel(stay, got, out):
    L = LEFT
    n = stay.shape[0] - 2 * L
    for src, lo, dst, m in ((stay, L, 0, L), (got, L, L, L), (stay, 2 * L, 2 * L, n), (got, 2 * L, 2 * L + n, n)):
        out[dst:dst + m] = src[lo:lo + m]


def pack(stay, got):
    n = 2 * (stay.shape[0] - LEFT)
    return call(pack_kernel, "pack", 8, [sds((n,) + stay.shape[1:], BF)], (stay, got))[0]


def rows_by_z_kernel(keep, got, *outs):
    z = place()[4]
    for d, dst in enumerate(outs):
        for s, src in enumerate((keep, got)):
            dst[s * 12:(s + 1) * 12] = src[0:12]
            dst[24 + s * 6:24 + (s + 1) * 6] = src[pl.ds(12 + (z ^ d) * 6, 6)]


def rows_by_z(keep, got, after=()):
    shape = sds((36,) + keep.shape[1:], BF)
    kernel = lambda a, b, *refs: rows_by_z_kernel(a, b, *refs[len(after):])
    return call(kernel, "rows_by_z", 16, [shape] * 4, (keep, got), after=after)


def row_weights_kernel(cut, count, *refs):
    ins, (pool_out, expand_out, reduce_out) = refs[:count], refs[count:]
    width = ins[0].shape[2] // cut.C
    D = width * cut.GX
    lefts, rights = [], []
    if cut.C == 2:
        for ref in ins:
            for s in range(2):
                for p in range(4):
                    lanes = slice(p % 2 * width, (p % 2 + 1) * width)
                    left, right = s * 12 + p // 2 * 6, 24 + s * 6 + p // 2 * 3
                    lefts.append([ref[left + i, :, lanes].astype(F32) for i in range(6)])
                    rights.append([ref[right + i, :, lanes].astype(F32) for i in range(3)])
    else:
        ref = ins[0]
        lefts.append([ref[i].astype(F32) for i in range(6)])
        rights.append([ref[6 + i].astype(F32) for i in range(ref.shape[0] - 6)])
    left = lambda i: jnp.concatenate([g[i] for g in lefts], 0).astype(BF)
    right = jnp.concatenate([jnp.concatenate(g, 1) for g in rights], 0).astype(BF)
    dn = D // cut.GY
    pool_out[...] = dot(left(0), right[:, 0:dn], TN)
    expand_out[...] = dot(left(1), right[:, 2 * dn:], TN)
    gy = right[:, dn:2 * dn]
    reduce_out[...] = dot(gy, jnp.concatenate([left(i) for i in range(2, 6)], 1), TN)


def row_weights(cut, arrays, after=()):
    width = arrays[0].shape[2] // cut.C
    D = width * cut.GX
    dn = D // cut.GY
    outs = [sds((width, dn), F32), sds((width, 4 * dn), F32), sds((dn, 4 * width), F32)]
    kernel = lambda *refs: row_weights_kernel(cut, len(arrays), *refs[:len(arrays)], *refs[len(arrays) + len(after):])
    return call(kernel, "row_weights", 32, outs, arrays, after=after)


def widen_kernel(gy_ref, dg_ref, w2_hbm, gf_out, eb_out, w2, sem):
    T, D = gy_ref.shape
    FF = dg_ref.shape[1]
    loads = start_all([(w2_hbm.at[0, pl.ds(i * D, D), :], w2.at[pl.ds(i * D, D), :]) for i in range(FF // D)], sem)
    for i in range(FF // D):
        loads[i].wait()
        cols = slice(i * D, (i + 1) * D)
        back = (dot(gy_ref[...], w2[cols, :], NT) * dg_ref[:, cols].astype(F32)).astype(BF)
        gf_out[:, cols] = back
        eb_out[0:1, cols] = total_rows(back.astype(F32))


def widen_back(gy, dg, w2):
    T, D = gy.shape
    FF = dg.shape[1]
    return call(widen_kernel, "widening_back", 24, [sds((T, FF), BF), sds((1, FF), F32)], (gy, dg), (w2,),
                scratch=[pltpu.VMEM((FF, D), BF), pltpu.SemaphoreType.DMA((FF // D,))], weight=LONG)


def narrow_weight_kernel(cut, *refs):
    C = cut.C
    gys, acts, outs, parts = refs[:C], refs[C:2 * C], refs[2 * C:2 * C + C * C], refs[2 * C + C * C:]
    T, D = gys[0].shape
    nw = D // cut.GY
    width = D // C
    left = [g[...].T for g in gys]
    for b in range(4):
        res = dot(left[0], acts[0][b])
        for c in range(1, C):
            res = res + dot(left[c], acts[c][b])
        res = res.astype(BF)
        y, lane = (b // 2, (b % 2) * width) if C == 2 else (0, b * width)
        for x in range(cut.X):
            for z in range(cut.Z):
                g = z * cut.X + x
                value = res[g * nw:(g + 1) * nw, :]
                if C == 1:
                    put(cut, parts, y, x, z, value, lanes=slice(lane, lane + width))
                else:
                    put(cut, parts, y, x, z, value, slice(b % 2 * nw, (b % 2 + 1) * nw))
    emit(cut, parts, outs)


def narrow_weight(cut, gys, acts, after=()):
    T, D = gys[0].shape
    scratch, outs = pieces(cut, cut.C * D // cut.GY, 4 * D // cut.GX // cut.C)
    n = 2 * cut.C
    kernel = lambda *refs: narrow_weight_kernel(cut, *refs[:n], *refs[n + len(after):])
    return call(kernel, "narrowing_weight", 24, outs, (*gys, *acts), after=after, scratch=scratch, weight=LONG)


def widen_weight_kernel(cut, *refs):
    C = cut.C
    acts, gfs, outs, parts = refs[:C], refs[C:2 * C], refs[2 * C:2 * C + C * C], refs[2 * C + C * C:]
    width = acts[0].shape[2]
    D = width * C
    FF = gfs[0].shape[1]
    lw, kr = FF // cut.GY, D // cut.GX
    left = [a[4].T for a in acts]
    W = D
    for i in range(FF // W):
        res = dot(left[0], gfs[0][:, i * W:(i + 1) * W])
        for c in range(1, C):
            res = res + dot(left[c], gfs[c][:, i * W:(i + 1) * W])
        res = res.astype(BF)
        if C == 1:
            put(cut, parts, 0, 0, 0, res, lanes=slice(i * W, (i + 1) * W))
            continue
        for h in range(W // lw):
            g = i * W // lw + h
            for y in range(cut.Y):
                put(cut, parts, y, g % cut.X, g // cut.X, res[y * kr:(y + 1) * kr, h * lw:(h + 1) * lw])
    emit(cut, parts, outs)


def widen_weight_back(cut, acts, gfs, after=()):
    D = acts[0].shape[2] * cut.C
    FF = gfs[0].shape[1]
    scratch, outs = pieces(cut, D // cut.GX, FF // cut.GY)
    n = 2 * cut.C
    kernel = lambda *refs: widen_weight_kernel(cut, *refs[:n], *refs[n + len(after):])
    return call(kernel, "widening_weight", 24, outs, (*acts, *gfs), after=after, scratch=scratch, weight=0.6)


def first_norm_kernel(extra, gz2_ref, n_ref, r_ref, gain_ref, gf_ref, w1_hbm, wo_hbm, *rest):
    gz_out, go_out, gc_out, vec_out, w1, wo, sem = rest[extra:]
    T, D = gz2_ref.shape
    FF = gf_ref.shape[1]
    cols = [pl.ds(i * D, D) for i in range(FF // D)]
    copies = start_all([(w1_hbm.at[0, :, c], w1.at[:, c]) for c in cols] + [(wo_hbm.at[0], wo)], sem)
    gh = gz2_ref[...]
    for i in range(FF // D):
        copies[i].wait()
        gh = gh + dot(gf_ref[:, i * D:(i + 1) * D], w1[:, i * D:(i + 1) * D], NT)
    n = n_ref[...].astype(F32)
    gz = norm_back(gh, n, r_ref[:, 0:1], gain_ref[0, 0:1, :])
    gz_out[...] = gz
    go = gz.astype(BF)
    go_out[...] = go
    vec_out[0:1, :] = total_rows(gh)
    vec_out[1:2, :] = total_rows(gh * n)
    vec_out[2:3, :] = total_rows(go.astype(F32))
    vec_out[3:8, :] = jnp.zeros((5, D), F32)
    copies[FF // D].wait()
    gc_out[...] = dot(go, wo[...], NT).astype(BF)


def first_norm_back(gz2, n1, r1, gains, gf, w1, wo, after=()):
    T, D = gz2.shape
    FF = gf.shape[1]
    V = pltpu.VMEM
    return call(functools.partial(first_norm_kernel, len(after)), "first_norm_back", 30,
                [sds((T, D), F32), sds((T, D), BF), sds((T, D), BF), sds((8, D), F32)],
                (gz2, n1, r1, gains, gf), (w1, wo),
                scratch=[V((D, FF), BF), V((D, D), BF), pltpu.SemaphoreType.DMA((FF // D + 1,))], after=after, weight=0.6)


def attend_kernel(extra, gc, go, q, k, v, a, vec1, vec2, eb0, eb1, *rest):
    gp, = rest[extra:]
    T, D = q.shape
    S = T // 64
    lane = lax.broadcasted_iota(jnp.int32, (128, 128), 1)
    low = lane < HD
    NB = D // 128

    def heads(p, _):
        rows = pl.ds(pl.multiple_of(p * 128, 128), 128)
        for j in range(NB):
            lanes = slice(128 * j, 128 * j + 128)
            gcj = gc[rows, lanes]
            gcm = jnp.concatenate([jnp.where(low, gcj, 0), jnp.where(low, 0, gcj)], 0)
            qj = q[rows, lanes]
            qm = jnp.concatenate([jnp.where(low, qj, 0), jnp.where(low, 0, qj)], 0)
            pb = a[p * NB + j]
            prob = pb.astype(F32)
            gp[rows, 2 * D + 128 * j:2 * D + 128 * j + 128] = dot(pb, gcm).astype(BF)
            ga = dot(v[rows, lanes], gcm, NT)
            gs = (prob * (ga - jnp.sum(ga * prob, 0, keepdims=True))).astype(BF)
            gp[rows, D + 128 * j:D + 128 * j + 128] = dot(gs, qm).astype(BF)
            gq = dot(gs, k[rows, lanes], TN)
            gq = jnp.where(low, gq[:128], gq[128:]).astype(BF)
            gp[rows, lanes] = (gq.astype(F32) * SCALE).astype(BF)
        return 0

    lax.fori_loop(0, S // 2, heads, 0)
    gp[0:T, 3 * D:] = go[...]
    one = lambda ref, i: ref[i:i + 1, :]
    vecs = [total_rows(gp[0:T, 0:D].astype(F32)), total_rows(gp[0:T, 2 * D:3 * D].astype(F32)),
            one(vec2, 2), one(vec2, 0), one(vec1, 11), one(vec1, 9)]
    vecs += [one(vec1, i) for i in range(6)] + [one(vec2, 1), one(vec1, 10), one(vec1, 6), one(vec1, 7), one(vec1, 8)]
    vecs += [jnp.zeros((1, D), F32)] * (32 - len(vecs))
    block = jnp.concatenate([jnp.concatenate(vecs[8 * i:8 * i + 8], 0) for i in range(4)], 1)
    wide = jnp.concatenate([eb0[...], eb1[...], jnp.zeros((6, 4 * D), F32)], 0)
    gp[T:T + 16, :] = jnp.concatenate([block, wide], 0).astype(BF)


def attend_back(gc, go, q, k, v, a, vectors, after=()):
    T, D = gc.shape
    return call(functools.partial(attend_kernel, len(after)), "attention_back", 24, [sds((T + 16, 4 * D), BF)],
                (gc, go, q, k, v, a, *vectors), after=after, weight=0.6)[0]


def attend_weight_kernel(cut, *refs):
    C = cut.C
    acts, gps, refs = refs[:C], refs[C:2 * C], refs[2 * C:]
    m = 10 if C == 2 else 1
    outs, parts, blocks = refs[:m], refs[m:-1], refs[-1]
    width = acts[0].shape[2]
    D = width * C
    T = gps[0].shape[0] - 16
    ct = [a[5].T for a in acts]
    xt = [a[6].T for a in acts]
    wa, wb = 3 * D // cut.GY, D // cut.GY
    main = wa // 128 * 128
    tail = wa - main
    kr = D // cut.GX

    def place_rows(res, x, z, lanes):
        res = res.astype(BF)
        for y in range(cut.Y):
            put(cut, parts, y, x, z, res[y * kr:(y + 1) * kr, :], slice(0, kr), lanes)

    both = lambda f: f(0) + f(1) if C == 2 else f(0)
    if cut.GY == 1:
        place_rows(dot(xt[0], gps[0][0:T, 0:3 * D]), 0, 0, slice(0, 3 * D))
        place_rows(dot(ct[0], gps[0][0:T, 3 * D:]), 0, 0, slice(3 * D, None))
        emit(cut, parts, outs)
        return
    for x in range(cut.X):
        for z in range(cut.Z):
            a0 = (z * cut.X + x) * wa
            place_rows(both(lambda c: dot(xt[c], gps[c][0:T, a0:a0 + main])), x, z, slice(0, main))
    order = [(x, z) for x in range(cut.X) for z in range(cut.Z)]
    for i in range(0, len(order), 2):
        def tails(c):
            ra, rb = [], []
            for x, z in order[i:i + 2]:
                g = z * cut.X + x
                a0, o0 = g * wa, 3 * D + g * wb
                ra += [gps[c][0:T, a0 + main:a0 + wa], jnp.zeros((T, 128 - tail), BF)]
                rb += [jnp.zeros((T, tail), BF), gps[c][0:T, o0:o0 + wb]]
            return dot(xt[c], jnp.concatenate(ra, 1)) + dot(ct[c], jnp.concatenate(rb, 1))
        res = both(tails)
        for m, (x, z) in enumerate(order[i:i + 2]):
            place_rows(res[:, 128 * m:128 * m + 128], x, z, slice(main, wa + wb))
    core = place()[1]
    vec = both(lambda c: gps[c][T:T + 16, :].astype(F32))
    n = 4 * 8
    dv, dw = D // n, 4 * D // n
    for d in range(n):
        pieces = [vec[0:8, k * D + d * dv:k * D + (d + 1) * dv] for k in range(3)]
        pieces += [jnp.zeros((8, 128 - 3 * dv), F32), vec[8:16, d * dw:(d + 1) * dw],
                   jnp.zeros((8, wa + wb - 128 - dw), F32)]
        blocks[d] = jnp.concatenate([jnp.concatenate(pieces, 1), jnp.zeros((8, wa + wb), F32)], 0).astype(BF)
    for y in range(cut.Y):
        for x in range(cut.X):
            for z in range(cut.Z):
                put(cut, parts, y, x, z, blocks[(2 * y + core) * 8 + z * cut.X + x], slice(kr, kr + 16))
    emit(cut, parts, outs)


def attend_weight(cut, acts, gps, after=()):
    T, D4 = gps[0].shape
    D = D4 // 4
    kr = D // cut.GX + (16 if cut.C == 2 else 0)
    scratch, outs = pieces(cut, kr, D4 // cut.GY, True)
    n = 2 * cut.C
    kernel = lambda *refs: attend_weight_kernel(cut, *refs[:n], *refs[n + len(after):])
    return call(kernel, "attention_weight", 30, outs, (*acts, *gps), after=after, weight=LONG,
                scratch=scratch + [pltpu.VMEM((32, 16, D4 // cut.GY), BF)])


def input_kernel(pairs, extra, len_ref, tot_ref, gz_ref, gp_ref, w_hbm, *rest):
    gx_out, sc_out, w, sem = rest[extra:]
    T, D = gz_ref.shape
    PH = len_ref.shape[1]
    copies = start_all([(w_hbm.at[0, :, pl.ds(i * D, D)], w.at[i]) for i in range(3)], sem)
    grad = gz_ref[...]
    for i in range(3):
        copies[i].wait()
        grad = grad + dot(gp_ref[0:T, i * D:(i + 1) * D], w[i], NT)
    inverse = 1.0 / tot_ref[0:1, 0:1]
    for s in range(T // 64):
        rows = slice(64 * s, 64 * s + 64)
        factor = (2.0 * pairs) * len_ref[s // PH, s % PH].astype(F32) * inverse
        gx_out[rows, :] = grad[rows, :]
        sc_out[rows, :] = grad[rows, :] * factor


def input_back(pairs, lengths, tot, gz1, gp, wqkv, after=()):
    T, D = gz1.shape
    return call(functools.partial(input_kernel, pairs, len(after)), "input_back", 24, [sds((T, D), F32)] * 2,
                (tot, gz1, gp), (wqkv,), (lengths,),
                scratch=[pltpu.VMEM((3, D, D), BF), pltpu.SemaphoreType.DMA((3,))], after=after, weight=LONG)


def plus(a, b):
    return (a.astype(F32) + b.astype(F32)).astype(BF)


def flip(values, axis, bits):
    return lax.ppermute(values, axis, [(i, i ^ bits) for i in range(lax.axis_size(axis))])


def fold_kernel(count, extra, *refs):
    ins, outs = refs[:count], refs[count + extra:]
    ybit, xbit = place()[2:4]
    n = count // 2
    for bit, (keep, *gots), mine, other in ((xbit, ins[:n], *outs[:2]), (ybit, ins[n:], *outs[2:])):
        if n == 2:
            other[...] = plus(keep[1 - bit], gots[0][1 - bit])
            mine[...] = plus(keep[bit], gots[0][bit])
            continue
        for z in range(2):
            first, second = plus(keep[0, z], gots[z][...]), plus(keep[1, z], gots[2 + z][...])
            other[z] = jnp.where(bit == 0, second, first)
            mine[z] = jnp.where(bit == 0, first, second)


def spread_kernel(counts, extra, *refs):
    ins, (keep_out, send_out) = refs[:sum(counts)], refs[sum(counts) + extra:]
    low = lax.rem(place()[4], 2)
    for i, count in enumerate(counts):
        mine, ins = ins[:count], ins[count:]
        n = mine[0].shape[0]
        for dst, parity in ((send_out, 1 - low), (keep_out, low)):
            for high in range(2):
                keep, got = mine[high * 2:high * 2 + 2] if n == 2 else mine
                z = parity if n == 2 else high * 2 + parity
                dst[i, high] = plus(keep[z], got[z])


def spread(chunks, after=()):
    shape = sds((len(chunks), 2) + chunks[0][0].shape[1:], BF)
    keep, send = call(
        functools.partial(spread_kernel, [len(c) for c in chunks], len(after)), "spread", 16, [shape] * 2,
        sum(chunks, []), after=after)
    return keep, flip(send, "gy", 2), send


def settle_kernel(extra, keep, got, *rest):
    own_out, send_out = rest[extra:]
    high = lax.div(place()[4], 2)
    send_out[...] = plus(keep[:, 1 - high], got[:, 1 - high])
    own_out[...] = keep[:, high].astype(F32) + got[:, high].astype(F32)


def settle(keep, got, after=()):
    shape = (keep.shape[0],) + keep.shape[2:]
    own, send = call(functools.partial(settle_kernel, len(after)), "settle", 16, [sds(shape, F32), sds(shape, BF)],
                     (keep, got), after=after)
    return own, flip(send, "gy", 4), send


X_SIDE, Y_SIDE = 3, 2


def cross(values, side):
    return flip(values, "gy", 1) if side == X_SIDE else flip(values, "gx", 2)


class Share:
    def __init__(self, chunk):
        n = len(chunk) // 2
        self.keep = [chunk[0], chunk[n]]
        self.got = [[cross(t, Y_SIDE) for t in chunk[1:n]], [cross(t, X_SIDE) for t in chunk[n + 1:]]]

    def operands(self):
        return [self.keep[0], *self.got[0], self.keep[1], *self.got[1]]

    def fold(self, *after):
        shape = sds(self.keep[0].shape[1:], BF)
        ins = self.operands()
        outs = call(functools.partial(fold_kernel, len(ins), len(after)), "fold", 16, [shape] * 4, ins, after=after)
        self.keep = [outs[0], outs[2]]
        self.got = [[cross(outs[1], X_SIDE)], [cross(outs[3], Y_SIDE)]]
        return outs[1]


def finish_wide_kernel(own, got, r1, e1, reduce_out, expand_out):
    both = own[...] + got[...].astype(F32)
    n = both.shape[1] // 2
    reduce_out[0] = jnp.concatenate([both[0, 0:n], both[0, n:]], 1)
    reduce_out[1] = r1[...]
    expand_out[0] = both[1]
    expand_out[1] = e1[...]


def finish_attend_kernel(wa, own4, got4, own1, got1, *outs):
    attend_out, output_out, bias_out, gains_out, wb_out, pb_out = outs
    a, b = own4[0] + got4[0].astype(F32), own1[0] + got1[0].astype(F32)
    kr = b.shape[0]
    for layer, v in enumerate((a[0:kr], b)):
        attend_out[layer] = v[:, 0:wa]
        output_out[layer] = v[:, wa:]
    vec = a[kr:kr + 8, :]
    dv = bias_out.shape[2]
    one = lambda i: vec[i % 8:i % 8 + 1, i // 8 * dv:i // 8 * dv + dv]
    for layer in range(2):
        for i in range(6):
            bias_out[i, layer:layer + 1, :] = one(6 * layer + i)
        for i in range(2):
            gains_out[layer, i:i + 1, :] = one(12 + 2 * layer + i)
    wb_out[...] = vec[0:2, 128:128 + 4 * dv]
    pb_out[...] = one(16)


def scatter(values, row_axis, col_axis):
    part = lax.psum_scatter(values.astype(BF), row_axis, scatter_dimension=0, tiled=True)
    return lax.psum_scatter(part, col_axis, scatter_dimension=1, tiled=True).astype(F32)


def shards(mesh, inputs, lengths, labels, wqkv, wo, w1, w2, bias, gains, wb, wp, pb):
    GX, GY = mesh.shape["gx"], mesh.shape["gy"]
    n = GX * GY
    near = (GX, GY) == (4, 8)
    cut = Cut(2, 2, 2, 4) if near else Cut(1, 1, 1, 1)
    PH = labels.shape[0]
    S = 2 * PH
    L, D = inputs.shape[2], inputs.shape[3]
    T = S * L
    FF = w1.shape[2]
    twin = lambda v: [v, flip(v, "gx", 1)] if near else [v]
    x = inputs.reshape(T, D)
    (q, k, v, a, n1, r1, dg, n2, r2, xb, small, big, a1, ax, qm, qw, dg1, rp, own, *acts) = forward(
        cut, x, lengths, labels, wqkv, wo, w1, w2, wp, bias.transpose(1, 0, 2), gains, wb, pb)
    if near:
        line = jnp.concatenate([own] + [flip(own, "gy", 2 * d) for d in (1, 2, 3)], 0)
        corner = lax.ppermute(line, ("gx", "gy"), [(i, i ^ 17) for i in range(n)])
        plane = jnp.concatenate([line, flip(line, "gy", 1), flip(line, "gx", 2), corner], 0)
        gathered = [plane, flip(plane, "gx", 1)]
        acts = [acts[0], flip(acts[1], "gx", 1)]
    else:
        gathered = [lax.all_gather(own, ("gx", "gy"), axis=0, tiled=True)]
    loss, tot, gy, gz2, vec1, eb1, *rows = top(
        cut, gathered, own, rp, small, big, dg1, a1, ax, qm, qw, xb, n2, r2, gains, wqkv, wo, w1, w2, wp)
    if near:
        stay, go_y = rows
        got_y = flip(go_y, "gx", 2)
    gys = twin(gy)
    gf, eb0 = widen_back(gy, dg, w2)
    if near:
        rows = [stay, got_y, flip(pack(stay, got_y), "gx", 1)]
    gfs = twin(gf)
    ch2 = narrow_weight(cut, gys, acts, (gf,) + tuple(rows[1:2]))
    ch1 = top_weights(cut, rows, (ch2[0],))
    if near:
        s2 = Share(ch2)
        got1 = cross(ch1[1], X_SIDE)
        keep_x, send_x = ch1[2:]
        got_x = cross(send_x, X_SIDE)
    ch3 = widen_weight_back(cut, acts, gfs, (ch1[0],))
    gz1, go, gc, vec2 = first_norm_back(gz2, n1, r1, gains, gf, w1, wo, (ch3[0],))
    after = (go,)
    if near:
        s3 = Share(ch3)
        after = (s2.fold(go),)
    gp = attend_back(gc, go, q, k, v, a, (vec1, vec2, eb0, eb1), after)
    gps = twin(gp)
    after = ()
    if near:
        rows_z = rows_by_z(keep_x, got_x, (s3.fold(gp),))
        after = (rows_z[0],)
        rows_z = [rows_z[0]] + [flip(rows_z[d], "gy", 2 * d) for d in (1, 2, 3)]
    gx0, sc0 = input_back(n * PH, lengths, tot, gz1, gp, wqkv, after)
    after = (gx0,)
    if near:
        keep23, got23, t = spread([s2.operands(), s3.operands()], (gx0,))
        after = (t,)
    ch4 = attend_weight(cut, acts, gps, after)
    shape = (2, PH, L, D)
    wa = 3 * D // GY
    if near:
        s4 = Share(ch4)
        kr, dn, dv = D // GX, D // GY, D // n
        keep1, got1, t = spread([[ch1[0], got1]], (ch4[0],))
        d_pool, d_expand1, d_reduce1 = row_weights(cut, rows_z, (t,))
        own23, got23, t = settle(keep23, got23, (d_reduce1,))
        t = s4.fold(t)
        own1, got1, t = settle(keep1, got1, (t,))
        keep4, got4, t = spread([s4.operands()], (t,))
        d_reduce, d_expand = call(
            finish_wide_kernel, "finish_wide", 16, [sds((2, dn, FF // GX), F32), sds((2, kr, FF // GY), F32)],
            (own23, got23, d_reduce1, d_expand1))
        own4, got4, _ = settle(keep4, got4, (d_reduce,))
        d_reduce = d_reduce.transpose(0, 2, 1)
        d_attend, d_output, d_bias, d_gains, d_wb, d_pb = call(
            functools.partial(finish_attend_kernel, wa), "finish_attend", 16,
            [sds((2, kr, wa), F32), sds((2, kr, dn), F32), sds((6, 2, dv), F32), sds((2, 2, dv), F32),
             sds((2, FF // n), F32), sds((1, dv), F32)], (own4, got4, own1, got1))
        d_bias, d_pb = d_bias.transpose(1, 0, 2), d_pb.reshape(dv)
    else:
        f1, f2, f3, f4 = (t[0].reshape(t[0].shape[-2:]) for t in (ch1, ch2, ch3, ch4))
        pool, expand1, reduce1 = row_weights(cut, ch1[1:])
        d_attend = jnp.stack([scatter(t[:, :3 * D], "gx", "gy") for t in (f4, f1)])
        d_output = jnp.stack([scatter(t[:, 3 * D:], "gx", "gy") for t in (f4, f1)])
        d_expand = jnp.stack([scatter(t, "gx", "gy") for t in (f3, expand1)])
        d_reduce = jnp.stack([scatter(t, "gy", "gx").T for t in (f2, reduce1)])
        d_pool = scatter(pool, "gx", "gy")
        me = lax.axis_index("gx") * GY + lax.axis_index("gy")
        sums = lax.psum(gp[T:].astype(F32), ("gx", "gy"))
        vec = sums[0:8].reshape(8, 4, D).transpose(1, 0, 2).reshape(32, D)
        vec = lax.dynamic_slice_in_dim(vec, me * (D // n), D // n, 1)
        d_bias, d_gains, d_pb = vec[0:12].reshape(2, 6, -1), vec[12:16].reshape(2, 2, -1), vec[16]
        d_wb = lax.dynamic_slice_in_dim(sums[8:10], me * (FF // n), FF // n, 1)
    return (loss[:PH, 0], gx0.reshape(shape), sc0.reshape(shape), d_attend, d_output, d_expand, d_reduce,
            d_bias, d_gains, d_wb, d_pool, d_pb)


def solution(mesh):
    both = ("gx", "gy")
    in_specs = (P(None, both, None, None), P(None, both), P(both)) + (P(),) * 9
    out_specs = (P(both), P(None, both, None, None), P(None, both, None, None), P(None, "gx", "gy"),
                 P(None, "gx", "gy"), P(None, "gx", "gy"), P(None, "gx", "gy"), P(None, None, both),
                 P(None, None, both), P(None, both), P("gx", "gy"), P(both))
    return jax.shard_map(functools.partial(shards, mesh), mesh=mesh, in_specs=in_specs, out_specs=out_specs,
                         check_vma=False)
```

```python
import functools
import jax
import jax.numpy as jnp
from jax import lax
from jax.sharding import PartitionSpec as P
from jax.experimental import pallas as pl
from jax.experimental.pallas import tpu as pltpu

H = 12
HD = 64


class Cut:
    def __init__(self, C, Y, X, Z):
        self.C, self.Y, self.X, self.Z = C, Y, X, Z
        self.GX, self.GY = C * Y, X * Z


BF = jnp.bfloat16
F32 = jnp.float32
ROOT_HALF = 0.7071067811865476
PHI_ZERO = 0.3989422804014327
MASKED = -1e9
EPS_NORM = 1e-12
EPS_UNIT = 1e-6
SCORE = 10.0
MARGIN = 0.3
SCALE = HD ** -0.5

NN = (((1,), (0,)), ((), ()))
NT = (((1,), (1,)), ((), ()))
TN = (((0,), (0,)), ((), ()))


def place():
    gx, gy = lax.axis_index("gx"), lax.axis_index("gy")
    return gx, lax.rem(gx, 2), lax.div(gx, 2), lax.rem(gy, 2), lax.div(gy, 2), gy


def dot(a, b, dims=NN):
    return lax.dot_general(a, b, dims, preferred_element_type=F32)


def normalize(z):
    centered = z - jnp.mean(z, -1, keepdims=True)
    variance = jnp.mean(centered * centered, -1, keepdims=True)
    root = lax.rsqrt(variance + EPS_NORM)
    return centered * root, root


def gelu_pair(f):
    cdf = 0.5 * (1.0 + lax.erf(f * ROOT_HALF))
    return f * cdf, cdf + f * (PHI_ZERO * jnp.exp(-0.5 * f * f))


def head_rows(values):
    lanes = lax.broadcasted_iota(jnp.int32, values.shape, 1) // HD
    return jnp.concatenate([jnp.where(lanes == h, values, 0) for h in range(H)], 0)


def head_fold(values):
    r = values.shape[0] // H
    lanes = lax.broadcasted_iota(jnp.int32, (r, values.shape[1]), 1) // HD
    out = jnp.zeros((r, values.shape[1]), values.dtype)
    for h in range(H):
        out = jnp.where(lanes == h, values[h * r:(h + 1) * r], out)
    return out


def by_core(cut, src, act, slot):
    if cut.C == 1:
        act[0, slot] = src[...]
        return
    width = src.shape[1] // cut.GX
    for ci in range(2):
        act[ci, slot] = jnp.concatenate(
            [src[:, (2 * y + ci) * width:(2 * y + ci + 1) * width] for y in range(cut.Y)], 1)


def fwd_kernel(cut, len_ref, lab_ref, x_hbm, wqkv_hbm, wo_hbm, w1_hbm, w2_hbm, wp_hbm, bias_ref, gain_ref, wb_ref, pb_ref,
               q_out, k_out, v_out, a_out, n1_out, r1_out, dg_out, n2_out, r2_out, xb_out,
               small_out, big_out, a1_out, ax_out, qm_out, qw_out, wide_out, rp_out, pay_out, *rest):
    row_outs, rest = rest[:cut.GX], rest[cut.GX:]
    acts = rest[:cut.C]
    (x, wqkv, wo, w1, w2, wqkv1, wo1, w11, w21, wp,
     q, k, v, a, c, n1, r1, hb, dg, n2, r2, xb, h1, acc, first, act, factors, sem, osem) = rest[cut.C:]
    core = place()[1]
    PH = lab_ref.shape[0]
    tokens = lambda s: len_ref[s // PH, s % PH]
    T, D = x.shape
    S = T // 64
    FF = w1.shape[1]
    loads = [(x_hbm, x)]
    for part in range(3):
        cols = pl.ds(part * D, D)
        loads.append((wqkv_hbm.at[0, :, cols], wqkv.at[part]))
    loads += [(wo_hbm.at[0], wo), (w1_hbm.at[0], w1), (w2_hbm.at[0], w2)]
    for part in range(3):
        cols = pl.ds(part * D, D)
        loads.append((wqkv_hbm.at[1, :, cols], wqkv1.at[part]))
    loads += [(wo_hbm.at[1], wo1), (w1_hbm.at[1], w11), (w2_hbm.at[1], w21), (wp_hbm, wp)]
    copies = [pltpu.make_async_copy(s, d, sem.at[i]) for i, (s, d) in enumerate(loads)]
    for copy in copies[:4]:
        copy.start()
    stores = []

    def store(src, dst):
        copy = pltpu.make_async_copy(src, dst, osem.at[len(stores)])
        copy.start()
        stores.append(copy)

    copies[0].wait()
    TILE = D
    for part, dst in enumerate((q, k, v)):
        copies[1 + part].wait()
        for copy in (copies[4:6], copies[6:7], copies[7:])[part]:
            copy.start()

        def project(j, _, part=part, dst=dst):
            cols = pl.ds(pl.multiple_of(j * TILE, TILE), TILE)
            p = dot(x[...], wqkv[part, :, cols])
            if part == 0:
                p = (p + bias_ref[0:1, 0, cols]) * SCALE
            if part == 2:
                p = p + bias_ref[1:2, 0, cols]
            dst[:, cols] = p.astype(BF)
            return 0

        lax.fori_loop(0, D // TILE, project, 0)
    store(q, q_out)
    store(k, k_out)
    store(v, v_out)

    key = lax.broadcasted_iota(jnp.int32, (128, 256), 0)
    query = lax.broadcasted_iota(jnp.int32, (128, 256), 1)
    lane = lax.broadcasted_iota(jnp.int32, (128, 128), 1)
    low = lane < HD

    def attend(p, _):
        rows = pl.ds(pl.multiple_of(p * 128, 128), 128)
        i = 2 * p
        limit = jnp.where(key < 64, len_ref[i // PH, i % PH], len_ref[i // PH, i % PH + 1] + 64)
        keep = ((key // 64) == ((query // 64) % 2)) & (key < limit)
        for j in range(D // 128):
            lanes = slice(128 * j, 128 * j + 128)
            qq = q[rows, lanes]
            qm = jnp.concatenate([jnp.where(low, qq, 0), jnp.where(low, 0, qq)], 0)
            s = jnp.where(keep, dot(k[rows, lanes], qm, NT), MASKED)
            e = jnp.exp(s - jnp.max(s, 0, keepdims=True))
            prob = (e * (1.0 / jnp.sum(e, 0, keepdims=True))).astype(BF)
            a[p * (D // 128) + j] = prob
            ctx = dot(prob, v[rows, lanes], TN)
            c[rows, lanes] = jnp.where(low, ctx[:128], ctx[128:]).astype(BF)
        return 0

    lax.fori_loop(0, S // 2, attend, 0)
    store(a, a_out)
    by_core(cut, c, act, 5)
    by_core(cut, x, act, 6)

    copies[4].wait()
    ROWS = 256

    def first_norm(i, _):
        rows = pl.ds(pl.multiple_of(i * ROWS, ROWS), ROWS)
        z = x[rows, :].astype(F32) + dot(c[rows, :], wo[...]) + bias_ref[2:3, 0, :]
        n, r = normalize(z)
        n1[rows, :] = n.astype(BF)
        r1[rows, :] = jnp.broadcast_to(r, (ROWS, 128))
        h = n * gain_ref[0, 0:1, :] + bias_ref[3:4, 0, :]
        h1[rows, :] = h
        hb[rows, :] = h.astype(BF)
        acc[rows, :] = h + bias_ref[4:5, 0, :]
        return 0

    lax.fori_loop(0, T // ROWS, first_norm, 0)
    store(n1, n1_out)
    store(r1, r1_out)
    by_core(cut, hb, act, 4)
    copies[5].wait()
    copies[6].wait()

    WIDE = D // cut.C

    def widen(j, _):
        cols = pl.ds(pl.multiple_of(j * D, D), D)
        f = dot(hb[...], w1[:, cols]) + wb_ref[0:1, cols]
        gj, dgj = gelu_pair(f)
        gj = gj.astype(BF)
        dg[:, cols] = dgj.astype(BF)
        for half in range(cut.C):
            act[j % cut.C, j // cut.C * cut.C + half] = gj[:, half * WIDE:(half + 1) * WIDE]
        acc[...] += dot(gj, w2[cols, :])
        return 0

    lax.fori_loop(0, FF // D, widen, 0)
    store(dg, dg_out)
    store(act.at[core], acts[0])
    if cut.C == 2:
        store(act.at[1 - core], acts[1])

    def second_norm(i, _):
        rows = pl.ds(pl.multiple_of(i * ROWS, ROWS), ROWS)
        n, r = normalize(acc[rows, :])
        n2[rows, :] = n.astype(BF)
        r2[rows, :] = jnp.broadcast_to(r, (ROWS, 128))
        h = n * gain_ref[0, 1:2, :] + bias_ref[5:6, 0, :]
        acc[rows, :] = h
        xb[rows, :] = h.astype(BF)
        return 0

    lax.fori_loop(0, T // ROWS, second_norm, 0)
    store(n2, n2_out)
    store(r2, r2_out)
    store(xb, xb_out)

    for s in range(S):
        first[s:s + 1, :] = acc[64 * s:64 * s + 1, :]
    x0 = first[...]
    x0b = x0.astype(BF)
    for i in (7, 8, 9):
        copies[i].wait()
    q0 = ((dot(x0b, wqkv1[0]) + bias_ref[0:1, 1, :]) * SCALE).astype(BF)
    qm = head_rows(q0.astype(F32)).astype(BF)
    qw = dot(qm, wqkv1[1], NT).astype(BF)
    xall = xb[...]
    scores = dot(qw, xall, NT)
    row = lax.broadcasted_iota(jnp.int32, scores.shape, 0) % S
    col = lax.broadcasted_iota(jnp.int32, scores.shape, 1)
    keep = jnp.zeros(scores.shape, jnp.bool_)
    for s in range(S):
        keep = keep | ((row == s) & (col >= 64 * s) & (col < 64 * s + tokens(s)))
    scores = jnp.where(keep, scores, MASKED)
    e = jnp.exp(scores - jnp.max(scores, 1, keepdims=True))
    prob = e * (1.0 / jnp.sum(e, 1, keepdims=True))
    probb = prob.astype(BF)
    ax = dot(probb, xall).astype(BF)
    c0 = (head_fold(dot(ax, wqkv1[2])) + bias_ref[1:2, 1, :]).astype(BF)
    copies[10].wait()
    n10, r10 = normalize(x0 + dot(c0, wo1[...]) + bias_ref[2:3, 1, :])
    h10 = n10 * gain_ref[1, 0:1, :] + bias_ref[3:4, 1, :]
    h10b = h10.astype(BF)
    copies[11].wait()
    f0 = dot(h10b, w11[...]) + wb_ref[1:2, :]
    g0, dg0 = gelu_pair(f0)
    g0b = g0.astype(BF)
    copies[12].wait()
    n20, r20 = normalize(h10 + dot(g0b, w21[...]) + bias_ref[4:5, 1, :])
    x20 = n20 * gain_ref[1, 1:2, :] + bias_ref[5:6, 1, :]
    e0 = x20.astype(BF)
    copies[13].wait()
    rp = dot(e0, wp[...]) + pb_ref[...].reshape(1, D)
    rp_out[...] = rp
    squashed = jnp.tanh(rp)
    unit = squashed * lax.rsqrt(jnp.sum(squashed * squashed, -1, keepdims=True) + EPS_UNIT)
    row = lax.broadcasted_iota(jnp.int32, (S, 128), 0)
    lane = lax.broadcasted_iota(jnp.int32, (S, 128), 1)
    tail = jnp.zeros((S, 128), F32)
    for s in range(S):
        if s < PH:
            label = lab_ref[s]
            tail = jnp.where((row == s) & (lane == 0), (label // 32).astype(F32), tail)
            tail = jnp.where((row == s) & (lane == 1), (label % 32).astype(F32), tail)
        tail = jnp.where((row == s) & (lane == 2), tokens(s).astype(F32), tail)
    pay_out[...] = jnp.concatenate([unit, tail], 1).astype(BF)
    small_out[0] = n10
    small_out[1] = n20
    small_out[2] = jnp.broadcast_to(r10, n10.shape)
    small_out[3] = jnp.broadcast_to(r20, n10.shape)
    wide_out[...] = dg0
    big_out[:, 0:D] = c0
    big_out[:, D:2 * D] = x0b
    for i in range(cut.GX):
        lanes = slice(i * D // cut.GX, (i + 1) * D // cut.GX)
        factors[i] = jnp.concatenate([e0[:, lanes], h10b[:, lanes], g0b[:, i * FF // cut.GX:(i + 1) * FF // cut.GX]], 1)
    for r, out in enumerate(row_outs):
        out[...] = factors[place()[0] ^ r] if cut.GX > 1 else factors[0]
    a1_out[...] = probb
    ax_out[...] = ax
    qm_out[...] = qm
    qw_out[...] = qw
    for copy in stores:
        copy.wait()


def forward(cut, x, lengths, labels, wqkv, wo, w1, w2, wp, bias, gains, wb, pb):
    T, D = x.shape
    S = T // 64
    FF = w1.shape[2]
    nb = (S // 2) * (D // 128)
    sd = jax.ShapeDtypeStruct
    hbm = pl.BlockSpec(memory_space=pltpu.HBM)
    vm = pl.BlockSpec(memory_space=pltpu.VMEM)
    td = sd((T, D), BF)
    tr = sd((T, 128), F32)
    outs = [td, td, td, sd((nb, 128, 256), BF), td, tr, sd((T, FF), BF), td, tr, td,
            sd((4, S, D), F32), sd((S, 2 * D), BF), sd((H * S, T), BF), sd((H * S, D), BF),
            sd((H * S, D), BF), sd((H * S, D), BF), sd((S, FF), F32), sd((S, D), F32), sd((S, D + 128), BF)]
    outs += [sd((S, 6 * D // cut.GX), BF)] * cut.GX
    outs += [sd((7, T, D // cut.C), BF)] * cut.C
    out_specs = [hbm] * 10 + [vm] * (9 + cut.GX) + [hbm] * cut.C
    V = pltpu.VMEM
    b, r = V((T, D), BF), V((T, 128), F32)
    scratch = [b, V((3, D, D), BF), V((D, D), BF), V((D, FF), BF), V((FF, D), BF),
               V((3, D, D), BF), V((D, D), BF), V((D, FF), BF), V((FF, D), BF), V((D, D), BF),
               b, b, b, V((nb, 128, 256), BF), b, b, r, b, V((T, FF), BF), b, r, b,
               V((T, D), F32), V((T, D), F32), V((S, D), F32), V((cut.C, 7, T, D // cut.C), BF),
               V((cut.GX, S, 6 * D // cut.GX), BF),
               pltpu.SemaphoreType.DMA((14,)), pltpu.SemaphoreType.DMA((12,))]
    return pl.pallas_call(
        functools.partial(fwd_kernel, cut), out_shape=outs, out_specs=out_specs,
        in_specs=[pl.BlockSpec(memory_space=pltpu.SMEM)] * 2 + [hbm] * 6 + [vm] * 4,
        scratch_shapes=scratch, name="encode",
        compiler_params=pltpu.CompilerParams(vmem_limit_bytes=55 << 20),
    )(lengths, labels, x, wqkv, wo, w1, w2, wp, bias, gains, wb, pb)


HBM = pl.BlockSpec(memory_space=pltpu.HBM)
VM = pl.BlockSpec(memory_space=pltpu.VMEM)
SM = pl.BlockSpec(memory_space=pltpu.SMEM)


def norm_back(grad, n, root, gain):
    gn = grad * gain
    inner = jnp.mean(gn * n, -1, keepdims=True)
    return root * (gn - jnp.mean(gn, -1, keepdims=True) - n * inner)


def total_rows(values):
    return jnp.sum(values, 0, keepdims=True)


def runs(mode):
    return [(axis, mode.index(axis), mode.count(axis)) for axis in sorted(set(mode), reverse=True)]


def emit(cut, mode, parts, outs):
    if cut.C == 1:
        outs[0][...] = parts[0][...]
        return
    side = dict(zip("yx", place()[2:4]))
    for i, (axis, _, _) in enumerate(runs(mode)):
        bit = side[axis]
        outs[2 * i][...] = parts[i][bit]
        outs[2 * i + 1][...] = parts[i][1 - bit]


def pieces(cut, mode, rows, lanes):
    if cut.C == 1:
        return [pltpu.VMEM((1, 1, 1, rows, lanes), BF)], [sds((1, 1, 1, rows, lanes), BF)]
    scratch = [pltpu.VMEM((2, 2, n, rows, lanes), BF) for _, _, n in runs(mode)]
    return scratch, [sds((2, n, rows, lanes), BF) for _, _, n in runs(mode) for _ in range(2)]


def put(cut, mode, parts, y, x, z, value, rows=slice(None), lanes=slice(None)):
    if cut.C == 1:
        parts[0][0, 0, 0, rows, lanes] = value
        return
    for part, (axis, start, n) in zip(parts, runs(mode)):
        if start <= z < start + n:
            first, second = (y, x) if axis == "y" else (x, y)
            part[first, second, z - start, rows, lanes] = value


def start_all(pairs, sem):
    copies = [pltpu.make_async_copy(s, d, sem.at[i]) for i, (s, d) in enumerate(pairs)]
    for copy in copies:
        copy.start()
    return copies


def join(refs, out):
    out[...] = jnp.concatenate([ref[...].astype(F32) for ref in refs], 0).astype(BF)


def top_kernel(cut, PH, count, extra, gain_ref, *refs):
    local, (wqkv_hbm, wo_hbm, w1_hbm, w2_hbm, wp_hbm), rest = refs[:15], refs[15:20], refs[20:]
    bufs, rest = rest[-16:-1], rest[:-16] + rest[-1:]
    (own_ref, rp_ref, small_ref, big_ref, dg_ref, a1_ref, ax_ref, qm_ref, qw_ref, xb_ref, n2_ref, r2_ref,
     n1_ref, r1_ref, dg0_ref) = bufs
    early = start_all(list(zip(local, bufs)), rest[-1].at[pl.ds(7, 15)])
    gathered = rest[:count]
    join(rest[count:count + cut.GX], rest[count + extra])
    rest = rest[:count + extra] + rest[count + extra + 1:]
    (loss_out, tot_out, gy_out, vec_out, eb_out, gf_out, eb0_out, gz1_out, gc_out, vec2_out), rest = (
        rest[count + extra:count + extra + 10], rest[count + extra + 10:])
    (stay_out, go_out), rest = (rest[0], rest[1 if cut.C == 2 else 0]), rest[cut.C:]
    wqkv, wo, w1, w2, wp, gx, left_s, sem = rest
    D = wo.shape[0]
    FF = w1.shape[1]
    for copy in early[:12]:
        copy.wait()
    S = own_ref.shape[0]
    R = sum(g.shape[0] for g in gathered)
    T = xb_ref.shape[0]
    loads = [(wp_hbm, wp), (w2_hbm.at[1], w2), (w1_hbm.at[1], w1), (wo_hbm.at[1], wo)]
    for p in range(3):
        loads.append((wqkv_hbm.at[1, :, pl.ds(p * D, D)], wqkv.at[p]))
    copies = [pltpu.make_async_copy(s, d, sem.at[i]) for i, (s, d) in enumerate(loads)]
    for copy in copies:
        copy.start()
    gxi, gyi = place()[0], place()[5]
    me = gxi * lax.axis_size("gy") + gyi

    def device(j):
        r = j // S
        if cut.C == 1:
            return r
        flips = ((r // 8) % 2 * 2 + r // 16) * 8 + r % 4 * 2 + (r // 4) % 2
        return me ^ flips


    everyone = jnp.concatenate([g[...] for g in gathered], 0) if count > 1 else gathered[0][...]
    units = everyone[:, 0:D]
    extra = everyone[:, D:D + 128]
    i8 = lax.broadcasted_iota(jnp.int32, (8, 128), 0)
    l8 = lax.broadcasted_iota(jnp.int32, (8, 128), 1)
    pick = jnp.where((i8 == 0) & (l8 == 0), 32.0, 0.0) + jnp.where((i8 == 0) & (l8 == 1), 1.0, 0.0)
    pick = pick + jnp.where((i8 == 1) & (l8 == 2), 1.0, 0.0)
    meta = dot(pick.astype(BF), extra, NT)
    label_row = meta[0:1, :]
    tokens = jnp.sum(meta[1:2, :], 1, keepdims=True)
    tot_out[...] = jnp.broadcast_to(tokens, tot_out.shape)
    parts = []
    BLK = min(R, 256)
    for b in range(R // BLK):
        mat = SCORE * dot(units, units[b * BLK:(b + 1) * BLK, :], NT)
        j = lax.broadcasted_iota(jnp.int32, (R, BLK), 0)
        target = (j % S) >= PH
        pair = (device(j) * PH + (j % S) - PH).astype(F32)
        chosen = target & (pair == label_row[:, b * BLK:(b + 1) * BLK])
        logits = jnp.where(target, mat - jnp.where(chosen, SCORE * MARGIN, 0.0), -1e30)
        top = jnp.max(logits, 0, keepdims=True)
        parts.append(top + jnp.log(jnp.sum(jnp.exp(logits - top), 0, keepdims=True)))
    lse_row = jnp.concatenate(parts, 1) if len(parts) > 1 else parts[0]
    own_units = own_ref[:, 0:D]
    own_extra = own_ref[:, D:D + 128].astype(F32)
    own_label = 32.0 * own_extra[:, 0:1] + own_extra[:, 1:2]
    mat = SCORE * dot(own_units, units, NT)
    j = lax.broadcasted_iota(jnp.int32, (S, R), 1)
    r = lax.broadcasted_iota(jnp.int32, (S, R), 0)
    target = (j % S) >= PH
    pair = (device(j) * PH + (j % S) - PH).astype(F32)
    chosen = target & (pair == own_label)
    logits = jnp.where(target, mat - jnp.where(chosen, SCORE * MARGIN, 0.0), -1e30)
    top = jnp.max(logits, 1, keepdims=True)
    lse = top + jnp.log(jnp.sum(jnp.exp(logits - top), 1, keepdims=True))
    loss = lse - jnp.sum(jnp.where(chosen, logits, 0.0), 1, keepdims=True)
    loss_out[...] = jnp.broadcast_to(loss, loss_out.shape)
    from_source = jnp.where(target, jnp.exp(logits - lse), 0.0) - jnp.where(chosen, 1.0, 0.0)
    pair_own = (me * PH + r - PH).astype(F32)
    source = (j % S) < PH
    chosen_t = source & (label_row == pair_own)
    logits_t = mat - jnp.where(chosen_t, SCORE * MARGIN, 0.0)
    from_target = jnp.where(source, jnp.exp(jnp.where(source, logits_t - lse_row, 0.0)), 0.0)
    from_target = from_target - jnp.where(chosen_t, 1.0, 0.0)
    glog = jnp.where(r < PH, from_source, from_target).astype(BF)
    gu = SCORE * dot(glog, units)
    squashed = jnp.tanh(rp_ref[...])
    rs = lax.rsqrt(jnp.sum(squashed * squashed, -1, keepdims=True) + EPS_UNIT)
    gt = rs * (gu - squashed * (rs * rs * jnp.sum(gu * squashed, -1, keepdims=True)))
    gr = (gt * (1.0 - squashed * squashed)).astype(BF)
    copies[0].wait()
    gx2 = dot(gr, wp[...], NT)

    n1, n2, r1, r2 = small_ref[0], small_ref[1], small_ref[2], small_ref[3]
    gz2 = norm_back(gx2, n2, r2, gain_ref[1, 1:2, :])
    gy = gz2.astype(BF)
    copies[1].wait()
    gf = (dot(gy, w2[...], NT) * dg_ref[...]).astype(BF)
    again = [pltpu.make_async_copy(w2_hbm.at[0], w2, sem.at[22])]
    again[0].start()
    copies[2].wait()
    gh1 = gz2 + dot(gf, w1[...], NT)
    again.append(pltpu.make_async_copy(w1_hbm.at[0], w1, sem.at[23]))
    again[1].start()
    gz1 = norm_back(gh1, n1, r1, gain_ref[1, 0:1, :])
    go = gz1.astype(BF)
    copies[3].wait()
    gc = dot(go, wo[...], NT).astype(BF).astype(F32)
    again.append(pltpu.make_async_copy(wo_hbm.at[0], wo, sem.at[24]))
    again[2].start()
    gcm = head_rows(gc).astype(BF)
    for i in (4, 5, 6):
        copies[i].wait()
    gcw = dot(gcm, wqkv[2], NT).astype(BF)
    xall = xb_ref[...]
    prob = a1_ref[...].astype(F32)
    ga = dot(gcw, xall, NT)
    gs = (prob * (ga - jnp.sum(ga * prob, 1, keepdims=True))).astype(BF)
    mm = dot(gs, xall).astype(BF)
    gpq = head_fold(dot(mm, wqkv[1])).astype(BF).astype(F32) * SCALE
    gpqb = gpq.astype(BF)
    back = dot(jnp.concatenate([gs, a1_ref[...]], 0), jnp.concatenate([qw_ref[...], gcw], 0), TN)
    gx[...] = back
    first = gz1 + dot(gpqb, wqkv[0], NT)
    for s in range(S):
        gx[64 * s:64 * s + 1, :] += first[s:s + 1, :]

    nx = n2_ref[...].astype(F32)
    gxv = gx[...]
    gzx = norm_back(gxv, nx, r2_ref[:, 0:1], gain_ref[0, 1:2, :])
    gyx = gzx.astype(BF)
    gy_out[...] = gyx
    for copy in early[12:]:
        copy.wait()
    again[0].wait()
    again[1].wait()
    gx[...] = gzx

    def feed(i, _):
        cols = pl.ds(pl.multiple_of(i * D, D), D)
        part = (dot(gy_out[...], w2[cols, :], NT) * dg0_ref[:, cols].astype(F32)).astype(BF)
        gf_out[:, cols] = part
        eb0_out[0:1, cols] = total_rows(part.astype(F32))
        gx[...] += dot(part, w1[:, cols], NT)
        return 0

    lax.fori_loop(0, FF // D, feed, 0)
    gh = gx[...]
    n10 = n1_ref[...].astype(F32)
    gz10 = norm_back(gh, n10, r1_ref[:, 0:1], gain_ref[0, 0:1, :])
    gz1_out[...] = gz10
    go0 = gz10.astype(BF)
    gf_out[:, FF:] = go0
    vec2_out[0:1, :] = total_rows(gh)
    vec2_out[1:2, :] = total_rows(gh * n10)
    vec2_out[2:3, :] = total_rows(go0.astype(F32))
    vec2_out[3:8, :] = jnp.zeros((5, D), F32)
    again[2].wait()
    gc_out[...] = dot(go0, wo[...], NT).astype(BF)

    vec_out[0:1, :] = total_rows(gpqb.astype(F32))
    vec_out[1:2, :] = total_rows(gc)
    vec_out[2:3, :] = total_rows(go.astype(F32))
    vec_out[3:4, :] = total_rows(gh1)
    vec_out[4:5, :] = total_rows(gy.astype(F32))
    vec_out[5:6, :] = total_rows(gx2)
    vec_out[6:7, :] = total_rows(gh1 * n1)
    vec_out[7:8, :] = total_rows(gx2 * n2)
    vec_out[8:9, :] = total_rows(gr.astype(F32))
    vec_out[9:10, :] = total_rows(gxv)
    vec_out[10:11, :] = total_rows(gxv * nx)
    vec_out[11:12, :] = total_rows(gyx.astype(F32))
    vec_out[12:16, :] = jnp.zeros((4, D), F32)
    eb_out[...] = total_rows(gf.astype(F32))

    width = D // cut.GX
    cut_up = lambda v: [v[:, i * width:(i + 1) * width] for i in range(v.shape[1] // width)]
    c0, x0 = big_ref[:, 0:D].astype(F32), big_ref[:, D:2 * D].astype(F32)
    mmf, axf = mm.astype(F32), ax_ref[...].astype(F32)
    for g in range(cut.GX):
        lanes = slice(g * width, (g + 1) * width)
        blocks = [v[h * S:(h + 1) * S, lanes] for v in (mmf, axf) for h in range(H)]
        blocks += [x0[:, lanes], c0[:, lanes]]
        dst = g if cut.C == 1 else g ^ gxi
        for i, block in enumerate(blocks):
            left_s[dst, i] = block.astype(BF)
    q0 = head_fold(qm_ref[...].astype(F32))
    right = cut_up(gpq) + cut_up(q0) + cut_up(gc) + cut_up(go.astype(F32))
    grf, gyf, gff = gr.astype(F32), gy.astype(F32), gf.astype(F32)
    dn, df = D // cut.GY, FF // cut.GY
    for g in range(cut.GY):
        mix = jnp.concatenate([grf[:, g * dn:(g + 1) * dn], gyf[:, g * dn:(g + 1) * dn],
                               gff[:, g * df:(g + 1) * df]], 1)
        right += cut_up(mix)
    right = [block.astype(BF) for block in right]
    L = LEFT
    for out, base in (((stay_out, 0), (go_out, 2)) if cut.C == 2 else ((stay_out, 0),)):
        for r in range(cut.C):
            out[r * L:(r + 1) * L] = left_s[base + r]
        for i, block in enumerate(right):
            out[cut.C * L + i] = block


LEFT = 2 * H + 2


def params(mb):
    return pltpu.CompilerParams(vmem_limit_bytes=mb << 20)


def cost(weight=0.0):
    return pl.CostEstimate(flops=int(weight * UNIT), bytes_accessed=1, transcendentals=0)


UNIT = 10 ** 10
MODE = {2: "yyxx", 3: "yyyy", 4: "yyxx"}
LONG = 1000.0


def call(kernel, name, mb, outs, ins, hbm=(), smem=(), scratch=(), after=(), weight=0.0):
    hbm = [in_hbm(t) for t in hbm]
    return pl.pallas_call(
        functools.partial(kernel), out_shape=list(outs), name=name,
        in_specs=[SM] * len(smem) + [VM] * len(ins) + [HBM] * (len(hbm) + len(after)), out_specs=[VM] * len(outs),
        scratch_shapes=list(scratch), compiler_params=params(mb), cost_estimate=cost(weight),
    )(*smem, *ins, *hbm, *after)


def in_hbm(t):
    return pltpu.with_memory_space_constraint(t, pltpu.HBM)


def sds(shape, dtype):
    return jax.ShapeDtypeStruct(shape, dtype)


def top(cut, after, factors, gathered, own, rp, small, big, dg, a1, ax, qm, qw, xb, n2, r2, n1, r1, dg0, gains, wqkv, wo, w1, w2, wp):
    S = own.shape[0]
    T, D = xb.shape
    FF = w1.shape[2]
    width = D // cut.GX
    V = pltpu.VMEM
    count = cut.C * LEFT + 4 * cut.GX + (2 * D + FF) // width
    td = sds((T, D), BF)
    after = [*factors, *after]
    outs = [sds((S * cut.GX, factors[0].shape[1]), BF), sds((S, 128), F32), sds((8, 128), F32), td, sds((16, D), F32), sds((1, FF), F32), sds((T, FF + D), BF),
            sds((1, FF), F32), sds((T, D), F32), td, sds((8, D), F32)] + [sds((count, S, width), BF)] * cut.C
    local = (own, rp, small, big, dg, a1, ax, qm, qw, xb, n2, r2, n1, r1, dg0)
    bufs = [V(t.shape, t.dtype) for t in local]
    return pl.pallas_call(
        functools.partial(top_kernel, cut, S // 2, len(gathered), len(after)), out_shape=outs,
        in_specs=[VM] + [HBM] * 20 + [VM] * (len(gathered) + cut.GX) + [HBM] * (len(after) - cut.GX), out_specs=[VM] * len(outs),
        scratch_shapes=[V((3, D, D), BF), V((D, D), BF), V((D, FF), BF), V((FF, D), BF), V((D, D), BF),
                        V((T, D), F32), V((cut.GX, LEFT, S, width), BF), *bufs, pltpu.SemaphoreType.DMA((25,))],
        name="rank_and_top_back", compiler_params=params(44 if cut.C == 2 else 58), cost_estimate=cost(),
    )(gains, *(in_hbm(t) for t in (*local, wqkv, wo, w1, w2, wp)), *gathered, *after)


def peers_of(cut, refs):
    L = LEFT
    if cut.C == 1:
        return [(refs[0], 0, L)]
    stay, got_y, got_c = refs
    n = stay.shape[0] - 2 * L
    return [(stay, 0, 2 * L), (got_y, 0, 2 * L), (got_c, 0, 2 * L), (got_c, L, 2 * L + n)]


def top_weights_kernel(cut, S, count, *refs):
    peers = peers_of(cut, refs[:count])
    outs = refs[count:]
    sides = cut.X
    chunks, part, stage = outs[:sides], outs[-2], outs[-1]
    xbit = place()[3] if sides == 2 else 0
    width = refs[0].shape[2]
    D = width * cut.GX
    G = cut.GX
    get = lambda ref, i: ref[i].astype(F32)
    lane_cat = lambda ref, i, m: jnp.concatenate([get(ref, i + k) for k in range(m)], 1) if m > 1 else get(ref, i)
    rights = [[lane_cat(ref, ro + k * G, G) for k in range(4)] for ref, lo, ro in peers]
    low = lax.broadcasted_iota(jnp.int32, (S, 128), 1) < HD
    stack = lambda pieces: jnp.concatenate(pieces, 0).astype(BF)
    cols = [dot(stack([get(ref, lo + 2 * H) for ref, lo, ro in peers]), stack([r[0] for r in rights]), TN)]
    for kind in range(2):
        for j in range(D // 128):
            lhs, rhs = [], []
            for (ref, lo, ro), r in zip(peers, rights):
                lhs += [get(ref, lo + kind * H + 2 * j), get(ref, lo + kind * H + 2 * j + 1)]
                blk = r[kind + 1][:, 128 * j:128 * j + 128]
                rhs += [jnp.where(low, blk, 0.0), jnp.where(low, 0.0, blk)]
            cols.append(dot(stack(lhs), stack(rhs), TN))
    qkv = jnp.concatenate(cols, 1)
    out = dot(stack([get(ref, lo + 2 * H + 1) for ref, lo, ro in peers]), stack([r[3] for r in rights]), TN)
    wa, wb = 3 * D // cut.GY, D // cut.GY
    halves = []
    for x in range(sides):
        blocks = []
        for z in range(cut.Z):
            b = z * sides + x
            blocks.append(jnp.concatenate(
                [qkv[:, b * wa:(b + 1) * wa], out[:, b * wb:(b + 1) * wb]], 1).astype(BF))
        halves.append(blocks)
    for z in range(cut.Z):
        for x in range(sides):
            part[x, z] = halves[x][z]
    for r, dst in enumerate(chunks):
        for z in range(cut.Z):
            dst[z * width:(z + 1) * width, :] = part[xbit ^ r, z] if sides == 2 else part[0, z]
    m = (2 * D + 4 * D) // cut.GY // width
    if sides == 1:
        ref, lo, ro = peers[0]
        outs[1][...] = ref[ro + 4 * G:ro + 4 * G + m]
        return
    n = cut.Z * width
    for r, dst in enumerate(chunks):
        x = xbit ^ r
        for p, (ref, lo, ro) in enumerate(peers):
            lanes = slice(p % 2 * width, (p % 2 + 1) * width)
            for z in range(cut.Z):
                for i in range(m):
                    to = n + ((z * 2 + p // 2) * m + i) * S
                    piece = ref[pl.ds(ro + 4 * G + (z * sides + x) * m + i, 1)]
                    stage[to - n:to - n + S, lanes] = piece[0].astype(F32)
        dst[n:, :] = stage[...].astype(BF)


def top_weights(cut, arrays, left=(), after=()):
    S, width = arrays[0].shape[1:]
    D = width * cut.GX
    peers = 4 if cut.C == 2 else 1
    m = 6 * D // cut.GY // width
    lanes = 4 * D // cut.GY
    extra = cut.Z * (peers // 2) * m * S
    outs = [sds((cut.Z * width + extra, lanes), BF)] * cut.X
    if cut.C == 1:
        outs.append(sds((m, S, width), BF))
    n = len(arrays)
    if cut.C == 2:
        outs.append(sds((2 * left[0].shape[0], left[0].shape[1]), BF))

    def kernel(*refs):
        ins, (left_a, left_b), refs = refs[:n], refs[n:n + 2] if left else (None, None), refs[n + len(left) + len(after):]
        if left:
            refs[cut.X][0:left_a.shape[0], :] = left_a[...]
            refs[cut.X][left_a.shape[0]:, :] = left_b[...]
            refs = refs[:cut.X] + refs[cut.X + 1:]
        top_weights_kernel(cut, S, n, *ins, *refs)

    return call(kernel, "top_weights", 20, outs, [*arrays, *left], after=after,
                scratch=[pltpu.VMEM((cut.X, cut.Z, width, lanes), BF), pltpu.VMEM((max(extra, 8), lanes), F32)], weight=LONG)


def pack_kernel(stay, got, left_a, left_b, *rest):
    out, left_out = rest[-2:]
    left_out[0:left_a.shape[0], :] = left_a[...]
    left_out[left_a.shape[0]:, :] = left_b[...]
    L = LEFT
    n = stay.shape[0] - 2 * L
    for src, lo, dst, m in ((stay, L, 0, L), (got, L, L, L), (stay, 2 * L, 2 * L, n), (got, 2 * L, 2 * L + n, n)):
        out[dst:dst + m] = src[lo:lo + m]


def pack(stay, got, left, left_got, after=()):
    n = 2 * (stay.shape[0] - LEFT)
    outs = [sds((n,) + stay.shape[1:], BF), sds((2 * left.shape[0], left.shape[1]), BF)]
    return call(pack_kernel, "pack", 8, outs, (stay, got, left, left_got), after=after)


def row_weights_kernel(cut, lefts, rights, pool_out, expand_out, reduce_out):
    dk = lefts[0].shape[-1] // 6
    D = dk * cut.GX
    dn = D // cut.GY
    if cut.C == 2:
        rows = []
        for d in range(4):
            ref, base = rights[d // 2], (0, dk)[d // 2]
            for s in range(2):
                for p in range(4):
                    at = base + d % 2 * 96 + s * 48 + p // 2 * 24
                    lanes = slice(p % 2 * dk, (p % 2 + 1) * dk)
                    rows.append(jnp.concatenate([ref[at + 8 * i:at + 8 * i + 8, lanes].astype(F32) for i in range(3)], 1))
        own, got = lefts
        n, lanes = own.shape[0], got.shape[1]
        blocks = [got[got.shape[0] - (3 - i) * n:got.shape[0] - (2 - i) * n, :] for i in range(3)]
        right = jnp.concatenate(rows, 0).astype(BF)
        near = jnp.concatenate([b.astype(F32) for b in blocks], 1).astype(BF)
        h = n // 2
        left = jnp.concatenate([own[0:h, :], near[0:h, :], own[h:, :], near[h:, :]], 0)
    else:
        left = lefts[0][...]
        right = jnp.concatenate([rights[0][i] for i in range(rights[0].shape[0])], 1)
    pool_out[...] = dot(left[:, 0:dk], right[:, 0:dn], TN)
    expand_out[...] = dot(left[:, dk:2 * dk], right[:, 2 * dn:], TN)
    reduce_out[...] = dot(right[:, dn:2 * dn], left[:, 2 * dk:], TN)


def row_weights(cut, lefts, rights, after=()):
    dk = lefts[0].shape[-1] // 6
    dn = dk * cut.GX // cut.GY
    outs = [sds((dk, dn), F32), sds((dk, 4 * dn), F32), sds((dn, 4 * dk), F32)]
    m, n = len(lefts), len(lefts) + len(rights)
    kernel = lambda *refs: row_weights_kernel(cut, refs[:m], refs[m:n], *refs[n + len(after):])
    return call(kernel, "row_weights", 32, outs, (*lefts, *rights), after=after)


def narrow_weight_kernel(cut, *refs):
    C = cut.C
    mode = MODE[2]
    m = 2 * C + (2 * len(runs(mode)) if C == 2 else 1)
    gys, acts, outs, parts, turned = refs[:C], refs[C:2 * C], refs[2 * C:m], refs[m:-1], refs[-1]
    T, D = acts[0].shape[1], acts[0].shape[2] * C
    nw = D // cut.GY
    width = D // C
    for c in range(C):
        turned[c] = gys[c][...].T

    def weigh(b, _):
        res = dot(turned[0], acts[0][b])
        for c in range(1, C):
            res = res + dot(turned[c], acts[c][b])
        res = res.astype(BF)
        for x in range(cut.X):
            for z in range(cut.Z):
                g = z * cut.X + x
                value = res[g * nw:(g + 1) * nw, :]
                if C == 1:
                    put(cut, mode, parts, 0, x, z, value, lanes=pl.ds(pl.multiple_of(b * width, 128), width))
                else:
                    put(cut, mode, parts, b // 2, x, z, value, pl.ds(pl.multiple_of(b % 2 * nw, 16), nw))
        return 0

    lax.fori_loop(0, 4, weigh, 0)
    emit(cut, mode, parts, outs)


def narrow_weight(cut, gys, acts, after=()):
    D = acts[0].shape[2] * cut.C
    scratch, outs = pieces(cut, MODE[2], cut.C * D // cut.GY, 4 * D // cut.GX // cut.C)
    n = 2 * cut.C
    kernel = lambda *refs: narrow_weight_kernel(cut, *refs[:n], *refs[n + len(after):])
    return call(kernel, "narrowing_weight", 24, outs, (*gys, *acts), after=after,
                scratch=scratch + [pltpu.VMEM((cut.C, D, gys[0].shape[0]), BF)])


def widen_weight_kernel(cut, *refs):
    C = cut.C
    mode = MODE[3]
    m = 2 * C + (2 * len(runs(mode)) if C == 2 else 1)
    acts, gfs, outs, parts = refs[:C], refs[C:2 * C], refs[2 * C:m], refs[m:]
    width = acts[0].shape[2]
    D = width * C
    FF = gfs[0].shape[1] - D
    lw, kr = FF // cut.GY, D // cut.GX
    left = [a[4].T for a in acts]
    W = D
    for i in range(FF // W):
        res = dot(left[0], gfs[0][:, i * W:(i + 1) * W])
        for c in range(1, C):
            res = res + dot(left[c], gfs[c][:, i * W:(i + 1) * W])
        res = res.astype(BF)
        if C == 1:
            put(cut, mode, parts, 0, 0, 0, res, lanes=slice(i * W, (i + 1) * W))
            continue
        for h in range(W // lw):
            g = i * W // lw + h
            for y in range(cut.Y):
                put(cut, mode, parts, y, g % cut.X, g // cut.X, res[y * kr:(y + 1) * kr, h * lw:(h + 1) * lw])
    emit(cut, mode, parts, outs)


def widen_weight_back(cut, acts, gfs, after=()):
    D = acts[0].shape[2] * cut.C
    FF = gfs[0].shape[1] - D
    scratch, outs = pieces(cut, MODE[3], D // cut.GX, FF // cut.GY)
    n = 2 * cut.C
    kernel = lambda *refs: widen_weight_kernel(cut, *refs[:n], *refs[n + len(after):])
    return call(kernel, "widening_weight", 24, outs, (*acts, *gfs), after=after, scratch=scratch)


def attend_kernel(extra, gc, q, k, v, a, vec1, vec2, eb0, eb1, *rest):
    gp = rest[-1]
    T, D = q.shape
    S = T // 64
    lane = lax.broadcasted_iota(jnp.int32, (128, 128), 1)
    low = lane < HD
    NB = D // 128

    def heads(p, _):
        rows = pl.ds(pl.multiple_of(p * 128, 128), 128)
        for j in range(NB):
            lanes = slice(128 * j, 128 * j + 128)
            gcj = gc[rows, lanes]
            gcm = jnp.concatenate([jnp.where(low, gcj, 0), jnp.where(low, 0, gcj)], 0)
            qj = q[rows, lanes]
            qm = jnp.concatenate([jnp.where(low, qj, 0), jnp.where(low, 0, qj)], 0)
            pb = a[p * NB + j]
            prob = pb.astype(F32)
            gp[rows, 2 * D + 128 * j:2 * D + 128 * j + 128] = dot(pb, gcm).astype(BF)
            ga = dot(v[rows, lanes], gcm, NT)
            gs = (prob * (ga - jnp.sum(ga * prob, 0, keepdims=True))).astype(BF)
            gp[rows, D + 128 * j:D + 128 * j + 128] = dot(gs, qm).astype(BF)
            gq = dot(gs, k[rows, lanes], TN)
            gq = jnp.where(low, gq[:128], gq[128:]).astype(BF)
            gp[rows, lanes] = (gq.astype(F32) * SCALE).astype(BF)
        return 0

    lax.fori_loop(0, S // 2, heads, 0)
    one = lambda ref, i: ref[i:i + 1, :]
    vecs = [total_rows(gp[0:T, 0:D].astype(F32)), total_rows(gp[0:T, 2 * D:3 * D].astype(F32)),
            one(vec2, 2), one(vec2, 0), one(vec1, 11), one(vec1, 9)]
    vecs += [one(vec1, i) for i in range(6)] + [one(vec2, 1), one(vec1, 10), one(vec1, 6), one(vec1, 7), one(vec1, 8)]
    vecs += [jnp.zeros((1, D), F32)] * (32 - len(vecs))
    gp[T:T + 16, :] = jnp.zeros((16, 3 * D), BF)
    block = jnp.concatenate([jnp.concatenate(vecs[8 * i:8 * i + 8], 0) for i in range(3)], 1)
    wide = jnp.concatenate([eb[:, i * D:(i + 1) * D] for eb in (eb0, eb1) for i in range(4)], 0)
    wide = jnp.concatenate([wide, jnp.zeros((8, 2 * D), F32)], 1)
    gp[T:T + 16, :] = jnp.concatenate([block, wide], 0).astype(BF)


def attend_back(gc, q, k, v, a, vectors, after=()):
    T, D = gc.shape
    return call(functools.partial(attend_kernel, len(after)), "attention_back", 30,
                [sds((T + 16, 3 * D), BF)], (gc, q, k, v, a, *vectors), after=after, weight=LONG)


def acts_width(ref, C):
    return ref.shape[2] * C


class Lanes:
    def __init__(self, refs):
        self.refs, self.rows, self.width = refs, refs[0].shape[0], refs[0].shape[1]

    def get(self, rows, start, stop):
        w = self.width
        found = [self.refs[i][rows, max(start - i * w, 0):min(stop - i * w, w)]
                 for i in range(start // w, (stop + w - 1) // w)]
        return jnp.concatenate(found, 1) if len(found) > 1 else found[0]


def attend_weight_kernel(cut, *refs):
    C = cut.C
    mode = MODE[4]
    n = 1
    acts, gos, gps = refs[:C], refs[C:2 * C], [Lanes(refs[2 * C + c * n:2 * C + (c + 1) * n]) for c in range(C)]
    refs = refs[2 * C + C * n:]
    m = 2 * len(runs(mode)) if C == 2 else 1
    outs, parts, blocks = refs[:m], refs[m:-1], refs[-1]
    width = acts[0].shape[2]
    D = width * C
    T = gps[0].rows - 16
    ct = [a[5].T for a in acts]
    xt = [a[6].T for a in acts]
    wa, wb = 3 * D // cut.GY, D // cut.GY
    main = wa // 128 * 128
    tail = wa - main
    kr = D // cut.GX

    def place_rows(res, x, z, lanes):
        res = res.astype(BF)
        for y in range(cut.Y):
            put(cut, mode, parts, y, x, z, res[y * kr:(y + 1) * kr, :], slice(0, kr), lanes)

    both = lambda f: f(0) + f(1) if C == 2 else f(0)
    if cut.GY == 1:
        place_rows(dot(xt[0], gps[0].get(slice(0, T), 0, 3 * D)), 0, 0, slice(0, 3 * D))
        place_rows(dot(ct[0], gos[0][:, 4 * D:]), 0, 0, slice(3 * D, None))
        emit(cut, mode, parts, outs)
        return
    for x in range(cut.X):
        for z in range(cut.Z):
            a0 = (z * cut.X + x) * wa
            place_rows(both(lambda c: dot(xt[c], gps[c].get(slice(0, T), a0, a0 + main))), x, z, slice(0, main))
    order = [(x, z) for x in range(cut.X) for z in range(cut.Z)]
    for i in range(0, len(order), 2):
        def tails(c):
            ra, rb = [], []
            for x, z in order[i:i + 2]:
                g = z * cut.X + x
                a0, o0 = g * wa, 4 * D + g * wb
                ra += [gps[c].get(slice(0, T), a0 + main, a0 + wa), jnp.zeros((T, 128 - tail), BF)]
                rb += [jnp.zeros((T, tail), BF), gos[c][:, o0:o0 + wb]]
            return dot(xt[c], jnp.concatenate(ra, 1)) + dot(ct[c], jnp.concatenate(rb, 1))
        res = both(tails)
        for m, (x, z) in enumerate(order[i:i + 2]):
            place_rows(res[:, 128 * m:128 * m + 128], x, z, slice(main, wa + wb))
    core = place()[1]
    vec = both(lambda c: gps[c].get(slice(T, T + 16), 0, 3 * D).astype(F32))
    n = 4 * 8
    dv, dw = D // n, 4 * D // n
    for d in range(n):
        pieces = [vec[0:8, k * D + d * dv:k * D + (d + 1) * dv] for k in range(3)]
        row, at = d * dw // D, d * dw % D
        pieces += [jnp.zeros((8, 128 - 3 * dv), F32), vec[8 + row:9 + row, at:at + dw], vec[12 + row:13 + row, at:at + dw]]
        pieces[-2:] = [jnp.concatenate(pieces[-2:] + [jnp.zeros((6, dw), F32)], 0),
                       jnp.zeros((8, wa + wb - 128 - dw), F32)]
        blocks[d] = jnp.concatenate([jnp.concatenate(pieces, 1), jnp.zeros((8, wa + wb), F32)], 0).astype(BF)
    for y in range(cut.Y):
        for x in range(cut.X):
            for z in range(cut.Z):
                put(cut, mode, parts, y, x, z, blocks[(2 * y + core) * 8 + z * cut.X + x], slice(kr, kr + 16))
    emit(cut, mode, parts, outs)


def attend_weight(cut, acts, gyos, gps, after=()):
    D = acts[0].shape[2] * cut.C
    D4 = 4 * D
    kr = D // cut.GX + (16 if cut.C == 2 else 0)
    scratch, outs = pieces(cut, MODE[4], kr, D4 // cut.GY)
    ins = [*acts, *gyos, *(part for parts in gps for part in parts)]
    n = len(ins)
    kernel = lambda *refs: attend_weight_kernel(cut, *refs[:n], *refs[n + len(after):])
    return call(kernel, "attention_weight", 30, outs, ins, after=after,
                scratch=scratch + [pltpu.VMEM((32, 16, D4 // cut.GY), BF)])


def input_kernel(pairs, extra, len_ref, tot_ref, gz_ref, *rest):
    n = 1
    gp, w_hbm, (gx_out, sc_out, w, sem) = Lanes(rest[:n]), rest[n], rest[n + 1 + extra:]
    T, D = gz_ref.shape
    PH = len_ref.shape[1]
    copies = start_all([(w_hbm.at[0, :, pl.ds(i * D, D)], w.at[i]) for i in range(3)], sem)
    for copy in copies:
        copy.wait()
    gx_out[...] = gz_ref[...]

    def project(i, _):
        gx_out[...] += dot(gp.refs[0][0:T, pl.ds(pl.multiple_of(i * D, D), D)], w[i], NT)
        return 0

    lax.fori_loop(0, 3, project, 0)
    inverse = 1.0 / tot_ref[0:1, 0:1]
    for s in range(T // 64):
        rows = slice(64 * s, 64 * s + 64)
        factor = (2.0 * pairs) * len_ref[s // PH, s % PH].astype(F32) * inverse
        sc_out[rows, :] = gx_out[rows, :] * factor


def input_back(pairs, lengths, tot, gz1, gp, wqkv, after=()):
    T, D = gz1.shape
    return call(functools.partial(input_kernel, pairs, len(after)), "input_back", 24, [sds((T, D), F32)] * 2,
                (tot, gz1, *gp), (wqkv,), (lengths,),
                scratch=[pltpu.VMEM((3, D, D), BF), pltpu.SemaphoreType.DMA((3,))], after=after, weight=LONG)


def plus(a, b):
    return (a.astype(F32) + b.astype(F32)).astype(BF)


def flip(values, axis, bits):
    return lax.ppermute(values, axis, [(i, i ^ bits) for i in range(lax.axis_size(axis))])


def fold_kernel(mode, extra, *refs):
    n = 2 * len(runs(mode))
    ins, outs = refs[:n], refs[n + extra:]
    side = dict(zip("yx", place()[2:4]))
    for i, (axis, _, _) in enumerate(runs(mode)):
        bit = side["x" if axis == "y" else "y"]
        keep, got = ins[2 * i:2 * i + 2]
        mine, other = outs[2 * i:2 * i + 2]
        other[...] = plus(keep[1 - bit], got[1 - bit])
        mine[...] = plus(keep[bit], got[bit])


def spread_kernel(mode, extra, *refs):
    n = 2 * len(runs(mode))
    ins, left, (keep_out, send_out, total) = refs[:n], refs[n], refs[n + 1 + extra:]
    low = lax.rem(place()[4], 2)
    for i, (_, start, count) in enumerate(runs(mode)):
        total[start:start + count] = plus(ins[2 * i][...], ins[2 * i + 1][...])
    rows, lanes = total.shape[1:]
    for dst, parity in ((send_out, 1 - low), (keep_out, low)):
        for high in range(2):
            dst[high * rows:(high + 1) * rows] = total[high * 2 + parity]
    m = left.shape[0]
    for i in range(left.shape[1] // lanes):
        send_out[2 * rows + i * m:2 * rows + (i + 1) * m] = left[:, i * lanes:(i + 1) * lanes]


def spread(mode, ins, left, after=()):
    rows, lanes = ins[0].shape[-2:]
    keep, send = call(functools.partial(spread_kernel, mode, len(after)), "spread", 16,
                      [sds((2 * rows, lanes), BF), sds((2 * rows + left.size // lanes, lanes), BF)], [*ins, left],
                      after=after, scratch=[pltpu.VMEM((4, rows, lanes), BF)])
    return keep, flip(send, "gy", 2), send


def spread_rows_kernel(extra, kr, keep, got, *rest):
    keep_out, send_out = rest[extra:]
    low = lax.rem(place()[4], 2)
    m = (keep.shape[0] - 4 * kr) // 4
    for dst, parity in ((send_out, 1 - low), (keep_out, low)):
        for high in range(2):
            z = high * 2 + parity
            at = high * (kr + 2 * m)
            rows = pl.ds(pl.multiple_of(z * kr, 16), kr)
            dst[at:at + kr] = plus(keep[rows, :], got[rows, :])
            rows = pl.ds(pl.multiple_of(4 * kr + z * m, 16), m)
            dst[at + kr:at + kr + m] = keep[rows, :]
            dst[at + kr + m:at + kr + 2 * m] = got[rows, :]


def spread_rows(keep, got, kr, after=()):
    shape = sds((2 * kr + keep.shape[0] - 4 * kr, keep.shape[1]), BF)
    keep, send = call(functools.partial(spread_rows_kernel, len(after), kr), "spread_rows", 16, [shape] * 2,
                      (keep, got), after=after)
    return keep, flip(send, "gy", 2), send


def settle_two_kernel(extra, kr, keep, got, keep2, got2, *rest):
    own_out, rows_out, own2_out, send_out = rest[extra:]
    high = lax.div(place()[4], 2)
    n = keep.shape[0] // 2
    m = n - kr
    part = lambda ref, h, start, size: ref[pl.ds(pl.multiple_of(h * n + start, 16), size), :]
    send_out[0:kr] = plus(part(keep, 1 - high, 0, kr), part(got, 1 - high, 0, kr))
    own_out[...] = part(keep, high, 0, kr).astype(F32) + part(got, high, 0, kr).astype(F32)
    for i, src in enumerate((keep, got)):
        send_out[kr + i * m:kr + (i + 1) * m] = part(src, 1 - high, kr, m)
        rows_out[i * m:(i + 1) * m] = part(src, high, kr, m)
    r2 = keep2.shape[0] // 2
    two = lambda ref, h: ref[pl.ds(pl.multiple_of(h * r2, 16), r2), :]
    send_out[kr + 2 * m:] = plus(two(keep2, 1 - high), two(got2, 1 - high))
    own2_out[...] = two(keep2, high).astype(F32) + two(got2, high).astype(F32)


def settle_two(keep, got, keep2, got2, kr, after=()):
    lanes, m = keep.shape[1], keep.shape[0] - 2 * kr
    r2 = keep2.shape[0] // 2
    outs = [sds((kr, lanes), F32), sds((m, lanes), BF), sds((r2, lanes), F32), sds((kr + m + r2, lanes), BF)]
    own, rows, own2, send = call(functools.partial(settle_two_kernel, len(after), kr), "settle_two", 16, outs,
                                 (keep, got, keep2, got2), after=after, weight=0.1)
    return own, rows, own2, flip(send, "gy", 4)


def spread_two_kernel(modes, extra, *refs):
    count = [2 * len(runs(mode)) for mode in modes]
    ins, outs = refs[:sum(count)], refs[sum(count) + extra:]
    low = lax.rem(place()[4], 2)
    for k, mode in enumerate(modes):
        keep_out, send_out, total = outs[2 * k], outs[2 * k + 1], outs[4 + k]
        for i, (_, start, n) in enumerate(runs(mode)):
            total[start:start + n] = plus(ins[2 * i][...], ins[2 * i + 1][...])
        ins = ins[2 * len(runs(mode)):]
        for dst, parity in ((send_out, 1 - low), (keep_out, low)):
            for high in range(2):
                dst[high] = total[high * 2 + parity]


def spread_two(first, second, after=()):
    ins = [first.operands(), second.operands()]
    tails = [t[0].shape[-2:] for t in ins]
    outs = call(functools.partial(spread_two_kernel, (first.mode, second.mode), len(after)), "spread_two", 16,
                [sds((2,) + t, BF) for t in tails for _ in range(2)], ins[0] + ins[1], after=after,
                scratch=[pltpu.VMEM((4,) + t, BF) for t in tails])
    return [outs[0], flip(outs[1], "gy", 2), outs[2], flip(outs[3], "gy", 2)], outs[1]


def settle_last_kernel(extra, keep3, got3, keep4, got4, *rest):
    own_out, send_out = rest[extra:]
    high = lax.div(place()[4], 2)
    n = keep3.shape[1]
    for keep, got, rows in ((keep3, got3, slice(0, n)), (keep4, got4, slice(n, None))):
        send_out[rows, :] = plus(keep[1 - high], got[1 - high])
        own_out[rows, :] = keep[high].astype(F32) + got[high].astype(F32)


def settle_last(ins, after=()):
    shape = (ins[0].shape[1] + ins[2].shape[1], ins[0].shape[2])
    own, send = call(functools.partial(settle_last_kernel, len(after)), "settle_last", 16,
                     [sds(shape, F32), sds(shape, BF)], ins, after=after)
    return own, flip(send, "gy", 4), send


def cross(values, axis):
    return flip(values, "gy", 1) if axis == "x" else flip(values, "gx", 2)


class Share:
    def __init__(self, chunk, mode):
        self.mode = mode
        self.keep = chunk[0::2]
        self.got = [cross(t, axis) for t, (axis, _, _) in zip(chunk[1::2], runs(mode))]

    def operands(self):
        return [t for pair in zip(self.keep, self.got) for t in pair]

    def fold(self, *after):
        outs = call(functools.partial(fold_kernel, self.mode, len(after)), "fold", 16,
                    [sds(t.shape[1:], BF) for t in self.keep for _ in range(2)], self.operands(), after=after)
        self.keep = outs[0::2]
        self.got = [cross(t, "x" if axis == "y" else "y") for t, (axis, _, _) in zip(outs[1::2], runs(self.mode))]
        return outs[1]

    def spread(self, left, *after):
        return spread(self.mode, self.operands(), left, after)


def finish_wide_kernel(own2, got12, own34, got34, r1, e1, reduce_out, expand_out):
    n = own2.shape[0]
    two = own2[...] + got12[got12.shape[0] - n:, :].astype(F32)
    reduce_out[0] = jnp.concatenate([two[0:n // 2], two[n // 2:]], 1)
    reduce_out[1] = r1[...]
    expand_out[0] = own34[0:n, :] + got34[0:n, :].astype(F32)
    expand_out[1] = e1[...]


def finish_attend_kernel(wa, own34, got34, own1, got12, *outs):
    attend_out, output_out, bias_out, gains_out, wb_out, pb_out = outs
    kr = own1.shape[0]
    a, b = own34[kr:, :] + got34[kr:, :].astype(F32), own1[...] + got12[0:kr, :].astype(F32)
    for layer, v in enumerate((a[0:kr], b)):
        attend_out[layer] = v[:, 0:wa]
        output_out[layer] = v[:, wa:]
    vec = a[kr:kr + 8, :]
    dv = bias_out.shape[2]
    one = lambda i: vec[i % 8:i % 8 + 1, i // 8 * dv:i // 8 * dv + dv]
    for layer in range(2):
        for i in range(6):
            bias_out[i, layer:layer + 1, :] = one(6 * layer + i)
        for i in range(2):
            gains_out[layer, i:i + 1, :] = one(12 + 2 * layer + i)
    wb_out[...] = vec[0:2, 128:128 + 4 * dv]
    pb_out[...] = one(16)


def scatter(values, row_axis, col_axis):
    part = lax.psum_scatter(values.astype(BF), row_axis, scatter_dimension=0, tiled=True)
    return lax.psum_scatter(part, col_axis, scatter_dimension=1, tiled=True).astype(F32)


def shards(mesh, inputs, lengths, labels, wqkv, wo, w1, w2, bias, gains, wb, wp, pb):
    GX, GY = mesh.shape["gx"], mesh.shape["gy"]
    n = GX * GY
    near = (GX, GY) == (4, 8)
    cut = Cut(2, 2, 2, 4) if near else Cut(1, 1, 1, 1)
    PH = labels.shape[0]
    S = 2 * PH
    L, D = inputs.shape[2], inputs.shape[3]
    T = S * L
    FF = w1.shape[2]
    twin = lambda v: [v, flip(v, "gx", 1)] if near else [v]
    x = inputs.reshape(T, D)
    (q, k, v, a, n1, r1, dg, n2, r2, xb, small, big, a1, ax, qm, qw, dg1, rp, own, *rest) = forward(
        cut, x, lengths, labels, wqkv, wo, w1, w2, wp, bias.transpose(1, 0, 2), gains, wb, pb)
    factors, acts = rest[:cut.GX], rest[cut.GX:]
    if near:
        factors = [flip(factors[r], "gx", r) if r else factors[0] for r in (0, 2, 1, 3)]
        line = jnp.concatenate([own] + [flip(own, "gy", 2 * d) for d in (1, 2, 3)], 0)
        corner = lax.ppermute(line, ("gx", "gy"), [(i, i ^ 17) for i in range(n)])
        plane = jnp.concatenate([line, flip(line, "gy", 1), flip(line, "gx", 2), corner], 0)
        gathered = [plane, flip(plane, "gx", 1)]
        acts = [acts[0], flip(acts[1], "gx", 1)]
    else:
        gathered = [lax.all_gather(own, ("gx", "gy"), axis=0, tiled=True)]
    left, loss, tot, gy, vec1, eb1, gfo, eb0, gz1, gc, vec2, *rows = top(
        cut, acts[1:], factors, gathered, own, rp, small, big, dg1, a1, ax, qm, qw, xb, n2, r2, n1, r1, dg, gains, wqkv, wo, w1, w2, wp)
    gfs, vectors = twin(gfo), (vec1, vec2, eb0, eb1)
    shape = (2, PH, L, D)
    wa = 3 * D // GY
    gys = twin(gy)
    if near:
        stay, go_y = rows
        got_y = cross(go_y, "y")
        ch2 = narrow_weight(cut, gys, acts)
        s2 = Share(ch2, MODE[2])
        gp = attend_back(gc, q, k, v, a, vectors, (ch2[0],))
        gps = twin(gp[0])
        packed, left = pack(stay, got_y, left, cross(left, "x"), (gp[0],))
        ch3 = widen_weight_back(cut, acts, gfs, (packed,))
        s3 = Share(ch3, MODE[3])
        t = s2.fold(ch3[0])
        ch1 = top_weights(cut, [stay, got_y, flip(packed, "gx", 1)], (left, flip(left, "gy", 4)), (t,))
        got1 = cross(ch1[1], "x")
        ch4 = attend_weight(cut, acts, gfs, [[t] for t in gps], (ch1[0],))
        keep2, got2, t = s2.spread(ch1[2], ch4[0])
        left = [ch1[2], got2]
        t = s3.fold(t, got1)
        s4 = Share(ch4, MODE[4])
        kr, dn, dv = D // GX, D // GY, D // n
        keep1, got1, t = spread_rows(ch1[0], got1, kr, (t,))
        gx0, sc0 = input_back(n * PH, lengths, tot, gz1, gp, wqkv, (t,))
        t = s4.fold(gx0)
        own1, rows1, own2, got12 = settle_two(keep1, got1, keep2, got2, kr, (t,))
        last, t = spread_two(s3, s4, (rows1,))
        own34, got34, t = settle_last(last, (t, got12))
        d_pool, d_expand1, d_reduce1 = row_weights(cut, left, [rows1, got12], (t,))
        d_reduce, d_expand = call(
            finish_wide_kernel, "finish_wide", 16, [sds((2, dn, FF // GX), F32), sds((2, kr, FF // GY), F32)],
            (own2, got12, own34, got34, d_reduce1, d_expand1))
        d_reduce = d_reduce.transpose(0, 2, 1)
        d_attend, d_output, d_bias, d_gains, d_wb, d_pb = call(
            functools.partial(finish_attend_kernel, wa), "finish_attend", 16,
            [sds((2, kr, wa), F32), sds((2, kr, dn), F32), sds((6, 2, dv), F32), sds((2, 2, dv), F32),
             sds((2, FF // n), F32), sds((1, dv), F32)], (own34, got34, own1, got12))
        d_bias, d_pb = d_bias.transpose(1, 0, 2), d_pb.reshape(dv)
    else:
        ch2 = narrow_weight(cut, gys, acts)
        ch3 = widen_weight_back(cut, acts, gfs)
        ch1 = top_weights(cut, rows)
        gp = attend_back(gc, q, k, v, a, vectors)
        ch4 = attend_weight(cut, acts, gfs, [gp])
        gx0, sc0 = input_back(n * PH, lengths, tot, gz1, gp, wqkv)
        f1, f2, f3, f4 = (t[0].reshape(t[0].shape[-2:]) for t in (ch1, ch2, ch3, ch4))
        pool, expand1, reduce1 = row_weights(cut, [left], ch1[1:])
        d_attend = jnp.stack([scatter(t[:, :3 * D], "gx", "gy") for t in (f4, f1)])
        d_output = jnp.stack([scatter(t[:, 3 * D:], "gx", "gy") for t in (f4, f1)])
        d_expand = jnp.stack([scatter(t, "gx", "gy") for t in (f3, expand1)])
        d_reduce = jnp.stack([scatter(t, "gy", "gx").T for t in (f2, reduce1)])
        d_pool = scatter(pool, "gx", "gy")
        me = lax.axis_index("gx") * GY + lax.axis_index("gy")
        sums = lax.psum(jnp.concatenate([t[T:] for t in gp], 1).astype(F32), ("gx", "gy"))
        vec = sums[0:8].reshape(8, 3, D).transpose(1, 0, 2).reshape(24, D)
        vec = lax.dynamic_slice_in_dim(vec, me * (D // n), D // n, 1)
        d_bias, d_gains, d_pb = vec[0:12].reshape(2, 6, -1), vec[12:16].reshape(2, 2, -1), vec[16]
        d_wb = lax.dynamic_slice_in_dim(sums[8:16, :D].reshape(2, FF), me * (FF // n), FF // n, 1)
    return (loss[:PH, 0], gx0.reshape(shape), sc0.reshape(shape), d_attend, d_output, d_expand, d_reduce,
            d_bias, d_gains, d_wb, d_pool, d_pb)


def solution(mesh):
    both = ("gx", "gy")
    in_specs = (P(None, both, None, None), P(None, both), P(both)) + (P(),) * 9
    out_specs = (P(both), P(None, both, None, None), P(None, both, None, None), P(None, "gx", "gy"),
                 P(None, "gx", "gy"), P(None, "gx", "gy"), P(None, "gx", "gy"), P(None, None, both),
                 P(None, None, both), P(None, both), P("gx", "gy"), P(both))
    return jax.shard_map(functools.partial(shards, mesh), mesh=mesh, in_specs=in_specs, out_specs=out_specs,
                         check_vma=False)
```

```python
import functools
import jax
import jax.numpy as jnp
from jax import lax
from jax.sharding import PartitionSpec as P
from jax.experimental import pallas as pl
from jax.experimental.pallas import tpu as pltpu

H = 12
HD = 64


class Cut:
    def __init__(self, C, Y, X, Z):
        self.C, self.Y, self.X, self.Z = C, Y, X, Z
        self.GX, self.GY = C * Y, X * Z


BF = jnp.bfloat16
F32 = jnp.float32
ROOT_HALF = 0.7071067811865476
PHI_ZERO = 0.3989422804014327
MASKED = -1e9
EPS_NORM = 1e-12
EPS_UNIT = 1e-6
SCORE = 10.0
MARGIN = 0.3
SCALE = HD ** -0.5

NN = (((1,), (0,)), ((), ()))
NT = (((1,), (1,)), ((), ()))
TN = (((0,), (0,)), ((), ()))


def place():
    gx, gy = lax.axis_index("gx"), lax.axis_index("gy")
    return gx, lax.rem(gx, 2), lax.div(gx, 2), lax.rem(gy, 2), lax.div(gy, 2), gy


def dot(a, b, dims=NN):
    return lax.dot_general(a, b, dims, preferred_element_type=F32)


def normalize(z):
    centered = z - jnp.mean(z, -1, keepdims=True)
    variance = jnp.mean(centered * centered, -1, keepdims=True)
    root = lax.rsqrt(variance + EPS_NORM)
    return centered * root, root


def gelu_pair(f):
    cdf = 0.5 * (1.0 + lax.erf(f * ROOT_HALF))
    return f * cdf, cdf + f * (PHI_ZERO * jnp.exp(-0.5 * f * f))


def head_rows(values):
    lanes = lax.broadcasted_iota(jnp.int32, values.shape, 1) // HD
    return jnp.concatenate([jnp.where(lanes == h, values, 0) for h in range(H)], 0)


def head_fold(values):
    r = values.shape[0] // H
    lanes = lax.broadcasted_iota(jnp.int32, (r, values.shape[1]), 1) // HD
    out = jnp.zeros((r, values.shape[1]), values.dtype)
    for h in range(H):
        out = jnp.where(lanes == h, values[h * r:(h + 1) * r], out)
    return out


def by_core(cut, src, act, slot):
    if cut.C == 1:
        act[0, slot] = src[...]
        return
    width = src.shape[1] // cut.GX
    for ci in range(2):
        act[ci, slot] = jnp.concatenate(
            [src[:, (2 * y + ci) * width:(2 * y + ci + 1) * width] for y in range(cut.Y)], 1)


def fwd_kernel(cut, len_ref, lab_ref, x_hbm, wqkv_hbm, wo_hbm, w1_hbm, w2_hbm, wp_hbm, bias_ref, gain_ref, wb_ref, pb_ref,
               q_out, k_out, v_out, a_out, n1_out, r1_out, dg_out, n2_out, r2_out, xb_out,
               small_out, big_out, a1_out, ax_out, qm_out, qw_out, wide_out, rp_out, pay_out, *rest):
    row_outs, rest = rest[:cut.GX], rest[cut.GX:]
    acts = rest[:cut.C]
    (x, wqkv, wo, w1, w2, wqkv1, wo1, w11, w21, wp,
     q, k, v, a, c, n1, r1, hb, dg, n2, r2, xb, h1, acc, first, act, factors, sem, osem) = rest[cut.C:]
    core = place()[1]
    PH = lab_ref.shape[0]
    tokens = lambda s: len_ref[s // PH, s % PH]
    T, D = x.shape
    S = T // 64
    FF = w1.shape[1]
    loads = [(x_hbm, x)]
    for part in range(3):
        cols = pl.ds(part * D, D)
        loads.append((wqkv_hbm.at[0, :, cols], wqkv.at[part]))
    loads += [(wo_hbm.at[0], wo), (w1_hbm.at[0], w1), (w2_hbm.at[0], w2)]
    for part in range(3):
        cols = pl.ds(part * D, D)
        loads.append((wqkv_hbm.at[1, :, cols], wqkv1.at[part]))
    loads += [(wo_hbm.at[1], wo1), (w1_hbm.at[1], w11), (w2_hbm.at[1], w21), (wp_hbm, wp)]
    copies = [pltpu.make_async_copy(s, d, sem.at[i]) for i, (s, d) in enumerate(loads)]
    for copy in copies[:4]:
        copy.start()
    stores = []

    def store(src, dst):
        copy = pltpu.make_async_copy(src, dst, osem.at[len(stores)])
        copy.start()
        stores.append(copy)

    copies[0].wait()
    TILE = D
    for part, dst in enumerate((q, k, v)):
        copies[1 + part].wait()
        for copy in (copies[4:6], copies[6:7], copies[7:])[part]:
            copy.start()

        def project(j, _, part=part, dst=dst):
            cols = pl.ds(pl.multiple_of(j * TILE, TILE), TILE)
            p = dot(x[...], wqkv[part, :, cols])
            if part == 0:
                p = (p + bias_ref[0:1, 0, cols]) * SCALE
            if part == 2:
                p = p + bias_ref[1:2, 0, cols]
            dst[:, cols] = p.astype(BF)
            return 0

        lax.fori_loop(0, D // TILE, project, 0)
    store(q, q_out)
    store(k, k_out)
    store(v, v_out)

    key = lax.broadcasted_iota(jnp.int32, (128, 256), 0)
    query = lax.broadcasted_iota(jnp.int32, (128, 256), 1)
    lane = lax.broadcasted_iota(jnp.int32, (128, 128), 1)
    low = lane < HD

    def attend(p, _):
        rows = pl.ds(pl.multiple_of(p * 128, 128), 128)
        i = 2 * p
        limit = jnp.where(key < 64, len_ref[i // PH, i % PH], len_ref[i // PH, i % PH + 1] + 64)
        keep = ((key // 64) == ((query // 64) % 2)) & (key < limit)
        for j in range(D // 128):
            lanes = slice(128 * j, 128 * j + 128)
            qq = q[rows, lanes]
            qm = jnp.concatenate([jnp.where(low, qq, 0), jnp.where(low, 0, qq)], 0)
            s = jnp.where(keep, dot(k[rows, lanes], qm, NT), MASKED)
            e = jnp.exp(s - jnp.max(s, 0, keepdims=True))
            prob = (e * (1.0 / jnp.sum(e, 0, keepdims=True))).astype(BF)
            a[p * (D // 128) + j] = prob
            ctx = dot(prob, v[rows, lanes], TN)
            c[rows, lanes] = jnp.where(low, ctx[:128], ctx[128:]).astype(BF)
        return 0

    lax.fori_loop(0, S // 2, attend, 0)
    store(a, a_out)
    by_core(cut, c, act, 5)
    by_core(cut, x, act, 6)

    copies[4].wait()
    ROWS = 256

    def first_norm(i, _):
        rows = pl.ds(pl.multiple_of(i * ROWS, ROWS), ROWS)
        z = x[rows, :].astype(F32) + dot(c[rows, :], wo[...]) + bias_ref[2:3, 0, :]
        n, r = normalize(z)
        n1[rows, :] = n.astype(BF)
        r1[rows, :] = jnp.broadcast_to(r, (ROWS, 128))
        h = n * gain_ref[0, 0:1, :] + bias_ref[3:4, 0, :]
        h1[rows, :] = h
        hb[rows, :] = h.astype(BF)
        acc[rows, :] = h + bias_ref[4:5, 0, :]
        return 0

    lax.fori_loop(0, T // ROWS, first_norm, 0)
    store(n1, n1_out)
    store(r1, r1_out)
    by_core(cut, hb, act, 4)
    copies[5].wait()
    copies[6].wait()

    WIDE = D // cut.C

    def widen(j, _):
        cols = pl.ds(pl.multiple_of(j * D, D), D)
        f = dot(hb[...], w1[:, cols]) + wb_ref[0:1, cols]
        gj, dgj = gelu_pair(f)
        gj = gj.astype(BF)
        dg[:, cols] = dgj.astype(BF)
        for half in range(cut.C):
            act[j % cut.C, j // cut.C * cut.C + half] = gj[:, half * WIDE:(half + 1) * WIDE]
        acc[...] += dot(gj, w2[cols, :])
        return 0

    lax.fori_loop(0, FF // D, widen, 0)
    store(dg, dg_out)
    store(act.at[core], acts[0])
    if cut.C == 2:
        store(act.at[1 - core], acts[1])

    def second_norm(i, _):
        rows = pl.ds(pl.multiple_of(i * ROWS, ROWS), ROWS)
        n, r = normalize(acc[rows, :])
        n2[rows, :] = n.astype(BF)
        r2[rows, :] = jnp.broadcast_to(r, (ROWS, 128))
        h = n * gain_ref[0, 1:2, :] + bias_ref[5:6, 0, :]
        acc[rows, :] = h
        xb[rows, :] = h.astype(BF)
        return 0

    lax.fori_loop(0, T // ROWS, second_norm, 0)
    store(n2, n2_out)
    store(r2, r2_out)
    store(xb, xb_out)

    for s in range(S):
        first[s:s + 1, :] = acc[64 * s:64 * s + 1, :]
    x0 = first[...]
    x0b = x0.astype(BF)
    for i in (7, 8, 9):
        copies[i].wait()
    q0 = ((dot(x0b, wqkv1[0]) + bias_ref[0:1, 1, :]) * SCALE).astype(BF)
    qm = head_rows(q0.astype(F32)).astype(BF)
    qw = dot(qm, wqkv1[1], NT).astype(BF)
    xall = xb[...]
    scores = dot(qw, xall, NT)
    row = lax.broadcasted_iota(jnp.int32, scores.shape, 0) % S
    col = lax.broadcasted_iota(jnp.int32, scores.shape, 1)
    keep = jnp.zeros(scores.shape, jnp.bool_)
    for s in range(S):
        keep = keep | ((row == s) & (col >= 64 * s) & (col < 64 * s + tokens(s)))
    scores = jnp.where(keep, scores, MASKED)
    e = jnp.exp(scores - jnp.max(scores, 1, keepdims=True))
    prob = e * (1.0 / jnp.sum(e, 1, keepdims=True))
    probb = prob.astype(BF)
    ax = dot(probb, xall).astype(BF)
    c0 = (head_fold(dot(ax, wqkv1[2])) + bias_ref[1:2, 1, :]).astype(BF)
    copies[10].wait()
    n10, r10 = normalize(x0 + dot(c0, wo1[...]) + bias_ref[2:3, 1, :])
    h10 = n10 * gain_ref[1, 0:1, :] + bias_ref[3:4, 1, :]
    h10b = h10.astype(BF)
    copies[11].wait()
    f0 = dot(h10b, w11[...]) + wb_ref[1:2, :]
    g0, dg0 = gelu_pair(f0)
    g0b = g0.astype(BF)
    copies[12].wait()
    n20, r20 = normalize(h10 + dot(g0b, w21[...]) + bias_ref[4:5, 1, :])
    x20 = n20 * gain_ref[1, 1:2, :] + bias_ref[5:6, 1, :]
    e0 = x20.astype(BF)
    copies[13].wait()
    rp = dot(e0, wp[...]) + pb_ref[...].reshape(1, D)
    rp_out[...] = rp
    squashed = jnp.tanh(rp)
    unit = squashed * lax.rsqrt(jnp.sum(squashed * squashed, -1, keepdims=True) + EPS_UNIT)
    row = lax.broadcasted_iota(jnp.int32, (S, 128), 0)
    lane = lax.broadcasted_iota(jnp.int32, (S, 128), 1)
    tail = jnp.zeros((S, 128), F32)
    for s in range(S):
        if s < PH:
            label = lab_ref[s]
            tail = jnp.where((row == s) & (lane == 0), (label // 32).astype(F32), tail)
            tail = jnp.where((row == s) & (lane == 1), (label % 32).astype(F32), tail)
        tail = jnp.where((row == s) & (lane == 2), tokens(s).astype(F32), tail)
    pay_out[...] = jnp.concatenate([unit, tail], 1).astype(BF)
    small_out[0] = n10
    small_out[1] = n20
    small_out[2] = jnp.broadcast_to(r10, n10.shape)
    small_out[3] = jnp.broadcast_to(r20, n10.shape)
    wide_out[...] = dg0
    big_out[:, 0:D] = c0
    big_out[:, D:2 * D] = x0b
    for i in range(cut.GX):
        lanes = slice(i * D // cut.GX, (i + 1) * D // cut.GX)
        factors[i] = jnp.concatenate([e0[:, lanes], h10b[:, lanes], g0b[:, i * FF // cut.GX:(i + 1) * FF // cut.GX]], 1)
    for r, out in enumerate(row_outs):
        out[...] = factors[place()[0] ^ r] if cut.GX > 1 else factors[0]
    a1_out[...] = probb
    ax_out[...] = ax
    qm_out[...] = qm
    qw_out[...] = qw
    for copy in stores:
        copy.wait()


def forward(cut, x, lengths, labels, wqkv, wo, w1, w2, wp, bias, gains, wb, pb):
    T, D = x.shape
    S = T // 64
    FF = w1.shape[2]
    nb = (S // 2) * (D // 128)
    sd = jax.ShapeDtypeStruct
    hbm = pl.BlockSpec(memory_space=pltpu.HBM)
    vm = pl.BlockSpec(memory_space=pltpu.VMEM)
    td = sd((T, D), BF)
    tr = sd((T, 128), F32)
    outs = [td, td, td, sd((nb, 128, 256), BF), td, tr, sd((T, FF), BF), td, tr, td,
            sd((4, S, D), F32), sd((S, 2 * D), BF), sd((H * S, T), BF), sd((H * S, D), BF),
            sd((H * S, D), BF), sd((H * S, D), BF), sd((S, FF), F32), sd((S, D), F32), sd((S, D + 128), BF)]
    outs += [sd((S, 6 * D // cut.GX), BF)] * cut.GX
    outs += [sd((7, T, D // cut.C), BF)] * cut.C
    out_specs = [hbm] * 10 + [vm] * (9 + cut.GX) + [hbm] * cut.C
    V = pltpu.VMEM
    b, r = V((T, D), BF), V((T, 128), F32)
    scratch = [b, V((3, D, D), BF), V((D, D), BF), V((D, FF), BF), V((FF, D), BF),
               V((3, D, D), BF), V((D, D), BF), V((D, FF), BF), V((FF, D), BF), V((D, D), BF),
               b, b, b, V((nb, 128, 256), BF), b, b, r, b, V((T, FF), BF), b, r, b,
               V((T, D), F32), V((T, D), F32), V((S, D), F32), V((cut.C, 7, T, D // cut.C), BF),
               V((cut.GX, S, 6 * D // cut.GX), BF),
               pltpu.SemaphoreType.DMA((14,)), pltpu.SemaphoreType.DMA((12,))]
    return pl.pallas_call(
        functools.partial(fwd_kernel, cut), out_shape=outs, out_specs=out_specs,
        in_specs=[pl.BlockSpec(memory_space=pltpu.SMEM)] * 2 + [hbm] * 6 + [vm] * 4,
        scratch_shapes=scratch, name="encode",
        compiler_params=pltpu.CompilerParams(vmem_limit_bytes=55 << 20),
    )(lengths, labels, x, wqkv, wo, w1, w2, wp, bias, gains, wb, pb)


HBM = pl.BlockSpec(memory_space=pltpu.HBM)
VM = pl.BlockSpec(memory_space=pltpu.VMEM)
SM = pl.BlockSpec(memory_space=pltpu.SMEM)


def norm_back(grad, n, root, gain):
    gn = grad * gain
    inner = jnp.mean(gn * n, -1, keepdims=True)
    return root * (gn - jnp.mean(gn, -1, keepdims=True) - n * inner)


def total_rows(values):
    return jnp.sum(values, 0, keepdims=True)


def runs(mode):
    return [(axis, mode.index(axis), mode.count(axis)) for axis in sorted(set(mode), reverse=True)]


def emit(cut, mode, parts, outs):
    if cut.C == 1:
        outs[0][...] = parts[0][...]
        return
    side = dict(zip("yx", place()[2:4]))
    for i, (axis, _, _) in enumerate(runs(mode)):
        bit = side[axis]
        outs[2 * i][...] = parts[i][bit]
        outs[2 * i + 1][...] = parts[i][1 - bit]


def pieces(cut, mode, rows, lanes):
    if cut.C == 1:
        return [pltpu.VMEM((1, 1, 1, rows, lanes), BF)], [sds((1, 1, 1, rows, lanes), BF)]
    scratch = [pltpu.VMEM((2, 2, n, rows, lanes), BF) for _, _, n in runs(mode)]
    return scratch, [sds((2, n, rows, lanes), BF) for _, _, n in runs(mode) for _ in range(2)]


def put(cut, mode, parts, y, x, z, value, rows=slice(None), lanes=slice(None)):
    if cut.C == 1:
        parts[0][0, 0, 0, rows, lanes] = value
        return
    for part, (axis, start, n) in zip(parts, runs(mode)):
        if start <= z < start + n:
            first, second = (y, x) if axis == "y" else (x, y)
            part[first, second, z - start, rows, lanes] = value


def start_all(pairs, sem):
    copies = [pltpu.make_async_copy(s, d, sem.at[i]) for i, (s, d) in enumerate(pairs)]
    for copy in copies:
        copy.start()
    return copies


def join(refs, out):
    out[...] = jnp.concatenate([ref[...].astype(F32) for ref in refs], 0).astype(BF)


def top_kernel(cut, PH, count, extra, gain_ref, *refs):
    local, (wqkv_hbm, wo_hbm, w1_hbm, w2_hbm, wp_hbm), rest = refs[:15], refs[15:20], refs[20:]
    bufs, rest = rest[-16:-1], rest[:-16] + rest[-1:]
    (own_ref, rp_ref, small_ref, big_ref, dg_ref, a1_ref, ax_ref, qm_ref, qw_ref, xb_ref, n2_ref, r2_ref,
     n1_ref, r1_ref, dg0_ref) = bufs
    early = start_all(list(zip(local, bufs)), rest[-1].at[pl.ds(7, 15)])
    gathered = rest[:count]
    join(rest[count:count + cut.GX], rest[count + extra])
    rest = rest[:count + extra] + rest[count + extra + 1:]
    (loss_out, tot_out, gy_out, vec_out, eb_out, gf_out, eb0_out, gz1_out, gc_out, vec2_out), rest = (
        rest[count + extra:count + extra + 10], rest[count + extra + 10:])
    (stay_out, go_out), rest = (rest[0], rest[1 if cut.C == 2 else 0]), rest[cut.C:]
    wqkv, wo, w1, w2, wp, gx, left_s, sem = rest
    D = wo.shape[0]
    FF = w1.shape[1]
    for copy in early[:12]:
        copy.wait()
    S = own_ref.shape[0]
    R = sum(g.shape[0] for g in gathered)
    T = xb_ref.shape[0]
    loads = [(wp_hbm, wp), (w2_hbm.at[1], w2), (w1_hbm.at[1], w1), (wo_hbm.at[1], wo)]
    for p in range(3):
        loads.append((wqkv_hbm.at[1, :, pl.ds(p * D, D)], wqkv.at[p]))
    copies = [pltpu.make_async_copy(s, d, sem.at[i]) for i, (s, d) in enumerate(loads)]
    for copy in copies:
        copy.start()
    gxi, gyi = place()[0], place()[5]
    me = gxi * lax.axis_size("gy") + gyi

    def device(j):
        r = j // S
        if cut.C == 1:
            return r
        flips = ((r // 8) % 2 * 2 + r // 16) * 8 + r % 4 * 2 + (r // 4) % 2
        return me ^ flips


    everyone = jnp.concatenate([g[...] for g in gathered], 0) if count > 1 else gathered[0][...]
    units = everyone[:, 0:D]
    extra = everyone[:, D:D + 128]
    i8 = lax.broadcasted_iota(jnp.int32, (8, 128), 0)
    l8 = lax.broadcasted_iota(jnp.int32, (8, 128), 1)
    pick = jnp.where((i8 == 0) & (l8 == 0), 32.0, 0.0) + jnp.where((i8 == 0) & (l8 == 1), 1.0, 0.0)
    pick = pick + jnp.where((i8 == 1) & (l8 == 2), 1.0, 0.0)
    meta = dot(pick.astype(BF), extra, NT)
    label_row = meta[0:1, :]
    tokens = jnp.sum(meta[1:2, :], 1, keepdims=True)
    tot_out[...] = jnp.broadcast_to(tokens, tot_out.shape)
    parts = []
    BLK = min(R, 256)
    for b in range(R // BLK):
        mat = SCORE * dot(units, units[b * BLK:(b + 1) * BLK, :], NT)
        j = lax.broadcasted_iota(jnp.int32, (R, BLK), 0)
        target = (j % S) >= PH
        pair = (device(j) * PH + (j % S) - PH).astype(F32)
        chosen = target & (pair == label_row[:, b * BLK:(b + 1) * BLK])
        logits = jnp.where(target, mat - jnp.where(chosen, SCORE * MARGIN, 0.0), -1e30)
        top = jnp.max(logits, 0, keepdims=True)
        parts.append(top + jnp.log(jnp.sum(jnp.exp(logits - top), 0, keepdims=True)))
    lse_row = jnp.concatenate(parts, 1) if len(parts) > 1 else parts[0]
    own_units = own_ref[:, 0:D]
    own_extra = own_ref[:, D:D + 128].astype(F32)
    own_label = 32.0 * own_extra[:, 0:1] + own_extra[:, 1:2]
    mat = SCORE * dot(own_units, units, NT)
    j = lax.broadcasted_iota(jnp.int32, (S, R), 1)
    r = lax.broadcasted_iota(jnp.int32, (S, R), 0)
    target = (j % S) >= PH
    pair = (device(j) * PH + (j % S) - PH).astype(F32)
    chosen = target & (pair == own_label)
    logits = jnp.where(target, mat - jnp.where(chosen, SCORE * MARGIN, 0.0), -1e30)
    top = jnp.max(logits, 1, keepdims=True)
    lse = top + jnp.log(jnp.sum(jnp.exp(logits - top), 1, keepdims=True))
    loss = lse - jnp.sum(jnp.where(chosen, logits, 0.0), 1, keepdims=True)
    loss_out[...] = jnp.broadcast_to(loss, loss_out.shape)
    from_source = jnp.where(target, jnp.exp(logits - lse), 0.0) - jnp.where(chosen, 1.0, 0.0)
    pair_own = (me * PH + r - PH).astype(F32)
    source = (j % S) < PH
    chosen_t = source & (label_row == pair_own)
    logits_t = mat - jnp.where(chosen_t, SCORE * MARGIN, 0.0)
    from_target = jnp.where(source, jnp.exp(jnp.where(source, logits_t - lse_row, 0.0)), 0.0)
    from_target = from_target - jnp.where(chosen_t, 1.0, 0.0)
    glog = jnp.where(r < PH, from_source, from_target).astype(BF)
    gu = SCORE * dot(glog, units)
    squashed = jnp.tanh(rp_ref[...])
    rs = lax.rsqrt(jnp.sum(squashed * squashed, -1, keepdims=True) + EPS_UNIT)
    gt = rs * (gu - squashed * (rs * rs * jnp.sum(gu * squashed, -1, keepdims=True)))
    gr = (gt * (1.0 - squashed * squashed)).astype(BF)
    copies[0].wait()
    gx2 = dot(gr, wp[...], NT)

    n1, n2, r1, r2 = small_ref[0], small_ref[1], small_ref[2], small_ref[3]
    gz2 = norm_back(gx2, n2, r2, gain_ref[1, 1:2, :])
    gy = gz2.astype(BF)
    copies[1].wait()
    gf = (dot(gy, w2[...], NT) * dg_ref[...]).astype(BF)
    again = [pltpu.make_async_copy(w2_hbm.at[0], w2, sem.at[22])]
    again[0].start()
    copies[2].wait()
    gh1 = gz2 + dot(gf, w1[...], NT)
    again.append(pltpu.make_async_copy(w1_hbm.at[0], w1, sem.at[23]))
    again[1].start()
    gz1 = norm_back(gh1, n1, r1, gain_ref[1, 0:1, :])
    go = gz1.astype(BF)
    copies[3].wait()
    gc = dot(go, wo[...], NT).astype(BF).astype(F32)
    again.append(pltpu.make_async_copy(wo_hbm.at[0], wo, sem.at[24]))
    again[2].start()
    gcm = head_rows(gc).astype(BF)
    for i in (4, 5, 6):
        copies[i].wait()
    gcw = dot(gcm, wqkv[2], NT).astype(BF)
    xall = xb_ref[...]
    prob = a1_ref[...].astype(F32)
    ga = dot(gcw, xall, NT)
    gs = (prob * (ga - jnp.sum(ga * prob, 1, keepdims=True))).astype(BF)
    mm = dot(gs, xall).astype(BF)
    gpq = head_fold(dot(mm, wqkv[1])).astype(BF).astype(F32) * SCALE
    gpqb = gpq.astype(BF)
    back = dot(jnp.concatenate([gs, a1_ref[...]], 0), jnp.concatenate([qw_ref[...], gcw], 0), TN)
    gx[...] = back
    first = gz1 + dot(gpqb, wqkv[0], NT)
    for s in range(S):
        gx[64 * s:64 * s + 1, :] += first[s:s + 1, :]

    nx = n2_ref[...].astype(F32)
    gxv = gx[...]
    gzx = norm_back(gxv, nx, r2_ref[:, 0:1], gain_ref[0, 1:2, :])
    gyx = gzx.astype(BF)
    gy_out[...] = gyx
    for copy in early[12:]:
        copy.wait()
    again[0].wait()
    again[1].wait()
    gx[...] = gzx

    def feed(i, _):
        cols = pl.ds(pl.multiple_of(i * D, D), D)
        part = (dot(gy_out[...], w2[cols, :], NT) * dg0_ref[:, cols].astype(F32)).astype(BF)
        gf_out[:, cols] = part
        eb0_out[0:1, cols] = total_rows(part.astype(F32))
        gx[...] += dot(part, w1[:, cols], NT)
        return 0

    lax.fori_loop(0, FF // D, feed, 0)
    gh = gx[...]
    n10 = n1_ref[...].astype(F32)
    gz10 = norm_back(gh, n10, r1_ref[:, 0:1], gain_ref[0, 0:1, :])
    gz1_out[...] = gz10
    go0 = gz10.astype(BF)
    gf_out[:, FF:] = go0
    vec2_out[0:1, :] = total_rows(gh)
    vec2_out[1:2, :] = total_rows(gh * n10)
    vec2_out[2:3, :] = total_rows(go0.astype(F32))
    vec2_out[3:8, :] = jnp.zeros((5, D), F32)
    again[2].wait()
    gc_out[...] = dot(go0, wo[...], NT).astype(BF)

    vec_out[0:1, :] = total_rows(gpqb.astype(F32))
    vec_out[1:2, :] = total_rows(gc)
    vec_out[2:3, :] = total_rows(go.astype(F32))
    vec_out[3:4, :] = total_rows(gh1)
    vec_out[4:5, :] = total_rows(gy.astype(F32))
    vec_out[5:6, :] = total_rows(gx2)
    vec_out[6:7, :] = total_rows(gh1 * n1)
    vec_out[7:8, :] = total_rows(gx2 * n2)
    vec_out[8:9, :] = total_rows(gr.astype(F32))
    vec_out[9:10, :] = total_rows(gxv)
    vec_out[10:11, :] = total_rows(gxv * nx)
    vec_out[11:12, :] = total_rows(gyx.astype(F32))
    vec_out[12:16, :] = jnp.zeros((4, D), F32)
    eb_out[...] = total_rows(gf.astype(F32))

    width = D // cut.GX
    cut_up = lambda v: [v[:, i * width:(i + 1) * width] for i in range(v.shape[1] // width)]
    c0, x0 = big_ref[:, 0:D].astype(F32), big_ref[:, D:2 * D].astype(F32)
    mmf, axf = mm.astype(F32), ax_ref[...].astype(F32)
    for g in range(cut.GX):
        lanes = slice(g * width, (g + 1) * width)
        blocks = [v[h * S:(h + 1) * S, lanes] for v in (mmf, axf) for h in range(H)]
        blocks += [x0[:, lanes], c0[:, lanes]]
        dst = g if cut.C == 1 else g ^ gxi
        for i, block in enumerate(blocks):
            left_s[dst, i] = block.astype(BF)
    q0 = head_fold(qm_ref[...].astype(F32))
    right = cut_up(gpq) + cut_up(q0) + cut_up(gc) + cut_up(go.astype(F32))
    grf, gyf, gff = gr.astype(F32), gy.astype(F32), gf.astype(F32)
    dn, df = D // cut.GY, FF // cut.GY
    for g in range(cut.GY):
        mix = jnp.concatenate([grf[:, g * dn:(g + 1) * dn], gyf[:, g * dn:(g + 1) * dn],
                               gff[:, g * df:(g + 1) * df]], 1)
        right += cut_up(mix)
    right = [block.astype(BF) for block in right]
    L = LEFT
    for out, base in (((stay_out, 0), (go_out, 2)) if cut.C == 2 else ((stay_out, 0),)):
        for r in range(cut.C):
            out[r * L:(r + 1) * L] = left_s[base + r]
        for i, block in enumerate(right):
            out[cut.C * L + i] = block


LEFT = 2 * H + 2


def params(mb):
    return pltpu.CompilerParams(vmem_limit_bytes=mb << 20)


def cost(weight=0.0):
    return pl.CostEstimate(flops=int(weight * UNIT), bytes_accessed=1, transcendentals=0)


UNIT = 10 ** 10
MODE = {2: "yyxx", 3: "yyyy", 4: "yyxx"}
LONG = 1000.0


def call(kernel, name, mb, outs, ins, hbm=(), smem=(), scratch=(), after=(), weight=0.0):
    hbm = [in_hbm(t) for t in hbm]
    return pl.pallas_call(
        functools.partial(kernel), out_shape=list(outs), name=name,
        in_specs=[SM] * len(smem) + [VM] * len(ins) + [HBM] * (len(hbm) + len(after)), out_specs=[VM] * len(outs),
        scratch_shapes=list(scratch), compiler_params=params(mb), cost_estimate=cost(weight),
    )(*smem, *ins, *hbm, *after)


def in_hbm(t):
    return pltpu.with_memory_space_constraint(t, pltpu.HBM)


def sds(shape, dtype):
    return jax.ShapeDtypeStruct(shape, dtype)


def top(cut, after, factors, gathered, own, rp, small, big, dg, a1, ax, qm, qw, xb, n2, r2, n1, r1, dg0, gains, wqkv, wo, w1, w2, wp):
    S = own.shape[0]
    T, D = xb.shape
    FF = w1.shape[2]
    width = D // cut.GX
    V = pltpu.VMEM
    count = cut.C * LEFT + 4 * cut.GX + (2 * D + FF) // width
    td = sds((T, D), BF)
    after = [*factors, *after]
    outs = [sds((S * cut.GX, factors[0].shape[1]), BF), sds((S, 128), F32), sds((8, 128), F32), td, sds((16, D), F32), sds((1, FF), F32), sds((T, FF + D), BF),
            sds((1, FF), F32), sds((T, D), F32), td, sds((8, D), F32)] + [sds((count, S, width), BF)] * cut.C
    local = (own, rp, small, big, dg, a1, ax, qm, qw, xb, n2, r2, n1, r1, dg0)
    bufs = [V(t.shape, t.dtype) for t in local]
    return pl.pallas_call(
        functools.partial(top_kernel, cut, S // 2, len(gathered), len(after)), out_shape=outs,
        in_specs=[VM] + [HBM] * 20 + [VM] * (len(gathered) + cut.GX) + [HBM] * (len(after) - cut.GX), out_specs=[VM] * len(outs),
        scratch_shapes=[V((3, D, D), BF), V((D, D), BF), V((D, FF), BF), V((FF, D), BF), V((D, D), BF),
                        V((T, D), F32), V((cut.GX, LEFT, S, width), BF), *bufs, pltpu.SemaphoreType.DMA((25,))],
        name="rank_and_top_back", compiler_params=params(44 if cut.C == 2 else 58), cost_estimate=cost(),
    )(gains, *(in_hbm(t) for t in (*local, wqkv, wo, w1, w2, wp)), *gathered, *after)


def peers_of(cut, refs):
    L = LEFT
    if cut.C == 1:
        return [(refs[0], 0, L)]
    stay, got_y, got_c = refs
    n = stay.shape[0] - 2 * L
    return [(stay, 0, 2 * L), (got_y, 0, 2 * L), (got_c, 0, 2 * L), (got_c, L, 2 * L + n)]


def top_weights_kernel(cut, S, count, *refs):
    peers = peers_of(cut, refs[:count])
    outs = refs[count:]
    sides = cut.X
    chunks, part, stage = outs[:sides], outs[-2], outs[-1]
    xbit = place()[3] if sides == 2 else 0
    width = refs[0].shape[2]
    D = width * cut.GX
    G = cut.GX
    get = lambda ref, i: ref[i].astype(F32)
    lane_cat = lambda ref, i, m: jnp.concatenate([get(ref, i + k) for k in range(m)], 1) if m > 1 else get(ref, i)
    rights = [[lane_cat(ref, ro + k * G, G) for k in range(4)] for ref, lo, ro in peers]
    low = lax.broadcasted_iota(jnp.int32, (S, 128), 1) < HD
    stack = lambda pieces: jnp.concatenate(pieces, 0).astype(BF)
    cols = [dot(stack([get(ref, lo + 2 * H) for ref, lo, ro in peers]), stack([r[0] for r in rights]), TN)]
    for kind in range(2):
        for j in range(D // 128):
            lhs, rhs = [], []
            for (ref, lo, ro), r in zip(peers, rights):
                lhs += [get(ref, lo + kind * H + 2 * j), get(ref, lo + kind * H + 2 * j + 1)]
                blk = r[kind + 1][:, 128 * j:128 * j + 128]
                rhs += [jnp.where(low, blk, 0.0), jnp.where(low, 0.0, blk)]
            cols.append(dot(stack(lhs), stack(rhs), TN))
    qkv = jnp.concatenate(cols, 1)
    out = dot(stack([get(ref, lo + 2 * H + 1) for ref, lo, ro in peers]), stack([r[3] for r in rights]), TN)
    wa, wb = 3 * D // cut.GY, D // cut.GY
    halves = []
    for x in range(sides):
        blocks = []
        for z in range(cut.Z):
            b = z * sides + x
            blocks.append(jnp.concatenate(
                [qkv[:, b * wa:(b + 1) * wa], out[:, b * wb:(b + 1) * wb]], 1).astype(BF))
        halves.append(blocks)
    for z in range(cut.Z):
        for x in range(sides):
            part[x, z] = halves[x][z]
    for r, dst in enumerate(chunks):
        for z in range(cut.Z):
            dst[z * width:(z + 1) * width, :] = part[xbit ^ r, z] if sides == 2 else part[0, z]
    m = (2 * D + 4 * D) // cut.GY // width
    if sides == 1:
        ref, lo, ro = peers[0]
        outs[1][...] = ref[ro + 4 * G:ro + 4 * G + m]
        return
    n = cut.Z * width
    for r, dst in enumerate(chunks):
        x = xbit ^ r
        for p, (ref, lo, ro) in enumerate(peers):
            lanes = slice(p % 2 * width, (p % 2 + 1) * width)
            for z in range(cut.Z):
                for i in range(m):
                    to = n + ((z * 2 + p // 2) * m + i) * S
                    piece = ref[pl.ds(ro + 4 * G + (z * sides + x) * m + i, 1)]
                    stage[to - n:to - n + S, lanes] = piece[0].astype(F32)
        dst[n:, :] = stage[...].astype(BF)


def top_weights(cut, arrays, left=(), after=()):
    S, width = arrays[0].shape[1:]
    D = width * cut.GX
    peers = 4 if cut.C == 2 else 1
    m = 6 * D // cut.GY // width
    lanes = 4 * D // cut.GY
    extra = cut.Z * (peers // 2) * m * S
    outs = [sds((cut.Z * width + extra, lanes), BF)] * cut.X
    if cut.C == 1:
        outs.append(sds((m, S, width), BF))
    n = len(arrays)
    if cut.C == 2:
        outs.append(sds((2 * left[0].shape[0], left[0].shape[1]), BF))

    def kernel(*refs):
        ins, (left_a, left_b), refs = refs[:n], refs[n:n + 2] if left else (None, None), refs[n + len(left) + len(after):]
        if left:
            refs[cut.X][0:left_a.shape[0], :] = left_a[...]
            refs[cut.X][left_a.shape[0]:, :] = left_b[...]
            refs = refs[:cut.X] + refs[cut.X + 1:]
        top_weights_kernel(cut, S, n, *ins, *refs)

    return call(kernel, "top_weights", 20, outs, [*arrays, *left], after=after,
                scratch=[pltpu.VMEM((cut.X, cut.Z, width, lanes), BF), pltpu.VMEM((max(extra, 8), lanes), F32)], weight=LONG)


def pack_kernel(stay, got, left_a, left_b, *rest):
    out, left_out = rest[-2:]
    left_out[0:left_a.shape[0], :] = left_a[...]
    left_out[left_a.shape[0]:, :] = left_b[...]
    L = LEFT
    n = stay.shape[0] - 2 * L
    for src, lo, dst, m in ((stay, L, 0, L), (got, L, L, L), (stay, 2 * L, 2 * L, n), (got, 2 * L, 2 * L + n, n)):
        out[dst:dst + m] = src[lo:lo + m]


def pack(stay, got, left, left_got, after=()):
    n = 2 * (stay.shape[0] - LEFT)
    outs = [sds((n,) + stay.shape[1:], BF), sds((2 * left.shape[0], left.shape[1]), BF)]
    return call(pack_kernel, "pack", 8, outs, (stay, got, left, left_got), after=after)


def row_weights_kernel(cut, lefts, rights, pool_out, expand_out, reduce_out):
    dk = lefts[0].shape[-1] // 6
    D = dk * cut.GX
    dn = D // cut.GY
    if cut.C == 2:
        rows = []
        for d in range(4):
            ref, base = rights[d // 2], (0, dk)[d // 2]
            for s in range(2):
                for p in range(4):
                    at = base + d % 2 * 96 + s * 48 + p // 2 * 24
                    lanes = slice(p % 2 * dk, (p % 2 + 1) * dk)
                    rows.append(jnp.concatenate([ref[at + 8 * i:at + 8 * i + 8, lanes].astype(F32) for i in range(3)], 1))
        own, got = lefts
        n, lanes = own.shape[0], got.shape[1]
        blocks = [got[got.shape[0] - (3 - i) * n:got.shape[0] - (2 - i) * n, :] for i in range(3)]
        right = jnp.concatenate(rows, 0).astype(BF)
        near = jnp.concatenate([b.astype(F32) for b in blocks], 1).astype(BF)
        h = n // 2
        left = jnp.concatenate([own[0:h, :], near[0:h, :], own[h:, :], near[h:, :]], 0)
    else:
        left = lefts[0][...]
        right = jnp.concatenate([rights[0][i] for i in range(rights[0].shape[0])], 1)
    pool_out[...] = dot(left[:, 0:dk], right[:, 0:dn], TN)
    expand_out[...] = dot(left[:, dk:2 * dk], right[:, 2 * dn:], TN)
    reduce_out[...] = dot(right[:, dn:2 * dn], left[:, 2 * dk:], TN)


def row_weights(cut, lefts, rights, after=()):
    dk = lefts[0].shape[-1] // 6
    dn = dk * cut.GX // cut.GY
    outs = [sds((dk, dn), F32), sds((dk, 4 * dn), F32), sds((dn, 4 * dk), F32)]
    m, n = len(lefts), len(lefts) + len(rights)
    kernel = lambda *refs: row_weights_kernel(cut, refs[:m], refs[m:n], *refs[n + len(after):])
    return call(kernel, "row_weights", 32, outs, (*lefts, *rights), after=after)


def narrow_weight_kernel(cut, *refs):
    C = cut.C
    mode = MODE[2]
    m = 2 * C + (2 * len(runs(mode)) if C == 2 else 1)
    gys, acts, outs, parts, turned = refs[:C], refs[C:2 * C], refs[2 * C:m], refs[m:-1], refs[-1]
    T, D = acts[0].shape[1], acts[0].shape[2] * C
    nw = D // cut.GY
    width = D // C
    for c in range(C):
        turned[c] = gys[c][...].T

    def weigh(b, _):
        res = dot(turned[0], acts[0][b])
        for c in range(1, C):
            res = res + dot(turned[c], acts[c][b])
        res = res.astype(BF)
        for x in range(cut.X):
            for z in range(cut.Z):
                g = z * cut.X + x
                value = res[g * nw:(g + 1) * nw, :]
                if C == 1:
                    put(cut, mode, parts, 0, x, z, value, lanes=pl.ds(pl.multiple_of(b * width, 128), width))
                else:
                    put(cut, mode, parts, b // 2, x, z, value, pl.ds(pl.multiple_of(b % 2 * nw, 16), nw))
        return 0

    lax.fori_loop(0, 4, weigh, 0)
    emit(cut, mode, parts, outs)


def narrow_weight(cut, gys, acts, after=()):
    D = acts[0].shape[2] * cut.C
    scratch, outs = pieces(cut, MODE[2], cut.C * D // cut.GY, 4 * D // cut.GX // cut.C)
    n = 2 * cut.C
    kernel = lambda *refs: narrow_weight_kernel(cut, *refs[:n], *refs[n + len(after):])
    return call(kernel, "narrowing_weight", 24, outs, (*gys, *acts), after=after,
                scratch=scratch + [pltpu.VMEM((cut.C, D, gys[0].shape[0]), BF)])


def widen_weight_kernel(cut, *refs):
    C = cut.C
    mode = MODE[3]
    m = 2 * C + (2 * len(runs(mode)) if C == 2 else 1)
    acts, gfs, outs, parts = refs[:C], refs[C:2 * C], refs[2 * C:m], refs[m:]
    width = acts[0].shape[2]
    D = width * C
    FF = gfs[0].shape[1] - D
    lw, kr = FF // cut.GY, D // cut.GX
    left = [a[4].T for a in acts]
    W = D
    for i in range(FF // W):
        res = dot(left[0], gfs[0][:, i * W:(i + 1) * W])
        for c in range(1, C):
            res = res + dot(left[c], gfs[c][:, i * W:(i + 1) * W])
        res = res.astype(BF)
        if C == 1:
            put(cut, mode, parts, 0, 0, 0, res, lanes=slice(i * W, (i + 1) * W))
            continue
        for h in range(W // lw):
            g = i * W // lw + h
            for y in range(cut.Y):
                put(cut, mode, parts, y, g % cut.X, g // cut.X, res[y * kr:(y + 1) * kr, h * lw:(h + 1) * lw])
    emit(cut, mode, parts, outs)


def widen_weight_back(cut, acts, gfs, after=()):
    D = acts[0].shape[2] * cut.C
    FF = gfs[0].shape[1] - D
    scratch, outs = pieces(cut, MODE[3], D // cut.GX, FF // cut.GY)
    n = 2 * cut.C
    kernel = lambda *refs: widen_weight_kernel(cut, *refs[:n], *refs[n + len(after):])
    return call(kernel, "widening_weight", 24, outs, (*acts, *gfs), after=after, scratch=scratch)


def attend_kernel(extra, gc, q, k, v, a, vec1, vec2, eb0, eb1, *rest):
    gp = rest[-1]
    T, D = q.shape
    S = T // 64
    lane = lax.broadcasted_iota(jnp.int32, (128, 128), 1)
    low = lane < HD
    NB = D // 128

    def heads(p, _):
        rows = pl.ds(pl.multiple_of(p * 128, 128), 128)
        for j in range(NB):
            lanes = slice(128 * j, 128 * j + 128)
            gcj = gc[rows, lanes]
            gcm = jnp.concatenate([jnp.where(low, gcj, 0), jnp.where(low, 0, gcj)], 0)
            qj = q[rows, lanes]
            qm = jnp.concatenate([jnp.where(low, qj, 0), jnp.where(low, 0, qj)], 0)
            pb = a[p * NB + j]
            prob = pb.astype(F32)
            gp[rows, 2 * D + 128 * j:2 * D + 128 * j + 128] = dot(pb, gcm).astype(BF)
            ga = dot(v[rows, lanes], gcm, NT)
            gs = (prob * (ga - jnp.sum(ga * prob, 0, keepdims=True))).astype(BF)
            gp[rows, D + 128 * j:D + 128 * j + 128] = dot(gs, qm).astype(BF)
            gq = dot(gs, k[rows, lanes], TN)
            gq = jnp.where(low, gq[:128], gq[128:]).astype(BF)
            gp[rows, lanes] = (gq.astype(F32) * SCALE).astype(BF)
        return 0

    lax.fori_loop(0, S // 2, heads, 0)
    one = lambda ref, i: ref[i:i + 1, :]
    vecs = [total_rows(gp[0:T, 0:D].astype(F32)), total_rows(gp[0:T, 2 * D:3 * D].astype(F32)),
            one(vec2, 2), one(vec2, 0), one(vec1, 11), one(vec1, 9)]
    vecs += [one(vec1, i) for i in range(6)] + [one(vec2, 1), one(vec1, 10), one(vec1, 6), one(vec1, 7), one(vec1, 8)]
    vecs += [jnp.zeros((1, D), F32)] * (32 - len(vecs))
    gp[T:T + 16, :] = jnp.zeros((16, 3 * D), BF)
    block = jnp.concatenate([jnp.concatenate(vecs[8 * i:8 * i + 8], 0) for i in range(3)], 1)
    wide = jnp.concatenate([eb[:, i * D:(i + 1) * D] for eb in (eb0, eb1) for i in range(4)], 0)
    wide = jnp.concatenate([wide, jnp.zeros((8, 2 * D), F32)], 1)
    gp[T:T + 16, :] = jnp.concatenate([block, wide], 0).astype(BF)


def attend_back(gc, q, k, v, a, vectors, after=()):
    T, D = gc.shape
    return call(functools.partial(attend_kernel, len(after)), "attention_back", 30,
                [sds((T + 16, 3 * D), BF)], (gc, q, k, v, a, *vectors), after=after, weight=LONG)


def acts_width(ref, C):
    return ref.shape[2] * C


class Lanes:
    def __init__(self, refs):
        self.refs, self.rows, self.width = refs, refs[0].shape[0], refs[0].shape[1]

    def get(self, rows, start, stop):
        w = self.width
        found = [self.refs[i][rows, max(start - i * w, 0):min(stop - i * w, w)]
                 for i in range(start // w, (stop + w - 1) // w)]
        return jnp.concatenate(found, 1) if len(found) > 1 else found[0]


def attend_weight_kernel(cut, *refs):
    C = cut.C
    mode = MODE[4]
    n = 1
    acts, gos, gps = refs[:C], refs[C:2 * C], [Lanes(refs[2 * C + c * n:2 * C + (c + 1) * n]) for c in range(C)]
    refs = refs[2 * C + C * n:]
    m = 2 * len(runs(mode)) if C == 2 else 1
    outs, parts, blocks = refs[:m], refs[m:-1], refs[-1]
    width = acts[0].shape[2]
    D = width * C
    T = gps[0].rows - 16
    ct = [a[5].T for a in acts]
    xt = [a[6].T for a in acts]
    wa, wb = 3 * D // cut.GY, D // cut.GY
    main = wa // 128 * 128
    tail = wa - main
    kr = D // cut.GX

    def place_rows(res, x, z, lanes):
        res = res.astype(BF)
        for y in range(cut.Y):
            put(cut, mode, parts, y, x, z, res[y * kr:(y + 1) * kr, :], slice(0, kr), lanes)

    both = lambda f: f(0) + f(1) if C == 2 else f(0)
    if cut.GY == 1:
        place_rows(dot(xt[0], gps[0].get(slice(0, T), 0, 3 * D)), 0, 0, slice(0, 3 * D))
        place_rows(dot(ct[0], gos[0][:, 4 * D:]), 0, 0, slice(3 * D, None))
        emit(cut, mode, parts, outs)
        return
    for x in range(cut.X):
        for z in range(cut.Z):
            a0 = (z * cut.X + x) * wa
            place_rows(both(lambda c: dot(xt[c], gps[c].get(slice(0, T), a0, a0 + main))), x, z, slice(0, main))
    order = [(x, z) for x in range(cut.X) for z in range(cut.Z)]
    for i in range(0, len(order), 2):
        def tails(c):
            ra, rb = [], []
            for x, z in order[i:i + 2]:
                g = z * cut.X + x
                a0, o0 = g * wa, 4 * D + g * wb
                ra += [gps[c].get(slice(0, T), a0 + main, a0 + wa), jnp.zeros((T, 128 - tail), BF)]
                rb += [jnp.zeros((T, tail), BF), gos[c][:, o0:o0 + wb]]
            return dot(xt[c], jnp.concatenate(ra, 1)) + dot(ct[c], jnp.concatenate(rb, 1))
        res = both(tails)
        for m, (x, z) in enumerate(order[i:i + 2]):
            place_rows(res[:, 128 * m:128 * m + 128], x, z, slice(main, wa + wb))
    core = place()[1]
    vec = both(lambda c: gps[c].get(slice(T, T + 16), 0, 3 * D).astype(F32))
    n = 4 * 8
    dv, dw = D // n, 4 * D // n
    for d in range(n):
        pieces = [vec[0:8, k * D + d * dv:k * D + (d + 1) * dv] for k in range(3)]
        row, at = d * dw // D, d * dw % D
        pieces += [jnp.zeros((8, 128 - 3 * dv), F32), vec[8 + row:9 + row, at:at + dw], vec[12 + row:13 + row, at:at + dw]]
        pieces[-2:] = [jnp.concatenate(pieces[-2:] + [jnp.zeros((6, dw), F32)], 0),
                       jnp.zeros((8, wa + wb - 128 - dw), F32)]
        blocks[d] = jnp.concatenate([jnp.concatenate(pieces, 1), jnp.zeros((8, wa + wb), F32)], 0).astype(BF)
    for y in range(cut.Y):
        for x in range(cut.X):
            for z in range(cut.Z):
                put(cut, mode, parts, y, x, z, blocks[(2 * y + core) * 8 + z * cut.X + x], slice(kr, kr + 16))
    emit(cut, mode, parts, outs)


def attend_weight(cut, acts, gyos, gps, after=()):
    D = acts[0].shape[2] * cut.C
    D4 = 4 * D
    kr = D // cut.GX + (16 if cut.C == 2 else 0)
    scratch, outs = pieces(cut, MODE[4], kr, D4 // cut.GY)
    ins = [*acts, *gyos, *(part for parts in gps for part in parts)]
    n = len(ins)
    kernel = lambda *refs: attend_weight_kernel(cut, *refs[:n], *refs[n + len(after):])
    return call(kernel, "attention_weight", 30, outs, ins, after=after,
                scratch=scratch + [pltpu.VMEM((32, 16, D4 // cut.GY), BF)])


def input_kernel(pairs, extra, len_ref, tot_ref, gz_ref, *rest):
    n = 1
    gp, w_hbm, (gx_out, sc_out, w, sem) = Lanes(rest[:n]), rest[n], rest[n + 1 + extra:]
    T, D = gz_ref.shape
    PH = len_ref.shape[1]
    copies = start_all([(w_hbm.at[0, :, pl.ds(i * D, D)], w.at[i]) for i in range(3)], sem)
    for copy in copies:
        copy.wait()
    gx_out[...] = gz_ref[...]

    def project(i, _):
        gx_out[...] += dot(gp.refs[0][0:T, pl.ds(pl.multiple_of(i * D, D), D)], w[i], NT)
        return 0

    lax.fori_loop(0, 3, project, 0)
    inverse = 1.0 / tot_ref[0:1, 0:1]
    for s in range(T // 64):
        rows = slice(64 * s, 64 * s + 64)
        factor = (2.0 * pairs) * len_ref[s // PH, s % PH].astype(F32) * inverse
        sc_out[rows, :] = gx_out[rows, :] * factor


def input_back(pairs, lengths, tot, gz1, gp, wqkv, after=()):
    T, D = gz1.shape
    return call(functools.partial(input_kernel, pairs, len(after)), "input_back", 24, [sds((T, D), F32)] * 2,
                (tot, gz1, *gp), (wqkv,), (lengths,),
                scratch=[pltpu.VMEM((3, D, D), BF), pltpu.SemaphoreType.DMA((3,))], after=after, weight=LONG)


def plus(a, b):
    return (a.astype(F32) + b.astype(F32)).astype(BF)


def flip(values, axis, bits):
    return lax.ppermute(values, axis, [(i, i ^ bits) for i in range(lax.axis_size(axis))])


def fold_kernel(mode, extra, *refs):
    n = 2 * len(runs(mode))
    ins, outs = refs[:n], refs[n + extra:]
    side = dict(zip("yx", place()[2:4]))
    for i, (axis, _, _) in enumerate(runs(mode)):
        bit = side["x" if axis == "y" else "y"]
        keep, got = ins[2 * i:2 * i + 2]
        mine, other = outs[2 * i:2 * i + 2]
        other[...] = plus(keep[1 - bit], got[1 - bit])
        mine[...] = plus(keep[bit], got[bit])


def spread_kernel(mode, extra, *refs):
    n = 2 * len(runs(mode))
    ins, left, (keep_out, send_out, total) = refs[:n], refs[n], refs[n + 1 + extra:]
    low = lax.rem(place()[4], 2)
    for i, (_, start, count) in enumerate(runs(mode)):
        total[start:start + count] = plus(ins[2 * i][...], ins[2 * i + 1][...])
    rows, lanes = total.shape[1:]
    for dst, parity in ((send_out, 1 - low), (keep_out, low)):
        for high in range(2):
            dst[high * rows:(high + 1) * rows] = total[high * 2 + parity]
    m = left.shape[0]
    for i in range(left.shape[1] // lanes):
        send_out[2 * rows + i * m:2 * rows + (i + 1) * m] = left[:, i * lanes:(i + 1) * lanes]


def spread(mode, ins, left, after=()):
    rows, lanes = ins[0].shape[-2:]
    keep, send = call(functools.partial(spread_kernel, mode, len(after)), "spread", 16,
                      [sds((2 * rows, lanes), BF), sds((2 * rows + left.size // lanes, lanes), BF)], [*ins, left],
                      after=after, scratch=[pltpu.VMEM((4, rows, lanes), BF)])
    return keep, flip(send, "gy", 2), send


def spread_rows_kernel(extra, kr, keep, got, *rest):
    keep_out, send_out = rest[extra:]
    low = lax.rem(place()[4], 2)
    m = (keep.shape[0] - 4 * kr) // 4
    for dst, parity in ((send_out, 1 - low), (keep_out, low)):
        for high in range(2):
            z = high * 2 + parity
            at = high * (kr + 2 * m)
            rows = pl.ds(pl.multiple_of(z * kr, 16), kr)
            dst[at:at + kr] = plus(keep[rows, :], got[rows, :])
            rows = pl.ds(pl.multiple_of(4 * kr + z * m, 16), m)
            dst[at + kr:at + kr + m] = keep[rows, :]
            dst[at + kr + m:at + kr + 2 * m] = got[rows, :]


def spread_rows(keep, got, kr, after=()):
    shape = sds((2 * kr + keep.shape[0] - 4 * kr, keep.shape[1]), BF)
    keep, send = call(functools.partial(spread_rows_kernel, len(after), kr), "spread_rows", 16, [shape] * 2,
                      (keep, got), after=after)
    return keep, flip(send, "gy", 2), send


def settle_two_kernel(extra, kr, keep, got, keep2, got2, *rest):
    own_out, rows_out, own2_out, send_out = rest[extra:]
    high = lax.div(place()[4], 2)
    n = keep.shape[0] // 2
    m = n - kr
    part = lambda ref, h, start, size: ref[pl.ds(pl.multiple_of(h * n + start, 16), size), :]
    send_out[0:kr] = plus(part(keep, 1 - high, 0, kr), part(got, 1 - high, 0, kr))
    own_out[...] = part(keep, high, 0, kr).astype(F32) + part(got, high, 0, kr).astype(F32)
    for i, src in enumerate((keep, got)):
        send_out[kr + i * m:kr + (i + 1) * m] = part(src, 1 - high, kr, m)
        rows_out[i * m:(i + 1) * m] = part(src, high, kr, m)
    r2 = keep2.shape[0] // 2
    two = lambda ref, h: ref[pl.ds(pl.multiple_of(h * r2, 16), r2), :]
    send_out[kr + 2 * m:] = plus(two(keep2, 1 - high), two(got2, 1 - high))
    own2_out[...] = two(keep2, high).astype(F32) + two(got2, high).astype(F32)


def settle_two(keep, got, keep2, got2, kr, after=()):
    lanes, m = keep.shape[1], keep.shape[0] - 2 * kr
    r2 = keep2.shape[0] // 2
    outs = [sds((kr, lanes), F32), sds((m, lanes), BF), sds((r2, lanes), F32), sds((kr + m + r2, lanes), BF)]
    own, rows, own2, send = call(functools.partial(settle_two_kernel, len(after), kr), "settle_two", 16, outs,
                                 (keep, got, keep2, got2), after=after, weight=0.1)
    return own, rows, own2, flip(send, "gy", 4)


def spread_two_kernel(modes, extra, *refs):
    count = [2 * len(runs(mode)) for mode in modes]
    ins, outs = refs[:sum(count)], refs[sum(count) + extra:]
    low = lax.rem(place()[4], 2)
    for k, mode in enumerate(modes):
        keep_out, send_out, total = outs[2 * k], outs[2 * k + 1], outs[4 + k]
        for i, (_, start, n) in enumerate(runs(mode)):
            total[start:start + n] = plus(ins[2 * i][...], ins[2 * i + 1][...])
        ins = ins[2 * len(runs(mode)):]
        for dst, parity in ((send_out, 1 - low), (keep_out, low)):
            for high in range(2):
                dst[high] = total[high * 2 + parity]


def spread_two(first, second, after=()):
    ins = [first.operands(), second.operands()]
    tails = [t[0].shape[-2:] for t in ins]
    outs = call(functools.partial(spread_two_kernel, (first.mode, second.mode), len(after)), "spread_two", 16,
                [sds((2,) + t, BF) for t in tails for _ in range(2)], ins[0] + ins[1], after=after,
                scratch=[pltpu.VMEM((4,) + t, BF) for t in tails])
    return [outs[0], flip(outs[1], "gy", 2), outs[2], flip(outs[3], "gy", 2)], outs[1]


def settle_last_kernel(extra, keep3, got3, keep4, got4, *rest):
    own_out, send_out = rest[extra:]
    high = lax.div(place()[4], 2)
    n = keep3.shape[1]
    for keep, got, rows in ((keep3, got3, slice(0, n)), (keep4, got4, slice(n, None))):
        send_out[rows, :] = plus(keep[1 - high], got[1 - high])
        own_out[rows, :] = keep[high].astype(F32) + got[high].astype(F32)


def settle_last(ins, after=()):
    shape = (ins[0].shape[1] + ins[2].shape[1], ins[0].shape[2])
    own, send = call(functools.partial(settle_last_kernel, len(after)), "settle_last", 16,
                     [sds(shape, F32), sds(shape, BF)], ins, after=after)
    return own, flip(send, "gy", 4), send


def cross(values, axis):
    return flip(values, "gy", 1) if axis == "x" else flip(values, "gx", 2)


class Share:
    def __init__(self, chunk, mode):
        self.mode = mode
        self.keep = chunk[0::2]
        self.got = [cross(t, axis) for t, (axis, _, _) in zip(chunk[1::2], runs(mode))]

    def operands(self):
        return [t for pair in zip(self.keep, self.got) for t in pair]

    def fold(self, *after):
        outs = call(functools.partial(fold_kernel, self.mode, len(after)), "fold", 16,
                    [sds(t.shape[1:], BF) for t in self.keep for _ in range(2)], self.operands(), after=after)
        self.keep = outs[0::2]
        self.got = [cross(t, "x" if axis == "y" else "y") for t, (axis, _, _) in zip(outs[1::2], runs(self.mode))]
        return outs[1]

    def spread(self, left, *after):
        return spread(self.mode, self.operands(), left, after)


def finish_wide_kernel(own2, got12, own34, got34, r1, e1, reduce_out, expand_out):
    n = own2.shape[0]
    two = own2[...] + got12[got12.shape[0] - n:, :].astype(F32)
    reduce_out[0] = jnp.concatenate([two[0:n // 2], two[n // 2:]], 1)
    reduce_out[1] = r1[...]
    expand_out[0] = own34[0:n, :] + got34[0:n, :].astype(F32)
    expand_out[1] = e1[...]


def finish_kernel(wa, own1, own2, got12, own34, got34, r1, e1, reduce_out, expand_out, *outs):
    finish_wide_kernel(own2, got12, own34, got34, r1, e1, reduce_out, expand_out)
    finish_attend_kernel(wa, own34, got34, own1, got12, *outs)


def finish_attend_kernel(wa, own34, got34, own1, got12, *outs):
    attend_out, output_out, bias_out, gains_out, wb_out, pb_out = outs
    kr = own1.shape[0]
    a, b = own34[kr:, :] + got34[kr:, :].astype(F32), own1[...] + got12[0:kr, :].astype(F32)
    for layer, v in enumerate((a[0:kr], b)):
        attend_out[layer] = v[:, 0:wa]
        output_out[layer] = v[:, wa:]
    vec = a[kr:kr + 8, :]
    dv = bias_out.shape[2]
    one = lambda i: vec[i % 8:i % 8 + 1, i // 8 * dv:i // 8 * dv + dv]
    for layer in range(2):
        for i in range(6):
            bias_out[i, layer:layer + 1, :] = one(6 * layer + i)
        for i in range(2):
            gains_out[layer, i:i + 1, :] = one(12 + 2 * layer + i)
    wb_out[...] = vec[0:2, 128:128 + 4 * dv]
    pb_out[...] = one(16)


def scatter(values, row_axis, col_axis):
    part = lax.psum_scatter(values.astype(BF), row_axis, scatter_dimension=0, tiled=True)
    return lax.psum_scatter(part, col_axis, scatter_dimension=1, tiled=True).astype(F32)


def shards(mesh, inputs, lengths, labels, wqkv, wo, w1, w2, bias, gains, wb, wp, pb):
    GX, GY = mesh.shape["gx"], mesh.shape["gy"]
    n = GX * GY
    near = (GX, GY) == (4, 8)
    cut = Cut(2, 2, 2, 4) if near else Cut(1, 1, 1, 1)
    PH = labels.shape[0]
    S = 2 * PH
    L, D = inputs.shape[2], inputs.shape[3]
    T = S * L
    FF = w1.shape[2]
    twin = lambda v: [v, flip(v, "gx", 1)] if near else [v]
    x = inputs.reshape(T, D)
    (q, k, v, a, n1, r1, dg, n2, r2, xb, small, big, a1, ax, qm, qw, dg1, rp, own, *rest) = forward(
        cut, x, lengths, labels, wqkv, wo, w1, w2, wp, bias.transpose(1, 0, 2), gains, wb, pb)
    factors, acts = rest[:cut.GX], rest[cut.GX:]
    if near:
        factors = [flip(factors[r], "gx", r) if r else factors[0] for r in (0, 2, 1, 3)]
        line = jnp.concatenate([own] + [flip(own, "gy", 2 * d) for d in (1, 2, 3)], 0)
        corner = lax.ppermute(line, ("gx", "gy"), [(i, i ^ 17) for i in range(n)])
        plane = jnp.concatenate([line, flip(line, "gy", 1), flip(line, "gx", 2), corner], 0)
        gathered = [plane, flip(plane, "gx", 1)]
        acts = [acts[0], flip(acts[1], "gx", 1)]
    else:
        gathered = [lax.all_gather(own, ("gx", "gy"), axis=0, tiled=True)]
    left, loss, tot, gy, vec1, eb1, gfo, eb0, gz1, gc, vec2, *rows = top(
        cut, acts[1:], factors, gathered, own, rp, small, big, dg1, a1, ax, qm, qw, xb, n2, r2, n1, r1, dg, gains, wqkv, wo, w1, w2, wp)
    gfs, vectors = twin(gfo), (vec1, vec2, eb0, eb1)
    shape = (2, PH, L, D)
    wa = 3 * D // GY
    gys = twin(gy)
    if near:
        stay, go_y = rows
        got_y = cross(go_y, "y")
        ch2 = narrow_weight(cut, gys, acts)
        s2 = Share(ch2, MODE[2])
        gp = attend_back(gc, q, k, v, a, vectors, (ch2[0],))
        gps = twin(gp[0])
        packed, left = pack(stay, got_y, left, cross(left, "x"), (gp[0],))
        t = s2.fold(packed)
        ch3 = widen_weight_back(cut, acts, gfs, (t,))
        s3 = Share(ch3, MODE[3])
        ch1 = top_weights(cut, [stay, got_y, flip(packed, "gx", 1)], (left, flip(left, "gy", 4)), (ch3[0], *s2.got))
        got1 = cross(ch1[1], "x")
        keep2, got2, t = s2.spread(ch1[2], ch1[0])
        left = [ch1[2], got2]
        ch4 = attend_weight(cut, acts, gfs, [[t] for t in gps], (t,))
        s4 = Share(ch4, MODE[4])
        kr, dn, dv = D // GX, D // GY, D // n
        keep1, got1, t = spread_rows(ch1[0], got1, kr, (ch4[0],))
        t = s3.fold(t, got2)
        own1, rows1, own2, got12 = settle_two(keep1, got1, keep2, got2, kr, (t,))
        gx0, sc0 = input_back(n * PH, lengths, tot, gz1, gp, wqkv, (rows1,))
        t = s4.fold(gx0)
        last, t = spread_two(s3, s4, (t, got12))
        own34, got34, t = settle_last(last, (t,))
        d_pool, d_expand1, d_reduce1 = row_weights(cut, left, [rows1, got12], (t,))
        d_reduce, d_expand, d_attend, d_output, d_bias, d_gains, d_wb, d_pb = call(
            functools.partial(finish_kernel, wa), "finish", 24,
            [sds((2, dn, FF // GX), F32), sds((2, kr, FF // GY), F32), sds((2, kr, wa), F32), sds((2, kr, dn), F32),
             sds((6, 2, dv), F32), sds((2, 2, dv), F32), sds((2, FF // n), F32), sds((1, dv), F32)],
            (own1, own2, got12, own34, got34, d_reduce1, d_expand1))
        d_reduce = d_reduce.transpose(0, 2, 1)
        d_bias, d_pb = d_bias.transpose(1, 0, 2), d_pb.reshape(dv)
    else:
        ch2 = narrow_weight(cut, gys, acts)
        ch3 = widen_weight_back(cut, acts, gfs)
        ch1 = top_weights(cut, rows)
        gp = attend_back(gc, q, k, v, a, vectors)
        ch4 = attend_weight(cut, acts, gfs, [gp])
        gx0, sc0 = input_back(n * PH, lengths, tot, gz1, gp, wqkv)
        f1, f2, f3, f4 = (t[0].reshape(t[0].shape[-2:]) for t in (ch1, ch2, ch3, ch4))
        pool, expand1, reduce1 = row_weights(cut, [left], ch1[1:])
        d_attend = jnp.stack([scatter(t[:, :3 * D], "gx", "gy") for t in (f4, f1)])
        d_output = jnp.stack([scatter(t[:, 3 * D:], "gx", "gy") for t in (f4, f1)])
        d_expand = jnp.stack([scatter(t, "gx", "gy") for t in (f3, expand1)])
        d_reduce = jnp.stack([scatter(t, "gy", "gx").T for t in (f2, reduce1)])
        d_pool = scatter(pool, "gx", "gy")
        me = lax.axis_index("gx") * GY + lax.axis_index("gy")
        sums = lax.psum(jnp.concatenate([t[T:] for t in gp], 1).astype(F32), ("gx", "gy"))
        vec = sums[0:8].reshape(8, 3, D).transpose(1, 0, 2).reshape(24, D)
        vec = lax.dynamic_slice_in_dim(vec, me * (D // n), D // n, 1)
        d_bias, d_gains, d_pb = vec[0:12].reshape(2, 6, -1), vec[12:16].reshape(2, 2, -1), vec[16]
        d_wb = lax.dynamic_slice_in_dim(sums[8:16, :D].reshape(2, FF), me * (FF // n), FF // n, 1)
    return (loss[:PH, 0], gx0.reshape(shape), sc0.reshape(shape), d_attend, d_output, d_expand, d_reduce,
            d_bias, d_gains, d_wb, d_pool, d_pb)


def solution(mesh):
    both = ("gx", "gy")
    in_specs = (P(None, both, None, None), P(None, both), P(both)) + (P(),) * 9
    out_specs = (P(both), P(None, both, None, None), P(None, both, None, None), P(None, "gx", "gy"),
                 P(None, "gx", "gy"), P(None, "gx", "gy"), P(None, "gx", "gy"), P(None, None, both),
                 P(None, None, both), P(None, both), P("gx", "gy"), P(both))
    return jax.shard_map(functools.partial(shards, mesh), mesh=mesh, in_specs=in_specs, out_specs=out_specs,
                         check_vma=False)
```
